32 devices in a mesh: dp: 16 (over z, y, x), fsdp: 2 (over core).
Axes of the slice: x: 2, y: 2, z: 4, core: 2. Of those that a mesh axis runs over, the one named last changes fastest.
Arguments:
- mel_panels: bfloat16 [512, 10240], P(('dp', 'fsdp')), may hold values from -6 to 6
- frames: int32 [512], P(('dp', 'fsdp')), may hold values from 0 to 128, as said below
- target: int32 [512], P(('dp', 'fsdp')), may hold values from 0 to 15, as said below
- conv_first: bfloat16 [9, 256], P(None, 'fsdp'), may hold values from -2 to 2
- depth_a: bfloat16 [9, 256], P(None, 'fsdp'), may hold values from -3 to 3
- point_a: bfloat16 [256, 256], P(None, 'fsdp'), may hold values from -0.5 to 0.5
- depth_b: bfloat16 [9, 256], P(None, 'fsdp'), may hold values from -3 to 3
- point_b: bfloat16 [256, 256], P(None, 'fsdp'), may hold values from -0.5 to 0.5
- linear_weight: bfloat16 [2560, 1024], P(None, 'fsdp'), may hold values from -0.15625 to 0.15625
- norm_gain: bfloat16 [1024], P('fsdp'), may hold values from 0.099609375 to 1.8984375
- up_weight: bfloat16 [1024, 2048], P(None, 'fsdp'), may hold values from -0.1875 to 0.1875
- depth_kernel: bfloat16 [9, 1024], P(None, 'fsdp'), may hold values from -2 to 2
- conv_gain: bfloat16 [1024], P('fsdp'), may hold values from 0.099609375 to 1.8984375
- down_weight: bfloat16 [1024, 1024], P('fsdp'), may hold values from -0.1875 to 0.1875
- cotangent: bfloat16 [4096, 1024], P(('dp', 'fsdp')), may hold values from -6 to 6
Outputs:
- layer_out: bfloat16 [4096, 1024], P(('dp', 'fsdp'))
- grad_input: bfloat16 [4096, 1024], P(('dp', 'fsdp'))
- grad_down: float32 [1024, 1024], P('fsdp')
The draws below stay inside these ranges and needn't reach their ends.
Inputs may be any that keep to these rules, and one draw needn't show every extreme that they name: The slots of one loader are those of one index of dp and fsdp. A live slot holds a panel of 8 * m frames with 8 * m >= 32; frames = 0 marks an empty slot. Every device receives exactly 8 panels from the loaders of its own fsdp index, at most one from any loader, and one of them has 128 frames. `target`: only live slots are sent.
All inputs are finite; a program needn't handle non-finite values.
Results may differ from the reference program's by a relative error of at most 0.017.
Values may be sent and summed in bfloat16 or wider, within the bound.
No kernel may reach another device: no remote copies, remote signals or barrier semaphores. Data moves between devices by JAX's collectives and lax.ppermute only.
A program may use at most 192 MiB of HBM per device.

```python
import jax
import jax.numpy as jnp
from jax import lax

MELS = 80
CH = 256
D = 1024
KER = 9
PANEL = 128
U_DEV = 8
U_LOAD = 16
SUBF = 10
ROWS_DEV = 128
PANELS = 512
ROWS = 4096
N_DP = 16
N_FSDP = 2


def assign_panels(key):
    subkeys = jax.random.split(jax.random.fold_in(key, 11), 5)
    half_groups = N_DP // 2
    offsets = 2 * jax.random.permutation(subkeys[0], half_groups)[:U_DEV]
    parity = jax.random.randint(subkeys[1], (N_FSDP, N_DP), 0, 2)
    draws_len = 8 * jax.random.randint(subkeys[2], (N_FSDP, N_DP, U_DEV), max(PANEL // 32, 1), PANEL // 8 + 1)
    first_slot = jnp.arange(U_DEV)[None, None, :] == 0
    panel_len = jnp.where(first_slot, PANEL, draws_len)
    destinations = jnp.arange(N_DP)
    source = (destinations[None, :, None] + offsets[None, None, :] + parity[:, :, None]) % N_DP
    hit_table = source[:, None, :, :] == destinations[None, :, None, None]
    flat_hits = hit_table.reshape(N_FSDP, N_DP, N_DP * U_DEV).astype(jnp.int32)
    rank_table = jnp.cumsum(flat_hits, axis=2) - 1
    slot_ids = jnp.arange(U_LOAD)
    match_table = (rank_table[:, :, None, :] == slot_ids[None, None, :, None]) & (flat_hits[:, :, None, :] > 0)
    dest_of = jnp.broadcast_to(destinations[:, None], (N_DP, U_DEV)).reshape(-1)
    len_of = panel_len.reshape(N_FSDP, N_DP * U_DEV)
    filled = jnp.any(match_table, axis=3)
    fill_target = jnp.sum(jnp.where(match_table, dest_of[None, None, None, :], 0), axis=3)
    fill_len = jnp.sum(jnp.where(match_table, len_of[:, None, None, :], 0), axis=3)
    spare_dest = jax.random.randint(subkeys[3], (N_FSDP, N_DP, U_LOAD), 0, N_DP)
    targets = jnp.where(filled, fill_target, spare_dest)
    lengths = jnp.where(filled, fill_len, 0)
    scores = jax.random.randint(subkeys[4], (N_FSDP, N_DP, U_LOAD), 0, 1 << 20) * U_LOAD + slot_ids
    shuffle = jnp.argsort(scores, axis=2)
    targets = jnp.take_along_axis(targets, shuffle, axis=2)
    lengths = jnp.take_along_axis(lengths, shuffle, axis=2)
    targets = jnp.transpose(targets, (1, 0, 2)).reshape(-1).astype(jnp.int32)
    lengths = jnp.transpose(lengths, (1, 0, 2)).reshape(-1).astype(jnp.int32)
    return (targets, lengths)


def draw_frames(key, part):
    return assign_panels(key)[1]


def draw_target(key, part):
    return assign_panels(key)[0]


def levels(rng, shape, cuts, least, top_value):
    loudness, own = 1.0, jax.random.fold_in(rng, 6)
    for dim, blocks in cuts:
        steps = jnp.exp(jax.random.uniform(jax.random.fold_in(own, dim), (blocks,), jnp.float32, least / len(cuts), top_value / len(cuts)))
        loudness = loudness * jnp.repeat(steps, shape[dim] // blocks).reshape([-1 if axis == dim else 1 for axis in range(len(shape))])
    return loudness


def noise(rng, extent, scale, bound, cuts=(), kind=jnp.bfloat16):
    entries = jax.random.normal(rng, extent, jnp.float32) * scale
    if len(cuts) > 0:
        entries = levels(rng, extent, cuts, -0.22, 0.18) * entries
    return jnp.clip(entries, min=-bound, max=bound).astype(kind)


def setup_inputs(seed: int = 0) -> dict:
    splits = jax.random.split(jax.random.key(seed), 16)
    mel_panels = noise(splits[0], (PANELS, PANEL * MELS), 1.0, 6.0, ((0, 32),))
    frames = draw_frames(jax.random.fold_in(splits[15], 71), 0)
    target = draw_target(jax.random.fold_in(splits[15], 71), 0)
    conv_first = noise(splits[3], (9, CH), 9 ** -0.5, 2.0, ((1, 2),))
    depth_a = noise(splits[4], (9, CH), 4 ** -0.5, 3.0, ((1, 2),))
    point_a = noise(splits[5], (CH, CH), (CH // 2) ** -0.5, 0.5, ((1, 2),))
    depth_b = noise(splits[6], (9, CH), 4 ** -0.5, 3.0, ((1, 2),))
    point_b = noise(splits[7], (CH, CH), (CH // 2) ** -0.5, 0.5, ((1, 2),))
    linear_weight = noise(splits[8], (SUBF * CH, D), (SUBF * CH // 2) ** -0.5, 0.15625, ((1, 2),))
    norm_gain = jnp.clip(1.0 + 0.18 * jax.random.normal(splits[9], (D,), jnp.float32), 0.099609375, 1.8984375).astype(jnp.bfloat16)
    up_weight = noise(splits[10], (D, 2 * D), D ** -0.5, 0.1875, ((1, 2),))
    depth_kernel = noise(splits[11], (KER, D), KER ** -0.5, 2.0, ((1, 2),))
    conv_gain = jnp.clip(1.0 + 0.18 * jax.random.normal(splits[12], (D,), jnp.float32), 0.099609375, 1.8984375).astype(jnp.bfloat16)
    down_weight = noise(splits[13], (D, D), D ** -0.5, 0.1875, ((0, 2),))
    cotangent = noise(splits[14], (ROWS, D), 1.0, 6.0, ((0, 32),))
    return {"mel_panels": mel_panels, "frames": frames, "target": target, "conv_first": conv_first, "depth_a": depth_a, "point_a": point_a, "depth_b": depth_b, "point_b": point_b, "linear_weight": linear_weight, "norm_gain": norm_gain, "up_weight": up_weight, "depth_kernel": depth_kernel, "conv_gain": conv_gain, "down_weight": down_weight, "cotangent": cotangent}


EPSILON = 1e-05

def first_section(masked, weights):
    height = masked.shape[1] // 2
    breadth = masked.shape[2] // 2
    padded = jnp.pad(masked, ((0, 0), (1, 1), (1, 1)))
    summed = jnp.zeros((masked.shape[0], height, breadth, weights.shape[1]), jnp.float32)
    for i in range(3):
        for j in range(3):
            window = padded[:, i:i + 2 * height:2, j:j + 2 * breadth:2].astype(jnp.float32)
            summed = summed + window[:, :, :, None] * weights[3 * i + j].astype(jnp.float32)
    return jnp.maximum(summed, 0.0).astype(jnp.bfloat16)

def depth_stride(source, weights):
    height = source.shape[1] // 2
    breadth = source.shape[2] // 2
    padded = jnp.pad(source, ((0, 0), (1, 1), (1, 1), (0, 0)))
    summed = jnp.zeros((source.shape[0], height, breadth, source.shape[3]), jnp.float32)
    for i in range(3):
        for j in range(3):
            window = padded[:, i:i + 2 * height:2, j:j + 2 * breadth:2, :].astype(jnp.float32)
            summed = summed + window * weights[3 * i + j].astype(jnp.float32)
    return summed.astype(jnp.bfloat16)

def point_relu(spread, weights):
    shape_in = spread.shape
    mapped = jnp.dot(spread.reshape(-1, shape_in[3]), weights, preferred_element_type=jnp.float32)
    return jnp.maximum(mapped, 0.0).astype(jnp.bfloat16).reshape(shape_in[:3] + (weights.shape[1],))

def subsample(block_panels, block_lengths, conv_first, depth_a, point_a, depth_b, point_b):
    number = block_panels.shape[0]
    frames_in = block_panels.reshape(number, PANEL, MELS)
    inside = jnp.arange(PANEL)[None, :] < block_lengths[:, None]
    masked = jnp.where(inside[:, :, None], frames_in, jnp.zeros_like(frames_in))
    first = first_section(masked, conv_first)
    second = point_relu(depth_stride(first, depth_a), point_a)
    fourth = point_relu(depth_stride(second, depth_b), point_b)
    return fourth.reshape(number * fourth.shape[1], fourth.shape[2] * fourth.shape[3])

def depth_forward(gated, kernel, span):
    groups_in = gated.shape[0] // span
    half_width = kernel.shape[0] // 2
    shaped = jnp.pad(gated.reshape(groups_in, span, -1), ((0, 0), (half_width, half_width), (0, 0)))
    summed = jnp.zeros((groups_in, span, gated.shape[1]), jnp.float32)
    for k in range(kernel.shape[0]):
        summed = summed + shaped[:, k:k + span].astype(jnp.float32) * kernel[k].astype(jnp.float32)
    return summed.reshape(gated.shape[0], -1)

def depth_backward(upstream, kernel, span):
    groups_in = upstream.shape[0] // span
    half_width = kernel.shape[0] // 2
    shaped = jnp.pad(upstream.reshape(groups_in, span, -1), ((0, 0), (half_width, half_width), (0, 0)))
    summed = jnp.zeros((groups_in, span, upstream.shape[1]), jnp.float32)
    for k in range(kernel.shape[0]):
        offset = 2 * half_width - k
        summed = summed + shaped[:, offset:offset + span] * kernel[k].astype(jnp.float32)
    return summed.reshape(upstream.shape[0], -1)

def module_pass(features, keep, cotangent, norm_gain, up_weight, depth_kernel, conv_gain, down_weight, span):
    width = features.shape[1]
    values = features.astype(jnp.float32)
    centred = values - lax.optimization_barrier(jnp.mean(values, axis=1, keepdims=True))
    scale_one = lax.rsqrt(lax.optimization_barrier(jnp.mean(centred * centred, axis=1, keepdims=True)) + EPSILON)
    standard = centred * scale_one
    normed = (standard * norm_gain.astype(jnp.float32)).astype(jnp.bfloat16)
    projected = jnp.dot(normed, up_weight, preferred_element_type=jnp.float32)
    value_half = projected[:, :width]
    gate_half = jax.nn.sigmoid(projected[:, width:])
    row_keep = keep[:, None]
    gated = (row_keep * value_half * gate_half).astype(jnp.bfloat16)
    depthwise = depth_forward(gated, depth_kernel, span)
    centred_two = depthwise - lax.optimization_barrier(jnp.mean(depthwise, axis=1, keepdims=True))
    scale_two = lax.rsqrt(lax.optimization_barrier(jnp.mean(centred_two * centred_two, axis=1, keepdims=True)) + EPSILON)
    standard_two = centred_two * scale_two
    active = standard_two * conv_gain.astype(jnp.float32)
    swish_gate = jax.nn.sigmoid(active)
    hidden = (active * swish_gate).astype(jnp.bfloat16)
    mixed = jnp.dot(hidden, down_weight, preferred_element_type=jnp.float32)
    layer_out = (row_keep * (values + mixed)).astype(jnp.bfloat16)
    back_out = jnp.where(row_keep > 0, cotangent, jnp.zeros_like(cotangent))
    back_hidden = lax.dot_general(back_out, down_weight, (((1,), (1,)), ((), ())), preferred_element_type=jnp.float32)
    back_active = back_hidden * (swish_gate + active * swish_gate * (1.0 - swish_gate))
    gain_back = back_active * conv_gain.astype(jnp.float32)
    back_depth = scale_two * (gain_back - lax.optimization_barrier(jnp.mean(gain_back, axis=1, keepdims=True)) - standard_two * lax.optimization_barrier(jnp.mean(gain_back * standard_two, axis=1, keepdims=True)))
    back_gated = row_keep * depth_backward(back_depth, depth_kernel, span)
    back_proj = jnp.concatenate([back_gated * gate_half, back_gated * value_half * gate_half * (1.0 - gate_half)], axis=1).astype(jnp.bfloat16)
    back_normed = lax.dot_general(back_proj, up_weight, (((1,), (1,)), ((), ())), preferred_element_type=jnp.float32)
    gain_front = back_normed * norm_gain.astype(jnp.float32)
    back_input = scale_one * (gain_front - lax.optimization_barrier(jnp.mean(gain_front, axis=1, keepdims=True)) - standard * lax.optimization_barrier(jnp.mean(gain_front * standard, axis=1, keepdims=True)))
    grad_input = (back_out.astype(jnp.float32) + back_input).astype(jnp.bfloat16)
    return (layer_out, grad_input, hidden, back_out)

def reference(mel_panels, frames, target, conv_first, depth_a, point_a, depth_b, point_b, linear_weight, norm_gain, up_weight, depth_kernel, conv_gain, down_weight, cotangent):
    width_all = PANEL * MELS
    grouped_mel = mel_panels.reshape(N_DP, N_FSDP, U_LOAD, width_all)
    grouped_frames = frames.reshape(N_DP, N_FSDP, U_LOAD)
    grouped_target = target.reshape(N_DP, N_FSDP, U_LOAD)
    flat_index = jnp.arange(N_DP * U_LOAD, dtype=jnp.int32)
    destinations = jnp.arange(N_DP, dtype=jnp.int32)
    places = jnp.arange(U_DEV, dtype=jnp.int32)
    panel_parts = []
    length_parts = []
    for j in range(N_FSDP):
        frame_row = grouped_frames[:, j].reshape(-1)
        target_row = grouped_target[:, j].reshape(-1)
        flags = ((target_row[None, :] == destinations[:, None]) & (frame_row[None, :] > 0)).astype(jnp.int32)
        rank_table = (jnp.cumsum(flags, axis=1) - 1).astype(jnp.int32)
        match_table = (rank_table[:, None, :] == places[None, :, None]) & (flags[:, None, :] > 0)
        source = lax.optimization_barrier(jnp.sum(jnp.where(match_table, flat_index[None, None, :], 0), axis=2)).astype(jnp.int32)
        loader_pool = grouped_mel[:, j].reshape(N_DP * U_LOAD, width_all)
        panel_parts.append(loader_pool[source])
        length_parts.append(frame_row[source])
    panels = jnp.stack(panel_parts, axis=1).reshape(-1, width_all)
    lengths = jnp.stack(length_parts, axis=1).reshape(-1).astype(jnp.int32)
    per_block = 16
    blocks = panels.shape[0] // per_block

    def sub_block(block_args):
        flat_rows = subsample(block_args[0], block_args[1], conv_first, depth_a, point_a, depth_b, point_b)
        return jnp.dot(flat_rows, linear_weight, preferred_element_type=jnp.float32).astype(jnp.bfloat16)
    features = lax.map(sub_block, (panels.reshape(blocks, per_block, width_all), lengths.reshape(blocks, per_block))).reshape(ROWS, D)
    span = PANEL // 8
    keep = (jnp.arange(span)[None, :] < (lengths // 8)[:, None]).reshape(-1).astype(jnp.float32)
    devices = N_DP * N_FSDP

    def one_device(carry, device_args):
        layer_out, grad_input, hidden, back_out = module_pass(device_args[0], device_args[1], device_args[2], norm_gain, up_weight, depth_kernel, conv_gain, down_weight, span)
        contrib = lax.dot_general(hidden, back_out, (((0,), (0,)), ((), ())), preferred_element_type=jnp.float32)
        return (carry + contrib, (layer_out, grad_input))
    summed, (layers, grads) = lax.scan(one_device, jnp.zeros((D, D), jnp.float32), (features.reshape(devices, ROWS_DEV, D), keep.reshape(devices, ROWS_DEV), cotangent.reshape(devices, ROWS_DEV, D)))
    grad_down = summed / jnp.sqrt(jnp.float32(ROWS))
    return (layers.reshape(ROWS, D), grads.reshape(ROWS, D), grad_down)
```

```python
import math

import jax
import jax.numpy as jnp
from jax import lax
from jax.sharding import PartitionSpec as P

MELS = 80
PANEL = 128


EPSILON = 1e-05


def phase_rows(source):
    shape_in = source.shape
    split = source.reshape((shape_in[0], shape_in[1] // 2, 2) + shape_in[2:])
    even = split[:, :, 0]
    odd = split[:, :, 1]
    before = jnp.concatenate([jnp.zeros_like(odd[:, :1]), odd[:, :-1]], axis=1)
    return (before, even, odd)


def phase_cols(source):
    shape_in = source.shape
    split = source.reshape(shape_in[:2] + (shape_in[2] // 2, 2) + shape_in[3:])
    even = split[:, :, :, 0]
    odd = split[:, :, :, 1]
    before = jnp.concatenate([jnp.zeros_like(odd[:, :, :1]), odd[:, :, :-1]], axis=2)
    return (before, even, odd)


def first_section(masked, weights):
    height = masked.shape[1] // 2
    breadth = masked.shape[2] // 2
    summed = jnp.zeros((masked.shape[0], height, breadth, weights.shape[1]), jnp.float32)
    row_views = phase_rows(masked)
    for i in range(3):
        col_views = phase_cols(row_views[i])
        for j in range(3):
            window = col_views[j].astype(jnp.float32)
            summed = summed + window[:, :, :, None] * weights[3 * i + j].astype(jnp.float32)
    return jnp.maximum(summed, 0.0).astype(jnp.bfloat16)


def depth_stride(source, weights):
    height = source.shape[1] // 2
    breadth = source.shape[2] // 2
    summed = jnp.zeros((source.shape[0], height, breadth, source.shape[3]), jnp.float32)
    row_views = phase_rows(source)
    for i in range(3):
        col_views = phase_cols(row_views[i])
        for j in range(3):
            window = col_views[j].astype(jnp.float32)
            summed = summed + window * weights[3 * i + j].astype(jnp.float32)
    return summed.astype(jnp.bfloat16)


def point_relu(spread, weights):
    shape_in = spread.shape
    mapped = jnp.dot(spread.reshape(-1, shape_in[3]), weights, preferred_element_type=jnp.float32)
    return jnp.maximum(mapped, 0.0).astype(jnp.bfloat16).reshape(shape_in[:3] + (weights.shape[1],))


def subsample(block_panels, block_lengths, conv_first, depth_a, point_a, depth_b, point_b):
    number = block_panels.shape[0]
    frames_in = block_panels.reshape(number, PANEL, MELS)
    inside = jnp.arange(PANEL)[None, :] < block_lengths[:, None]
    masked = jnp.where(inside[:, :, None], frames_in, jnp.zeros_like(frames_in))
    first = first_section(masked, conv_first)
    second = point_relu(depth_stride(first, depth_a), point_a)
    fourth = point_relu(depth_stride(second, depth_b), point_b)
    return fourth.reshape(number * fourth.shape[1], fourth.shape[2] * fourth.shape[3])


def depth_forward(gated, kernel, span):
    groups_in = gated.shape[0] // span
    half_width = kernel.shape[0] // 2
    shaped = jnp.pad(gated.reshape(groups_in, span, -1), ((0, 0), (half_width, half_width), (0, 0)))
    summed = jnp.zeros((groups_in, span, gated.shape[1]), jnp.float32)
    for k in range(kernel.shape[0]):
        summed = summed + shaped[:, k : k + span].astype(jnp.float32) * kernel[k].astype(
            jnp.float32
        )
    return summed.reshape(gated.shape[0], -1)


def depth_backward(upstream, kernel, span):
    groups_in = upstream.shape[0] // span
    half_width = kernel.shape[0] // 2
    shaped = jnp.pad(
        upstream.reshape(groups_in, span, -1), ((0, 0), (half_width, half_width), (0, 0))
    )
    summed = jnp.zeros((groups_in, span, upstream.shape[1]), jnp.float32)
    for k in range(kernel.shape[0]):
        offset = 2 * half_width - k
        summed = summed + shaped[:, offset : offset + span] * kernel[k].astype(jnp.float32)
    return summed.reshape(upstream.shape[0], -1)


def module_forward(features, keep, gain_front, up_mine, up_other, kernel_full, gain_back, me, span):
    values = features.astype(jnp.float32)
    centred = values - jnp.mean(values, axis=1, keepdims=True)
    scale_one = lax.rsqrt(jnp.mean(centred * centred, axis=1, keepdims=True) + EPSILON)
    standard = centred * scale_one
    normed = (standard * gain_front).astype(jnp.bfloat16)
    mine = jnp.dot(normed, up_mine, preferred_element_type=jnp.float32)
    other = jnp.dot(normed, up_other, preferred_element_type=jnp.float32)
    value_half = jnp.where(me == 0, mine, other)
    gate_half = jax.nn.sigmoid(jnp.where(me == 0, other, mine))
    row_keep = keep[:, None]
    gated = (row_keep * value_half * gate_half).astype(jnp.bfloat16)
    depthwise = depth_forward(gated, kernel_full, span)
    centred_two = depthwise - jnp.mean(depthwise, axis=1, keepdims=True)
    scale_two = lax.rsqrt(jnp.mean(centred_two * centred_two, axis=1, keepdims=True) + EPSILON)
    standard_two = centred_two * scale_two
    active = standard_two * gain_back
    swish_gate = jax.nn.sigmoid(active)
    hidden = (active * swish_gate).astype(jnp.bfloat16)
    return hidden, (values, standard, scale_one, value_half, gate_half, scale_two, standard_two, active, swish_gate)


def module_backward(hidden, saved, keep, cotangent, gain_front, up_mine, up_other, kernel_full, gain_back, down_mine, down_other, me, span):
    values, standard, scale_one, value_half, gate_half, scale_two, standard_two, active, swish_gate = saved
    row_keep = keep[:, None]
    half = down_mine.shape[0]
    hidden_mine = lax.dynamic_slice_in_dim(hidden, me * half, half, axis=1)
    hidden_other = lax.dynamic_slice_in_dim(hidden, (1 - me) * half, half, axis=1)
    mixed = jnp.dot(hidden_mine, down_mine, preferred_element_type=jnp.float32) + jnp.dot(
        hidden_other, down_other, preferred_element_type=jnp.float32
    )
    layer_out = (row_keep * (values + mixed)).astype(jnp.bfloat16)
    back_out = jnp.where(row_keep > 0, cotangent, jnp.zeros_like(cotangent))
    across = (((1,), (1,)), ((), ()))
    back_mine = lax.dot_general(back_out, down_mine, across, preferred_element_type=jnp.float32)
    back_other = lax.dot_general(back_out, down_other, across, preferred_element_type=jnp.float32)
    back_hidden = jnp.concatenate(
        [jnp.where(me == 0, back_mine, back_other), jnp.where(me == 0, back_other, back_mine)], axis=1
    )
    back_active = back_hidden * (swish_gate + active * swish_gate * (1.0 - swish_gate))
    gain_up = back_active * gain_back
    back_depth = scale_two * (
        gain_up
        - jnp.mean(gain_up, axis=1, keepdims=True)
        - standard_two * jnp.mean(gain_up * standard_two, axis=1, keepdims=True)
    )
    back_gated = row_keep * depth_backward(back_depth, kernel_full, span)
    back_value = (back_gated * gate_half).astype(jnp.bfloat16)
    back_gate = (back_gated * value_half * gate_half * (1.0 - gate_half)).astype(jnp.bfloat16)
    back_normed = lax.dot_general(
        jnp.where(me == 0, back_value, back_gate), up_mine, across, preferred_element_type=jnp.float32
    ) + lax.dot_general(
        jnp.where(me == 0, back_gate, back_value), up_other, across, preferred_element_type=jnp.float32
    )
    gain_in = back_normed * gain_front
    back_input = scale_one * (
        gain_in
        - jnp.mean(gain_in, axis=1, keepdims=True)
        - standard * jnp.mean(gain_in * standard, axis=1, keepdims=True)
    )
    grad_input = (back_out.astype(jnp.float32) + back_input).astype(jnp.bfloat16)
    return layer_out, grad_input


def swap_cores(block):
    return lax.ppermute(block, "fsdp", [(0, 1), (1, 0)])


def swap_bit(block, bit, groups):
    return lax.ppermute(block, "dp", [(i, i ^ (1 << bit)) for i in range(groups)])


def pick(block, index):
    return lax.dynamic_index_in_dim(block, index, axis=0, keepdims=False)


def halve(total, bit, groups):
    side = (lax.axis_index("dp") >> bit) & 1
    pair = total.reshape(2, total.shape[0] // 2, total.shape[1])
    given = swap_bit(pick(pair, 1 - side).astype(jnp.bfloat16), bit, groups)
    return pick(pair, side) + given.astype(jnp.float32)


def double(block, bit, groups):
    side = (lax.axis_index("dp") >> bit) & 1
    given = swap_bit(block, bit, groups)
    return jnp.concatenate(
        [jnp.where(side == 0, block, given), jnp.where(side == 0, given, block)], axis=0
    )


def sum_over_dp(total, scale, groups):
    bits = groups.bit_length() - 1
    half = total.shape[1] // 2
    orders = ([0, 1], [1, 0])
    parts = [total[:, :half], total[:, half:]]
    for step in range(2):
        parts = [halve(part, order[step], groups) for part, order in zip(parts, orders)]
    joined = jnp.concatenate(parts, axis=1)
    for bit in range(2, bits - 1):
        joined = halve(joined, bit, groups)
    rounded = joined.astype(jnp.bfloat16)
    given = swap_bit(rounded, bits - 1, groups)
    block = ((rounded.astype(jnp.float32) + given.astype(jnp.float32)) * scale).astype(jnp.bfloat16)
    for bit in reversed(range(2, bits - 1)):
        block = double(block, bit, groups)
    parts = [block[:, :half], block[:, half:]]
    for step in reversed(range(2)):
        parts = [double(part, order[step], groups) for part, order in zip(parts, orders)]
    return jnp.concatenate(parts, axis=1).astype(jnp.float32)


def pack_rows(arrays):
    flat = []
    for array in arrays:
        rows = array.reshape(-1, 128)
        flat.append(jnp.pad(rows, ((0, -rows.shape[0] % 16), (0, 0))))
    return jnp.concatenate(flat, axis=0)


def unpack_rows(packed, arrays):
    out = []
    at = 0
    for array in arrays:
        count = array.size // 128
        out.append(packed[at : at + count].reshape(array.shape))
        at += count + (-count % 16)
    return out


def both(mine, other, me, axis):
    return jnp.concatenate(
        [jnp.where(me == 0, mine, other), jnp.where(me == 0, other, mine)], axis=axis
    )


def local(
    mel_panels,
    frames,
    target,
    conv_first,
    depth_a,
    point_a,
    depth_b,
    point_b,
    linear_weight,
    norm_gain,
    up_weight,
    depth_kernel,
    conv_gain,
    down_weight,
    cotangent,
):
    groups = lax.axis_size("dp")
    members = lax.axis_size("fsdp")
    me = lax.axis_index("fsdp")
    span = PANEL // 8
    panel_count = cotangent.shape[0] // span
    width_in = mel_panels.shape[1]
    destinations = jnp.arange(groups, dtype=jnp.int32)
    selected = (target[None, :] == destinations[:, None]) & (frames[None, :] > 0)
    carried = jnp.concatenate(
        [mel_panels, jnp.broadcast_to(frames[:, None], (frames.shape[0], 128)).astype(jnp.bfloat16)], axis=1
    )
    outgoing = jnp.dot(
        selected.astype(jnp.bfloat16), carried, preferred_element_type=jnp.float32
    ).astype(jnp.bfloat16)
    incoming = lax.all_to_all(outgoing, "dp", split_axis=0, concat_axis=0, tiled=True)
    got_frames = incoming[:, width_in].astype(jnp.int32)
    present = got_frames > 0
    position = jnp.cumsum(present.astype(jnp.int32)) - 1
    places = jnp.arange(panel_count, dtype=jnp.int32)
    placing = (position[None, :] == places[:, None]) & present[None, :]
    panels = jnp.dot(
        placing.astype(jnp.bfloat16), incoming[:, :width_in], preferred_element_type=jnp.float32
    ).astype(jnp.bfloat16)
    lengths = jnp.sum(jnp.where(placing, got_frames[None, :], 0), axis=1).astype(jnp.int32)
    small = [conv_first, depth_a, point_a, depth_b, point_b, norm_gain, depth_kernel, conv_gain]
    packed = swap_cores(pack_rows(small))
    linear_other = swap_cores(linear_weight)
    up_other = swap_cores(up_weight)
    down_other = swap_cores(down_weight)
    cotangent_other = swap_cores(cotangent)
    first_full, depth_one, point_one, depth_two, point_two, gain_front, kernel_full, gain_back = [
        both(mine, other, me, mine.ndim - 1) for mine, other in zip(small, unpack_rows(packed, small))
    ]
    gain_front = gain_front.astype(jnp.float32)
    gain_back = gain_back.astype(jnp.float32)
    flat_rows = subsample(panels, lengths, first_full, depth_one, point_one, depth_two, point_two)
    features = both(
        jnp.dot(flat_rows, linear_weight, preferred_element_type=jnp.float32).astype(jnp.bfloat16),
        jnp.dot(flat_rows, linear_other, preferred_element_type=jnp.float32).astype(jnp.bfloat16),
        me,
        1,
    )
    keep = (jnp.arange(span)[None, :] < (lengths // 8)[:, None]).reshape(-1).astype(jnp.float32)
    hidden, saved = module_forward(
        features, keep, gain_front, up_weight, up_other, kernel_full, gain_back, me, span
    )
    half = hidden.shape[1] // members
    kept = hidden * keep[:, None].astype(jnp.bfloat16)
    kept_mine = lax.dynamic_slice_in_dim(kept, me * half, half, axis=1)
    kept_other = swap_cores(lax.dynamic_slice_in_dim(kept, (1 - me) * half, half, axis=1))
    down_rows = (((0,), (0,)), ((), ()))
    product = lax.dot_general(
        kept_mine, cotangent, down_rows, preferred_element_type=jnp.float32
    ) + lax.dot_general(kept_other, cotangent_other, down_rows, preferred_element_type=jnp.float32)
    scale = 1.0 / math.sqrt(cotangent.shape[0] * groups * members)
    grad_down = sum_over_dp(product, scale, groups)
    layer_out, grad_input = module_backward(
        hidden, saved, keep, cotangent, gain_front, up_weight, up_other, kernel_full, gain_back,
        down_weight, down_other, me, span,
    )
    return (layer_out, grad_input, grad_down)


def solution(mesh):
    placed = (
        P(("dp", "fsdp"), None),
        P(("dp", "fsdp")),
        P(("dp", "fsdp")),
        P(None, "fsdp"),
        P(None, "fsdp"),
        P(None, "fsdp"),
        P(None, "fsdp"),
        P(None, "fsdp"),
        P(None, "fsdp"),
        P("fsdp"),
        P(None, "fsdp"),
        P(None, "fsdp"),
        P("fsdp"),
        P("fsdp", None),
        P(("dp", "fsdp"), None),
    )
    return jax.shard_map(
        local,
        mesh=mesh,
        in_specs=placed,
        out_specs=(P(("dp", "fsdp"), None), P(("dp", "fsdp"), None), P("fsdp", None)),
        check_vma=False,
    )
```

```python
import functools
import math

import jax
import jax.numpy as jnp
from jax import lax
from jax.experimental import pallas as pl
from jax.experimental.pallas import tpu as pltpu
from jax.sharding import PartitionSpec as P

MELS = 80
PANEL = 128
EPSILON = 1e-05
SPAN = PANEL // 8
BLOCK = 8
ROWS = BLOCK * SPAN
BINS = 40
GROUP = 10
WINDOW = 2 * GROUP + 1
LEAD = 256
BF = jnp.bfloat16
F32 = jnp.float32
ACROSS = (((1,), (1,)), ((), ()))
DOWN = (((0,), (0,)), ((), ()))


def dot(left, right, dims=(((1,), (0,)), ((), ()))):
    return lax.dot_general(left, right, dims, preferred_element_type=F32)


def iota(shape, dim):
    return lax.broadcasted_iota(jnp.int32, shape, dim)


def row_order():
    n = iota((ROWS, ROWS), 0)
    r = iota((ROWS, ROWS), 1)
    return jnp.where((n % SPAN) * BLOCK + n // SPAN == r, 1.0, 0.0).astype(BF)


def send_kernel(
    mel, frames, target, first, depth_a, point_a, depth_b, point_b, norm_gain, depth_kernel, conv_gain,
    outgoing, packed, rows,
):
    count = outgoing.shape[0]
    slots = mel.shape[0]
    width = mel.shape[1]
    wanted = iota((count, slots), 0)
    chosen = jnp.where((target[...] == wanted) & (frames[...] > 0), 1.0, 0.0)
    outgoing[:, :width] = dot(chosen.astype(BF), mel[...]).astype(BF)
    sent = jnp.sum(chosen * frames[...].astype(F32), axis=1, keepdims=True)
    outgoing[:, width:] = jnp.broadcast_to(sent, (count, 128)).astype(BF)
    rows[...] = jnp.zeros_like(rows)
    rows[0:9, :] = depth_kernel[...].astype(F32)
    rows[9:10, :] = norm_gain[...].astype(F32)
    rows[10:11, :] = conv_gain[...].astype(F32)
    rows[16:25, 0:128] = first[...].astype(F32)
    rows[16:25, 128:256] = depth_a[...].astype(F32)
    rows[16:25, 256:384] = depth_b[...].astype(F32)
    packed[0:32, :] = rows[...].astype(BF)
    packed[32:160, 0:128] = point_a[0:128, :]
    packed[32:160, 128:256] = point_a[128:256, :]
    packed[32:160, 256:384] = point_b[0:128, :]
    packed[32:160, 384:512] = point_b[128:256, :]


def weights_kernel(mine, other, band, taps_a, taps_b, point_a, point_b, rows):
    me = lax.axis_index("fsdp")
    near = mine[...].astype(F32)
    far = other[...].astype(F32)
    low = jnp.where(me == 0, near, far)
    high = jnp.where(me == 0, far, near)
    rows[:, 0:512] = low[0:16]
    rows[:, 512:1024] = high[0:16]
    first = jnp.concatenate([low[16:32, 0:128], high[16:32, 0:128]], axis=1).astype(BF)
    taps_a[...] = jnp.concatenate([low[16:32, 128:256], high[16:32, 128:256]], axis=1)
    taps_b[...] = jnp.concatenate([low[16:32, 256:384], high[16:32, 256:384]], axis=1)
    for half, source in ((0, low), (1, high)):
        at = slice(half * 128, half * 128 + 128)
        point_a[0:128, at] = source[32:160, 0:128].astype(BF)
        point_a[128:256, at] = source[32:160, 128:256].astype(BF)
        point_b[0:128, at] = source[32:160, 256:384].astype(BF)
        point_b[128:256, at] = source[32:160, 384:512].astype(BF)
    tap = iota((256, 16), 1)
    base = jnp.where(tap < 9, (tap // 3) * MELS + tap % 3, -1000) - iota((256, 16), 0)
    for f in range(GROUP):
        place = jnp.where(base == -2 * f, 1.0, 0.0).astype(BF)
        band[:, f * 256 : (f + 1) * 256] = dot(place, first).astype(BF)


def fetch(pairs, sems, me):
    copies = []
    for number, (mine, other, held) in enumerate(pairs):
        copies.append(pltpu.make_async_copy(mine, held.at[me], sems.at[2 * number]))
        copies.append(pltpu.make_async_copy(other, held.at[1 - me], sems.at[2 * number + 1]))
    return copies


def centre(values):
    return values - jnp.mean(values, axis=1, keepdims=True)


def forward_kernel(
    incoming, band, taps_a, taps_b, point_a, point_b, rows, linear_mine, linear_other, up_mine, up_other,
    hidden_out, kept_out, features_out, standard_out, value_out, gate_out, standard_two_out, scales_out, keep_out,
    linear_s, up_s, ext_s, x_s, first_s, spread_s, even_s, odd_s, flat_s, gated_s, sems,
):
    step = pl.program_id(0)
    me = lax.axis_index("fsdp")
    copies = fetch(((linear_mine, linear_other, linear_s), (up_mine, up_other, up_s)), sems, me)

    @pl.when(step == 0)
    def _():
        for copy in copies:
            copy.start()

    sources = incoming.shape[0]
    width = incoming.shape[1] - 128
    got = incoming[:, width:]
    present = jnp.where(got > 0, 1.0, 0.0)
    below = jnp.where(iota((sources, sources), 1) <= iota((sources, sources), 0), 1.0, 0.0).astype(BF)
    position = dot(below, present.astype(BF)) - 1.0
    slot = (iota((sources, 128), 1) + step * BLOCK).astype(F32)
    placing = jnp.where((position == slot) & (present > 0), 1.0, 0.0).astype(BF)[:, :BLOCK]
    length = dot(placing, got, DOWN)
    stretch = width // SPAN
    ext_s[0:BLOCK, 0:LEAD] = jnp.zeros((BLOCK, LEAD), F32)
    for t in range(SPAN):
        live = length > 8.0 * t
        keep_out[t * BLOCK : (t + 1) * BLOCK, :] = jnp.where(live, 1.0, 0.0)
        part = dot(placing, incoming[:, t * stretch : (t + 1) * stretch], DOWN)
        part = jnp.where(live[:, 0:1], part, 0.0)
        ext_s[t * BLOCK : (t + 1) * BLOCK, LEAD:] = part
        if t + 1 < SPAN:
            ext_s[(t + 1) * BLOCK : (t + 2) * BLOCK, 0:LEAD] = part[:, stretch - LEAD :]
    lane = iota((ROWS, 256), 1)
    edge = (lane == 0) | (lane == MELS) | (lane == 2 * MELS)
    for q in range(5):
        for b in range(4):
            start = LEAD + (2 * q - 3) * MELS + 2 * GROUP * b - 1
            tile = start // 128 * 128
            shift = start - tile
            span = 256 if shift + 2 * MELS + WINDOW <= 256 else 384
            part = ext_s[:, tile : tile + span]
            part = pltpu.roll(part, span - shift, 1)[:, :256]
            if b == 0:
                part = jnp.where(edge, 0.0, part)
            x_s[b, q * ROWS : (q + 1) * ROWS, :] = part.astype(BF)

    first_s[0] = jnp.zeros(first_s.shape[1:], F32)
    odd_s[:, 0:BLOCK, :] = jnp.zeros((odd_s.shape[0], BLOCK, 256), F32)

    def section(b, carry):
        source = x_s[b]
        for f in range(GROUP):
            first_s[1 + f] = jnp.maximum(dot(source, band[:, f * 256 : (f + 1) * 256]), 0.0)
        for g in range(GROUP // 2):
            for s in range(2):
                total = None
                for j in range(3):
                    for i in range(3):
                        at = (2 * s + i) * ROWS
                        term = first_s[2 * g + j, at : at + ROWS, :] * taps_a[3 * i + j : 3 * i + j + 1, :]
                        total = term if total is None else total + term
                spread_s[(2 * g + s) * ROWS : (2 * g + s + 1) * ROWS, :] = total.astype(BF)
        first_s[0] = first_s[GROUP]
        second = jnp.maximum(dot(spread_s[...], point_a[...]), 0.0)
        for g in range(GROUP // 2):
            even_s[b * (GROUP // 2) + g] = second[2 * g * ROWS : (2 * g + 1) * ROWS]
            odd_s[b * (GROUP // 2) + g, BLOCK:, :] = second[(2 * g + 1) * ROWS : (2 * g + 2) * ROWS]
        return carry

    lax.fori_loop(0, BINS // GROUP, section, 0)

    for f in range(BINS // 4):
        total = None
        for j in range(3):
            at = 2 * f + j - 1
            if at < 0:
                continue
            for i, view in enumerate((odd_s.at[at, 0:ROWS, :], even_s.at[at], odd_s.at[at, BLOCK : BLOCK + ROWS, :])):
                term = view[...] * taps_b[3 * i + j : 3 * i + j + 1, :]
                total = term if total is None else total + term
        fourth = jnp.maximum(dot(total.astype(BF), point_b[...]), 0.0)
        flat_s[:, f * 256 : (f + 1) * 256] = fourth.astype(BF)

    @pl.when(step == 0)
    def _():
        copies[0].wait()
        copies[1].wait()

    half = linear_s.shape[2]
    for side in range(2):
        features_out[:, side * half : (side + 1) * half] = dot(flat_s[...], linear_s[side]).astype(BF)
    centred = centre(features_out[...].astype(F32))
    scale_one = lax.rsqrt(jnp.mean(centred * centred, axis=1, keepdims=True) + EPSILON)
    standard = centred * scale_one
    standard_out[...] = standard
    normed = (standard * rows[9:10, :]).astype(BF)

    @pl.when(step == 0)
    def _():
        copies[2].wait()
        copies[3].wait()

    row_keep = keep_out[:, 0:1]
    value = dot(normed, up_s[0])
    value_out[...] = value
    gate = jax.nn.sigmoid(dot(normed, up_s[1]))
    gate_out[...] = gate
    reach = 4 * BLOCK
    gated_s[0:reach, :] = jnp.zeros((reach, gated_s.shape[1]), F32)
    gated_s[reach + ROWS :, :] = jnp.zeros((reach, gated_s.shape[1]), F32)
    gated_s[reach : reach + ROWS, :] = (row_keep * value * gate).astype(BF).astype(F32)
    total = None
    for k in range(9):
        term = gated_s[k * BLOCK : k * BLOCK + ROWS, :] * rows[k : k + 1, :]
        total = term if total is None else total + term
    centred = centre(total)
    scale_two = lax.rsqrt(jnp.mean(centred * centred, axis=1, keepdims=True) + EPSILON)
    standard_two = centred * scale_two
    standard_two_out[...] = standard_two
    active = standard_two * rows[10:11, :]
    hidden = (active * jax.nn.sigmoid(active)).astype(BF)
    hidden_out[...] = hidden
    scales_out[:, 0:128] = jnp.broadcast_to(scale_one, (ROWS, 128))
    scales_out[:, 128:256] = jnp.broadcast_to(scale_two, (ROWS, 128))
    kept = jnp.where(row_keep > 0, hidden, jnp.zeros_like(hidden))
    kept = dot(row_order(), kept).astype(BF)
    kept_out[me] = kept[:, :half]
    kept_out[1 - me] = kept[:, half:]


def backward_kernel(
    hidden_in, features_in, standard_in, value_in, gate_in, standard_two_in, scales_in, keep_in, rows, cotangent,
    down_mine, down_other, up_mine, up_other,
    layer_out, grad_out,
    down_s, up_s, depth_s, sems,
):
    step = pl.program_id(0)
    me = lax.axis_index("fsdp")
    copies = fetch(((down_mine, down_other, down_s), (up_mine, up_other, up_s)), sems, me)

    @pl.when(step == 0)
    def _():
        for copy in copies:
            copy.start()

    order = row_order()
    row_keep = keep_in[:, 0:1]
    back_out = jnp.where(row_keep > 0, dot(order, cotangent[...], DOWN), 0.0)
    back_bf = back_out.astype(BF)
    standard_two = standard_two_in[...]
    active = standard_two * rows[10:11, :]
    swish = jax.nn.sigmoid(active)
    slope = (swish + active * swish * (1.0 - swish)) * rows[10:11, :]

    @pl.when(step == 0)
    def _():
        copies[0].wait()
        copies[1].wait()

    half = down_s.shape[1]
    mixed = dot(hidden_in[:, :half], down_s[0]) + dot(hidden_in[:, half:], down_s[1])
    layer = jnp.where(row_keep > 0, features_in[...].astype(F32) + mixed, 0.0).astype(BF)
    layer_out[...] = dot(order, layer).astype(BF)
    back_hidden = jnp.concatenate([dot(back_bf, down_s[0], ACROSS), dot(back_bf, down_s[1], ACROSS)], axis=1)
    gain_up = back_hidden * slope
    scale_one = scales_in[:, 0:1]
    scale_two = scales_in[:, 128:129]
    back_depth = scale_two * (
        gain_up
        - jnp.mean(gain_up, axis=1, keepdims=True)
        - standard_two * jnp.mean(gain_up * standard_two, axis=1, keepdims=True)
    )
    reach = 4 * BLOCK
    depth_s[0:reach, :] = jnp.zeros((reach, depth_s.shape[1]), F32)
    depth_s[reach + ROWS :, :] = jnp.zeros((reach, depth_s.shape[1]), F32)
    depth_s[reach : reach + ROWS, :] = back_depth
    total = None
    for k in range(9):
        term = depth_s[(8 - k) * BLOCK : (8 - k) * BLOCK + ROWS, :] * rows[k : k + 1, :]
        total = term if total is None else total + term
    back_gated = row_keep * total
    gate = gate_in[...]
    back_value = back_gated * gate
    back_gate = (back_value * value_in[...] * (1.0 - gate)).astype(BF)

    @pl.when(step == 0)
    def _():
        copies[2].wait()
        copies[3].wait()

    back_normed = dot(back_value.astype(BF), up_s[0], ACROSS) + dot(back_gate, up_s[1], ACROSS)
    gain_in = back_normed * rows[9:10, :]
    standard = standard_in[...]
    back_input = scale_one * (
        gain_in
        - jnp.mean(gain_in, axis=1, keepdims=True)
        - standard * jnp.mean(gain_in * standard, axis=1, keepdims=True)
    )
    grad_out[...] = dot(order, (back_out + back_input).astype(BF)).astype(BF)


def whole(shape):
    return pl.BlockSpec(shape, lambda g: (0,) * len(shape))


def params(megabytes):
    return pltpu.CompilerParams(vmem_limit_bytes=megabytes * 1024 * 1024)


def cost(flops, moved):
    return pl.CostEstimate(flops=int(flops), bytes_accessed=int(moved), transcendentals=0)


def swap_cores(block):
    return lax.ppermute(block, "fsdp", [(0, 1), (1, 0)])


def swap_bit(block, bit, groups):
    return lax.ppermute(block, "dp", [(i, i ^ (1 << bit)) for i in range(groups)])


def pick(block, index):
    return lax.dynamic_index_in_dim(block, index, axis=0, keepdims=False)


def halve(total, bit, groups):
    side = (lax.axis_index("dp") >> bit) & 1
    pair = total.reshape(2, total.shape[0] // 2, total.shape[1])
    given = swap_bit(pick(pair, 1 - side).astype(jnp.bfloat16), bit, groups)
    return pick(pair, side) + given.astype(jnp.float32)


def double(block, bit, groups):
    side = (lax.axis_index("dp") >> bit) & 1
    given = swap_bit(block, bit, groups)
    return jnp.concatenate(
        [jnp.where(side == 0, block, given), jnp.where(side == 0, given, block)], axis=0
    )


def sum_over_dp(total, scale, groups):
    bits = groups.bit_length() - 1
    half = total.shape[1] // 2
    orders = ([0, 1], [1, 0])
    parts = [total[:, :half], total[:, half:]]
    for step in range(2):
        parts = [halve(part, order[step], groups) for part, order in zip(parts, orders)]
    joined = jnp.concatenate(parts, axis=1)
    for bit in range(2, bits - 1):
        joined = halve(joined, bit, groups)
    rounded = joined.astype(jnp.bfloat16)
    given = swap_bit(rounded, bits - 1, groups)
    block = ((rounded.astype(jnp.float32) + given.astype(jnp.float32)) * scale).astype(jnp.bfloat16)
    for bit in reversed(range(2, bits - 1)):
        block = double(block, bit, groups)
    parts = [block[:, :half], block[:, half:]]
    for step in reversed(range(2)):
        parts = [double(part, order[step], groups) for part, order in zip(parts, orders)]
    return jnp.concatenate(parts, axis=1).astype(jnp.float32)


def local(
    mel_panels,
    frames,
    target,
    conv_first,
    depth_a,
    point_a,
    depth_b,
    point_b,
    linear_weight,
    norm_gain,
    up_weight,
    depth_kernel,
    conv_gain,
    down_weight,
    cotangent,
):
    groups = lax.axis_size("dp")
    members = lax.axis_size("fsdp")
    slots, width_in = mel_panels.shape
    rows_here, width = cotangent.shape
    blocks = rows_here // ROWS
    half = width // members
    shape = jax.ShapeDtypeStruct
    outgoing, packed = pl.pallas_call(
        send_kernel,
        out_shape=(shape((groups, width_in + 128), BF), shape((160, 512), BF)),
        scratch_shapes=[pltpu.VMEM((32, 512), F32)],
        compiler_params=params(16),
        cost_estimate=cost(2e8, 1e6),
        name="send",
    )(
        mel_panels, frames.reshape(1, slots), target.reshape(1, slots), conv_first, depth_a, point_a, depth_b, point_b,
        norm_gain.reshape(1, half), depth_kernel, conv_gain.reshape(1, half),
    )
    incoming = lax.all_to_all(outgoing, "dp", split_axis=0, concat_axis=0, tiled=True)
    packed_other = swap_cores(packed)
    linear_other = swap_cores(linear_weight)
    up_other = swap_cores(up_weight)
    down_other = swap_cores(down_weight)
    cotangent_other = swap_cores(cotangent)
    band, taps_a, taps_b, point_one, point_two, rows = pl.pallas_call(
        weights_kernel,
        out_shape=(
            shape((256, GROUP * 256), BF),
            shape((16, 256), F32),
            shape((16, 256), F32),
            shape((256, 256), BF),
            shape((256, 256), BF),
            shape((16, width), F32),
        ),
        compiler_params=params(16),
        cost_estimate=cost(2e8, 2e6),
        name="weights",
    )(packed, packed_other)

    def by_rows(columns):
        return pl.BlockSpec((ROWS, columns), lambda g: (g, 0))

    anywhere = pl.BlockSpec(memory_space=pl.ANY)
    hidden, kept, features, standard, value, gate, standard_two, scales, keep = pl.pallas_call(
        forward_kernel,
        grid=(blocks,),
        in_specs=[
            whole(incoming.shape), whole(band.shape), whole(taps_a.shape), whole(taps_b.shape), whole(point_one.shape),
            whole(point_two.shape), whole(rows.shape), anywhere, anywhere, anywhere, anywhere,
        ],
        out_specs=[
            by_rows(width), pl.BlockSpec((members, ROWS, half), lambda g: (0, g, 0)), by_rows(width), by_rows(width),
            by_rows(width), by_rows(width), by_rows(width), by_rows(256), by_rows(128),
        ],
        out_shape=(
            shape((rows_here, width), BF),
            shape((members, rows_here, half), BF),
            shape((rows_here, width), BF),
            shape((rows_here, width), F32),
            shape((rows_here, width), F32),
            shape((rows_here, width), F32),
            shape((rows_here, width), F32),
            shape((rows_here, 256), F32),
            shape((rows_here, 128), F32),
        ),
        scratch_shapes=[
            pltpu.VMEM((2,) + linear_weight.shape, BF),
            pltpu.VMEM((2,) + up_weight.shape, BF),
            pltpu.VMEM((ROWS, LEAD + width_in // SPAN), F32),
            pltpu.VMEM((4, 5 * ROWS, 256), BF),
            pltpu.VMEM((GROUP + 1, 5 * ROWS, 256), F32),
            pltpu.VMEM((GROUP * ROWS, 256), BF),
            pltpu.VMEM((BINS // 2, ROWS, 256), F32),
            pltpu.VMEM((BINS // 2, ROWS + BLOCK, 256), F32),
            pltpu.VMEM((ROWS, BINS // 4 * 256), BF),
            pltpu.VMEM((ROWS + 8 * BLOCK, width), F32),
            pltpu.SemaphoreType.DMA((4,)),
        ],
        compiler_params=params(52),
        cost_estimate=cost(2e10 * blocks, 1e7),
        name="forward",
    )(incoming, band, taps_a, taps_b, point_one, point_two, rows, linear_weight, linear_other, up_weight, up_other)
    kept_mine = pick(kept, 0)
    kept_other = swap_cores(pick(kept, 1))
    product = dot(kept_mine, cotangent, DOWN) + dot(kept_other, cotangent_other, DOWN)
    scale = 1.0 / math.sqrt(rows_here * groups * members)
    grad_down = sum_over_dp(product, scale, groups)
    layer_out, grad_input = pl.pallas_call(
        backward_kernel,
        grid=(blocks,),
        in_specs=[
            by_rows(width), by_rows(width), by_rows(width), by_rows(width), by_rows(width), by_rows(width), by_rows(256),
            by_rows(128), whole(rows.shape), by_rows(width), anywhere, anywhere, anywhere, anywhere,
        ],
        out_specs=[by_rows(width), by_rows(width)],
        out_shape=(shape((rows_here, width), BF), shape((rows_here, width), BF)),
        scratch_shapes=[
            pltpu.VMEM((2,) + down_weight.shape, BF),
            pltpu.VMEM((2,) + up_weight.shape, BF),
            pltpu.VMEM((ROWS + 8 * BLOCK, width), F32),
            pltpu.SemaphoreType.DMA((4,)),
        ],
        compiler_params=params(32),
        cost_estimate=cost(4e9 * blocks, 1e7),
        name="backward",
    )(
        hidden, features, standard, value, gate, standard_two, scales, keep, rows, cotangent,
        down_weight, down_other, up_weight, up_other,
    )
    return (layer_out, grad_input, grad_down)


def solution(mesh):
    placed = (
        P(("dp", "fsdp"), None),
        P(("dp", "fsdp")),
        P(("dp", "fsdp")),
        P(None, "fsdp"),
        P(None, "fsdp"),
        P(None, "fsdp"),
        P(None, "fsdp"),
        P(None, "fsdp"),
        P(None, "fsdp"),
        P("fsdp"),
        P(None, "fsdp"),
        P(None, "fsdp"),
        P("fsdp"),
        P("fsdp", None),
        P(("dp", "fsdp"), None),
    )
    return jax.shard_map(
        local,
        mesh=mesh,
        in_specs=placed,
        out_specs=(P(("dp", "fsdp"), None), P(("dp", "fsdp"), None), P("fsdp", None)),
        check_vma=False,
    )
```

```python
import functools
import math

import jax
import jax.numpy as jnp
from jax import lax
from jax.experimental import pallas as pl
from jax.experimental.pallas import tpu as pltpu
from jax.sharding import PartitionSpec as P

MELS = 80
PANEL = 128
EPSILON = 1e-05
SPAN = PANEL // 8
BLOCK = 8
ROWS = BLOCK * SPAN
BINS = 40
GROUP = 10
WINDOW = 2 * GROUP + 1
LEAD = 256
BF = jnp.bfloat16
F32 = jnp.float32
ACROSS = (((1,), (1,)), ((), ()))
DOWN = (((0,), (0,)), ((), ()))


def dot(left, right, dims=(((1,), (0,)), ((), ()))):
    return lax.dot_general(left, right, dims, preferred_element_type=F32)


def iota(shape, dim):
    return lax.broadcasted_iota(jnp.int32, shape, dim)


def row_order():
    n = iota((ROWS, ROWS), 0)
    r = iota((ROWS, ROWS), 1)
    return jnp.where((n % SPAN) * BLOCK + n // SPAN == r, 1.0, 0.0).astype(BF)


def send_kernel(
    mel, frames, target, first, depth_a, point_a, depth_b, point_b, norm_gain, depth_kernel, conv_gain,
    outgoing, packed,
    mel_s, first_s, depth_a_s, point_a_s, depth_b_s, point_b_s, norm_s, kernel_s, conv_s, rows, lines, sems,
):
    pairs = (
        (mel, mel_s), (first, first_s), (depth_a, depth_a_s), (point_a, point_a_s), (depth_b, depth_b_s),
        (point_b, point_b_s), (norm_gain, norm_s), (depth_kernel, kernel_s), (conv_gain, conv_s),
    )
    copies = [pltpu.make_async_copy(source, held, sems.at[n]) for n, (source, held) in enumerate(pairs)]
    for copy in copies:
        copy.start()
    count = outgoing.shape[0]
    slots = mel_s.shape[0]
    lanes = mel_s.shape[1] // 128
    wanted = iota((count, slots), 0)
    chosen = jnp.where((target[...] == wanted) & (frames[...] > 0), 1.0, 0.0)
    sent = jnp.sum(chosen * frames[...].astype(F32), axis=1, keepdims=True)
    sent = jnp.broadcast_to(sent, (count, 128))
    for k in range(8):
        lines[pl.ds(lanes + k, count, stride=lanes + 8), :] = sent
    copies[0].wait()
    chosen = chosen.astype(BF)
    for k in range(lanes):
        lines[pl.ds(k, count, stride=lanes + 8), :] = dot(chosen, mel_s[:, k * 128 : (k + 1) * 128])
    for d in range(count):
        outgoing[d] = lines[d * (lanes + 8) : (d + 1) * (lanes + 8), :].astype(BF)
    for copy in copies[1:]:
        copy.wait()
    rows[...] = jnp.zeros_like(rows)
    rows[0:9, :] = kernel_s[...].astype(F32)
    rows[9:10, :] = norm_s[...].astype(F32).reshape(1, 512)
    rows[10:11, :] = conv_s[...].astype(F32).reshape(1, 512)
    rows[16:25, 0:128] = first_s[...].astype(F32)
    rows[16:25, 128:256] = depth_a_s[...].astype(F32)
    rows[16:25, 256:384] = depth_b_s[...].astype(F32)
    packed[0:32, :] = rows[...].astype(BF)
    packed[32:160, 0:128] = point_a_s[0:128, :]
    packed[32:160, 128:256] = point_a_s[128:256, :]
    packed[32:160, 256:384] = point_b_s[0:128, :]
    packed[32:160, 384:512] = point_b_s[128:256, :]


def weights_kernel(mine, other, band, taps_a, taps_b, point_a, point_b, rows):
    me = lax.axis_index("fsdp")
    near = mine[...].astype(F32)
    far = other[...].astype(F32)
    low = jnp.where(me == 0, near, far)
    high = jnp.where(me == 0, far, near)
    rows[:, 0:512] = low[0:16]
    rows[:, 512:1024] = high[0:16]
    first = jnp.concatenate([low[16:32, 0:128], high[16:32, 0:128]], axis=1).astype(BF)
    taps_a[...] = jnp.concatenate([low[16:32, 128:256], high[16:32, 128:256]], axis=1)
    taps_b[...] = jnp.concatenate([low[16:32, 256:384], high[16:32, 256:384]], axis=1)
    for half, source in ((0, low), (1, high)):
        at = slice(half * 128, half * 128 + 128)
        point_a[0:128, at] = source[32:160, 0:128].astype(BF)
        point_a[128:256, at] = source[32:160, 128:256].astype(BF)
        point_b[0:128, at] = source[32:160, 256:384].astype(BF)
        point_b[128:256, at] = source[32:160, 384:512].astype(BF)
    tap = iota((256, 16), 1)
    base = jnp.where(tap < 9, (tap // 3) * MELS + tap % 3, -1000) - iota((256, 16), 0)
    for f in range(GROUP):
        place = jnp.where(base == -2 * f, 1.0, 0.0).astype(BF)
        band[:, f * 256 : (f + 1) * 256] = dot(place, first).astype(BF)


def fetch(pairs, sems, me):
    copies = []
    for number, (mine, other, held) in enumerate(pairs):
        copies.append(pltpu.make_async_copy(mine, held.at[me], sems.at[2 * number]))
        copies.append(pltpu.make_async_copy(other, held.at[1 - me], sems.at[2 * number + 1]))
    return copies


def centre(values):
    return values - jnp.mean(values, axis=1, keepdims=True)


def forward_kernel(
    incoming, band, taps_a, taps_b, point_a, point_b, rows, linear_mine, linear_other, up_mine, up_other,
    hidden_out, kept_out, features_out, standard_out, value_out, gate_out, standard_two_out, scales_out, keep_out,
    linear_s, up_s, pick_s, ext_s, x_s, first_s, spread_s, even_s, odd_s, flat_s, gated_s, sems,
):
    step = pl.program_id(0)
    me = lax.axis_index("fsdp")
    copies = fetch(((linear_mine, linear_other, linear_s), (up_mine, up_other, up_s)), sems, me)

    @pl.when(step == 0)
    def _():
        for copy in copies:
            copy.start()

    sources = incoming.shape[0]
    lanes = incoming.shape[1] - 8
    got = jnp.concatenate([incoming[source, lanes:, :].astype(F32)[0:1] for source in range(sources)], axis=0)
    present = jnp.where(got > 0, 1.0, 0.0)
    below = jnp.where(iota((sources, sources), 1) <= iota((sources, sources), 0), 1.0, 0.0).astype(BF)
    position = dot(below, present.astype(BF)) - 1.0
    slot = (iota((sources, 128), 1) + step * BLOCK).astype(F32)
    placing = jnp.where((position == slot) & (present > 0), 1.0, 0.0).astype(BF)[:, :BLOCK]
    length = dot(placing, got.astype(BF), DOWN)
    source = dot(placing, iota((sources, 128), 0).astype(F32).astype(BF), DOWN)
    per_step = lanes // SPAN
    lane = iota((BLOCK, 128), 1).astype(F32)
    base = source * lanes - lane
    for t in range(SPAN):
        live = length > 8.0 * t
        keep_out[t * BLOCK : (t + 1) * BLOCK, :] = jnp.where(live, 1.0, 0.0)
        here = jnp.where(live, base, -1e6)
        for k in range(per_step):
            at = k * ROWS + t * BLOCK
            for c in range(sources * lanes // 128):
                hit = here == 128.0 * c - (per_step * t + k)
                pick_s[at : at + BLOCK, c * 128 : (c + 1) * 128] = jnp.where(hit, 1.0, 0.0)
    lines = jnp.concatenate([incoming[source, :lanes, :] for source in range(sources)], axis=0)
    placed = dot(pick_s[...].astype(BF), lines)
    ext_s[0:BLOCK, 0:LEAD] = jnp.zeros((BLOCK, LEAD), F32)
    for k in range(per_step):
        part = placed[k * ROWS : (k + 1) * ROWS]
        ext_s[:, LEAD + k * 128 : LEAD + (k + 1) * 128] = part
        ahead = k + LEAD // 128 - per_step
        if ahead >= 0:
            ext_s[BLOCK:, ahead * 128 : (ahead + 1) * 128] = part[: ROWS - BLOCK]
    lane = iota((ROWS, 256), 1)
    edge = (lane == 0) | (lane == MELS) | (lane == 2 * MELS)
    for q in range(5):
        for b in range(4):
            start = LEAD + (2 * q - 3) * MELS + 2 * GROUP * b - 1
            tile = start // 128 * 128
            shift = start - tile
            span = 256 if shift + 2 * MELS + WINDOW <= 256 else 384
            part = ext_s[:, tile : tile + span]
            part = pltpu.roll(part, span - shift, 1)[:, :256]
            if b == 0:
                part = jnp.where(edge, 0.0, part)
            x_s[b, q * ROWS : (q + 1) * ROWS, :] = part.astype(BF)

    first_s[0] = jnp.zeros(first_s.shape[1:], F32)
    odd_s[:, 0:BLOCK, :] = jnp.zeros((odd_s.shape[0], BLOCK, 256), F32)

    def section(b, carry):
        source = x_s[b]
        for f in range(GROUP):
            first_s[1 + f] = jnp.maximum(dot(source, band[:, f * 256 : (f + 1) * 256]), 0.0)
        for g in range(GROUP // 2):
            for s in range(2):
                total = None
                for j in range(3):
                    for i in range(3):
                        at = (2 * s + i) * ROWS
                        term = first_s[2 * g + j, at : at + ROWS, :] * taps_a[3 * i + j : 3 * i + j + 1, :]
                        total = term if total is None else total + term
                spread_s[(2 * g + s) * ROWS : (2 * g + s + 1) * ROWS, :] = total.astype(BF)
        first_s[0] = first_s[GROUP]
        second = jnp.maximum(dot(spread_s[...], point_a[...]), 0.0)
        for g in range(GROUP // 2):
            even_s[b * (GROUP // 2) + g] = second[2 * g * ROWS : (2 * g + 1) * ROWS]
            odd_s[b * (GROUP // 2) + g, BLOCK:, :] = second[(2 * g + 1) * ROWS : (2 * g + 2) * ROWS]
        return carry

    lax.fori_loop(0, BINS // GROUP, section, 0)

    for f in range(BINS // 4):
        total = None
        for j in range(3):
            at = 2 * f + j - 1
            if at < 0:
                continue
            for i, view in enumerate((odd_s.at[at, 0:ROWS, :], even_s.at[at], odd_s.at[at, BLOCK : BLOCK + ROWS, :])):
                term = view[...] * taps_b[3 * i + j : 3 * i + j + 1, :]
                total = term if total is None else total + term
        fourth = jnp.maximum(dot(total.astype(BF), point_b[...]), 0.0)
        flat_s[:, f * 256 : (f + 1) * 256] = fourth.astype(BF)

    @pl.when(step == 0)
    def _():
        copies[0].wait()
        copies[1].wait()

    half = linear_s.shape[2]
    for side in range(2):
        features_out[:, side * half : (side + 1) * half] = dot(flat_s[...], linear_s[side]).astype(BF)
    centred = centre(features_out[...].astype(F32))
    scale_one = lax.rsqrt(jnp.mean(centred * centred, axis=1, keepdims=True) + EPSILON)
    standard = centred * scale_one
    standard_out[...] = standard
    normed = (standard * rows[9:10, :]).astype(BF)

    @pl.when(step == 0)
    def _():
        copies[2].wait()
        copies[3].wait()

    row_keep = keep_out[:, 0:1]
    value = dot(normed, up_s[0])
    value_out[...] = value
    gate = jax.nn.sigmoid(dot(normed, up_s[1]))
    gate_out[...] = gate
    reach = 4 * BLOCK
    gated_s[0:reach, :] = jnp.zeros((reach, gated_s.shape[1]), F32)
    gated_s[reach + ROWS :, :] = jnp.zeros((reach, gated_s.shape[1]), F32)
    gated_s[reach : reach + ROWS, :] = (row_keep * value * gate).astype(BF).astype(F32)
    total = None
    for k in range(9):
        term = gated_s[k * BLOCK : k * BLOCK + ROWS, :] * rows[k : k + 1, :]
        total = term if total is None else total + term
    centred = centre(total)
    scale_two = lax.rsqrt(jnp.mean(centred * centred, axis=1, keepdims=True) + EPSILON)
    standard_two = centred * scale_two
    standard_two_out[...] = standard_two
    active = standard_two * rows[10:11, :]
    hidden = (active * jax.nn.sigmoid(active)).astype(BF)
    hidden_out[...] = hidden
    scales_out[:, 0:128] = jnp.broadcast_to(scale_one, (ROWS, 128))
    scales_out[:, 128:256] = jnp.broadcast_to(scale_two, (ROWS, 128))
    kept = jnp.where(row_keep > 0, hidden, jnp.zeros_like(hidden))
    kept = dot(row_order(), kept).astype(BF)
    kept_out[me] = kept[:, :half]
    kept_out[1 - me] = kept[:, half:]


def backward_kernel(
    hidden_in, features_in, standard_in, value_in, gate_in, standard_two_in, scales_in, keep_in, rows, cotangent,
    down_mine, down_other, up_mine, up_other,
    layer_out, grad_out,
    down_s, up_s, depth_s, sems,
):
    step = pl.program_id(0)
    me = lax.axis_index("fsdp")
    copies = fetch(((down_mine, down_other, down_s), (up_mine, up_other, up_s)), sems, me)

    @pl.when(step == 0)
    def _():
        for copy in copies:
            copy.start()

    order = row_order()
    row_keep = keep_in[:, 0:1]
    back_out = jnp.where(row_keep > 0, dot(order, cotangent[...], DOWN), 0.0)
    back_bf = back_out.astype(BF)
    standard_two = standard_two_in[...]
    active = standard_two * rows[10:11, :]
    swish = jax.nn.sigmoid(active)
    slope = (swish + active * swish * (1.0 - swish)) * rows[10:11, :]

    @pl.when(step == 0)
    def _():
        copies[0].wait()
        copies[1].wait()

    half = down_s.shape[1]
    mixed = dot(hidden_in[:, :half], down_s[0]) + dot(hidden_in[:, half:], down_s[1])
    layer = jnp.where(row_keep > 0, features_in[...].astype(F32) + mixed, 0.0).astype(BF)
    layer_out[...] = dot(order, layer).astype(BF)
    back_hidden = jnp.concatenate([dot(back_bf, down_s[0], ACROSS), dot(back_bf, down_s[1], ACROSS)], axis=1)
    gain_up = back_hidden * slope
    scale_one = scales_in[:, 0:1]
    scale_two = scales_in[:, 128:129]
    back_depth = scale_two * (
        gain_up
        - jnp.mean(gain_up, axis=1, keepdims=True)
        - standard_two * jnp.mean(gain_up * standard_two, axis=1, keepdims=True)
    )
    reach = 4 * BLOCK
    depth_s[0:reach, :] = jnp.zeros((reach, depth_s.shape[1]), F32)
    depth_s[reach + ROWS :, :] = jnp.zeros((reach, depth_s.shape[1]), F32)
    depth_s[reach : reach + ROWS, :] = back_depth
    total = None
    for k in range(9):
        term = depth_s[(8 - k) * BLOCK : (8 - k) * BLOCK + ROWS, :] * rows[k : k + 1, :]
        total = term if total is None else total + term
    back_gated = row_keep * total
    gate = gate_in[...]
    back_value = back_gated * gate
    back_gate = (back_value * value_in[...] * (1.0 - gate)).astype(BF)

    @pl.when(step == 0)
    def _():
        copies[2].wait()
        copies[3].wait()

    back_normed = dot(back_value.astype(BF), up_s[0], ACROSS) + dot(back_gate, up_s[1], ACROSS)
    gain_in = back_normed * rows[9:10, :]
    standard = standard_in[...]
    back_input = scale_one * (
        gain_in
        - jnp.mean(gain_in, axis=1, keepdims=True)
        - standard * jnp.mean(gain_in * standard, axis=1, keepdims=True)
    )
    grad_out[...] = dot(order, (back_out + back_input).astype(BF)).astype(BF)


def whole(shape):
    return pl.BlockSpec(shape, lambda g: (0,) * len(shape))


def params(megabytes):
    return pltpu.CompilerParams(vmem_limit_bytes=megabytes * 1024 * 1024)


def cost(flops, moved):
    return pl.CostEstimate(flops=int(flops), bytes_accessed=int(moved), transcendentals=0)


def swap_cores(block):
    return lax.ppermute(block, "fsdp", [(0, 1), (1, 0)])


def swap_bit(block, bit, groups):
    return lax.ppermute(block, "dp", [(i, i ^ (1 << bit)) for i in range(groups)])


def pick(block, index):
    return lax.dynamic_index_in_dim(block, index, axis=0, keepdims=False)


def halve(total, bit, groups, beside=()):
    side = (lax.axis_index("dp") >> bit) & 1
    pair = total.reshape(2, total.shape[0] // 2, total.shape[1])
    given = swap_bit(pick(pair, 1 - side).astype(jnp.bfloat16), bit, groups)
    if beside:
        given, *beside = lax.optimization_barrier((given, *beside))
    return pick(pair, side) + given.astype(jnp.float32), beside


def double(block, bit, groups):
    side = (lax.axis_index("dp") >> bit) & 1
    given = swap_bit(block, bit, groups)
    return jnp.concatenate(
        [jnp.where(side == 0, block, given), jnp.where(side == 0, given, block)], axis=0
    )


def sum_over_dp(total, scale, groups, beside):
    bits = groups.bit_length() - 1
    half = total.shape[1] // 2
    orders = ([0, 1], [1, 0])
    parts = [total[:, :half], total[:, half:]]
    parts[0], beside = halve(parts[0], orders[0][0], groups, beside)
    parts[1], _ = halve(parts[1], orders[1][0], groups)
    parts = [halve(part, order[1], groups)[0] for part, order in zip(parts, orders)]
    joined = jnp.concatenate(parts, axis=1)
    for bit in range(2, bits - 1):
        joined, _ = halve(joined, bit, groups)
    rounded = joined.astype(jnp.bfloat16)
    given = swap_bit(rounded, bits - 1, groups)
    block = ((rounded.astype(jnp.float32) + given.astype(jnp.float32)) * scale).astype(jnp.bfloat16)
    for bit in reversed(range(2, bits - 1)):
        block = double(block, bit, groups)
    parts = [block[:, :half], block[:, half:]]
    for step in reversed(range(2)):
        parts = [double(part, order[step], groups) for part, order in zip(parts, orders)]
    return jnp.concatenate(parts, axis=1).astype(jnp.float32), beside


def local(
    mel_panels,
    frames,
    target,
    conv_first,
    depth_a,
    point_a,
    depth_b,
    point_b,
    linear_weight,
    norm_gain,
    up_weight,
    depth_kernel,
    conv_gain,
    down_weight,
    cotangent,
):
    groups = lax.axis_size("dp")
    members = lax.axis_size("fsdp")
    slots, width_in = mel_panels.shape
    rows_here, width = cotangent.shape
    blocks = rows_here // ROWS
    half = width // members
    shape = jax.ShapeDtypeStruct
    lines = width_in // 128 + 8
    anywhere = pl.BlockSpec(memory_space=pltpu.HBM)
    held = pl.BlockSpec(memory_space=pltpu.VMEM)
    small = (conv_first, depth_a, point_a, depth_b, point_b, norm_gain, depth_kernel, conv_gain)
    outgoing, packed = pl.pallas_call(
        send_kernel,
        in_specs=[anywhere, held, held] + [anywhere] * len(small),
        out_shape=(shape((groups, lines, 128), BF), shape((160, 512), BF)),
        scratch_shapes=[pltpu.VMEM(array.shape, BF) for array in (mel_panels,) + small]
        + [
            pltpu.VMEM((32, 512), F32),
            pltpu.VMEM((groups * lines, 128), F32),
            pltpu.SemaphoreType.DMA((1 + len(small),)),
        ],
        compiler_params=params(60),
        cost_estimate=cost(2e8, 1e6),
        name="send",
    )(mel_panels, frames.reshape(1, slots), target.reshape(1, slots), *small)
    incoming = lax.all_to_all(outgoing, "dp", split_axis=0, concat_axis=0, tiled=True)
    packed_other = swap_cores(packed)
    linear_other = swap_cores(linear_weight)
    up_other = swap_cores(up_weight)
    down_other = swap_cores(down_weight)
    cotangent_other = swap_cores(cotangent)
    band, taps_a, taps_b, point_one, point_two, rows = pl.pallas_call(
        weights_kernel,
        out_shape=(
            shape((256, GROUP * 256), BF),
            shape((16, 256), F32),
            shape((16, 256), F32),
            shape((256, 256), BF),
            shape((256, 256), BF),
            shape((16, width), F32),
        ),
        compiler_params=params(16),
        cost_estimate=cost(2e8, 2e6),
        name="weights",
    )(packed, packed_other)

    def by_rows(columns):
        return pl.BlockSpec((ROWS, columns), lambda g: (g, 0))

    hidden, kept, features, standard, value, gate, standard_two, scales, keep = pl.pallas_call(
        forward_kernel,
        grid=(blocks,),
        in_specs=[
            whole(incoming.shape), whole(band.shape), whole(taps_a.shape), whole(taps_b.shape), whole(point_one.shape),
            whole(point_two.shape), whole(rows.shape), anywhere, anywhere, anywhere, anywhere,
        ],
        out_specs=[
            by_rows(width), pl.BlockSpec((members, ROWS, half), lambda g: (0, g, 0)), by_rows(width), by_rows(width),
            by_rows(width), by_rows(width), by_rows(width), by_rows(256), by_rows(128),
        ],
        out_shape=(
            shape((rows_here, width), BF),
            shape((members, rows_here, half), BF),
            shape((rows_here, width), BF),
            shape((rows_here, width), F32),
            shape((rows_here, width), F32),
            shape((rows_here, width), F32),
            shape((rows_here, width), F32),
            shape((rows_here, 256), F32),
            shape((rows_here, 128), F32),
        ),
        scratch_shapes=[
            pltpu.VMEM((2,) + linear_weight.shape, BF),
            pltpu.VMEM((2,) + up_weight.shape, BF),
            pltpu.VMEM((ROWS * width_in // SPAN // 128, groups * width_in // 128), F32),
            pltpu.VMEM((ROWS, LEAD + width_in // SPAN), F32),
            pltpu.VMEM((4, 5 * ROWS, 256), BF),
            pltpu.VMEM((GROUP + 1, 5 * ROWS, 256), F32),
            pltpu.VMEM((GROUP * ROWS, 256), BF),
            pltpu.VMEM((BINS // 2, ROWS, 256), F32),
            pltpu.VMEM((BINS // 2, ROWS + BLOCK, 256), F32),
            pltpu.VMEM((ROWS, BINS // 4 * 256), BF),
            pltpu.VMEM((ROWS + 8 * BLOCK, width), F32),
            pltpu.SemaphoreType.DMA((4,)),
        ],
        compiler_params=params(44),
        cost_estimate=cost(2e10 * blocks, 1e7),
        name="forward",
    )(incoming, band, taps_a, taps_b, point_one, point_two, rows, linear_weight, linear_other, up_weight, up_other)
    kept_mine = kept[0]
    kept_other = swap_cores(kept[1])
    product = dot(kept_mine, cotangent, DOWN) + dot(kept_other, cotangent_other, DOWN)
    scale = 1.0 / math.sqrt(rows_here * groups * members)
    beside = pl.pallas_call(
        backward_kernel,
        grid=(blocks,),
        in_specs=[
            by_rows(width), by_rows(width), by_rows(width), by_rows(width), by_rows(width), by_rows(width), by_rows(256),
            by_rows(128), whole(rows.shape), by_rows(width), anywhere, anywhere, anywhere, anywhere,
        ],
        out_specs=[by_rows(width), by_rows(width)],
        out_shape=(shape((rows_here, width), BF), shape((rows_here, width), BF)),
        scratch_shapes=[
            pltpu.VMEM((2,) + down_weight.shape, BF),
            pltpu.VMEM((2,) + up_weight.shape, BF),
            pltpu.VMEM((ROWS + 8 * BLOCK, width), F32),
            pltpu.SemaphoreType.DMA((4,)),
        ],
        compiler_params=params(60),
        cost_estimate=cost(1e6, 1e5),
        name="backward",
    )(
        hidden, features, standard, value, gate, standard_two, scales, keep, rows, cotangent,
        down_weight, down_other, up_weight, up_other,
    )
    grad_down, (layer_out, grad_input) = sum_over_dp(product, scale, groups, beside)
    return (layer_out, grad_input, grad_down)


def solution(mesh):
    placed = (
        P(("dp", "fsdp"), None),
        P(("dp", "fsdp")),
        P(("dp", "fsdp")),
        P(None, "fsdp"),
        P(None, "fsdp"),
        P(None, "fsdp"),
        P(None, "fsdp"),
        P(None, "fsdp"),
        P(None, "fsdp"),
        P("fsdp"),
        P(None, "fsdp"),
        P(None, "fsdp"),
        P("fsdp"),
        P("fsdp", None),
        P(("dp", "fsdp"), None),
    )
    return jax.shard_map(
        local,
        mesh=mesh,
        in_specs=placed,
        out_specs=(P(("dp", "fsdp"), None), P(("dp", "fsdp"), None), P("fsdp", None)),
        check_vma=False,
    )
```

```python
import functools
import math

import jax
import jax.numpy as jnp
from jax import lax
from jax.experimental import pallas as pl
from jax.experimental.pallas import tpu as pltpu
from jax.sharding import PartitionSpec as P

MELS = 80
PANEL = 128
EPSILON = 1e-05
SPAN = PANEL // 8
BLOCK = 8
ROWS = BLOCK * SPAN
FRONT = 34
BACK = 14
BINS = 40
GROUP = 10
WINDOW = 2 * GROUP + 1
LEAD = 256
BF = jnp.bfloat16
F32 = jnp.float32
ACROSS = (((1,), (1,)), ((), ()))
DOWN = (((0,), (0,)), ((), ()))


def dot(left, right, dims=(((1,), (0,)), ((), ()))):
    return lax.dot_general(left, right, dims, preferred_element_type=F32)


def iota(shape, dim):
    return lax.broadcasted_iota(jnp.int32, shape, dim)


def row_order():
    n = iota((ROWS, ROWS), 0)
    r = iota((ROWS, ROWS), 1)
    return jnp.where((n % SPAN) * BLOCK + n // SPAN == r, 1.0, 0.0).astype(BF)


def send_kernel(
    mel, frames, target, first, depth_a, point_a, depth_b, point_b, norm_gain, depth_kernel, conv_gain,
    outgoing, packed,
    mel_s, first_s, depth_a_s, point_a_s, depth_b_s, point_b_s, norm_s, kernel_s, conv_s, rows, lines, sems,
):
    pairs = (
        (mel, mel_s), (first, first_s), (depth_a, depth_a_s), (point_a, point_a_s), (depth_b, depth_b_s),
        (point_b, point_b_s), (norm_gain, norm_s), (depth_kernel, kernel_s), (conv_gain, conv_s),
    )
    copies = [pltpu.make_async_copy(source, held, sems.at[n]) for n, (source, held) in enumerate(pairs)]
    for copy in copies:
        copy.start()
    count = outgoing.shape[0]
    slots = mel_s.shape[0]
    lanes = mel_s.shape[1] // 128
    wanted = iota((count, slots), 0)
    chosen = jnp.where((target[...] == wanted) & (frames[...] > 0), 1.0, 0.0)
    sent = jnp.sum(chosen * frames[...].astype(F32), axis=1, keepdims=True)
    sent = jnp.broadcast_to(sent, (count, 128))
    for k in range(8):
        lines[pl.ds(lanes + k, count, stride=lanes + 8), :] = sent
    copies[0].wait()
    chosen = chosen.astype(BF)
    for k in range(lanes):
        lines[pl.ds(k, count, stride=lanes + 8), :] = dot(chosen, mel_s[:, k * 128 : (k + 1) * 128])
    for d in range(count):
        outgoing[d] = lines[d * (lanes + 8) : (d + 1) * (lanes + 8), :].astype(BF)
    for copy in copies[1:]:
        copy.wait()
    rows[...] = jnp.zeros_like(rows)
    rows[0:9, :] = kernel_s[...].astype(F32)
    rows[9:10, :] = norm_s[...].astype(F32).reshape(1, 512)
    rows[10:11, :] = conv_s[...].astype(F32).reshape(1, 512)
    rows[16:25, 0:128] = first_s[...].astype(F32)
    rows[16:25, 128:256] = depth_a_s[...].astype(F32)
    rows[16:25, 256:384] = depth_b_s[...].astype(F32)
    packed[0:32, :] = rows[...].astype(BF)
    packed[32:160, 0:128] = point_a_s[0:128, :]
    packed[32:160, 128:256] = point_a_s[128:256, :]
    packed[32:160, 256:384] = point_b_s[0:128, :]
    packed[32:160, 384:512] = point_b_s[128:256, :]


def weights_kernel(mine, other, band, taps_a, taps_b, point_a, point_b, rows):
    me = lax.axis_index("fsdp")
    near = mine[...].astype(F32)
    far = other[...].astype(F32)
    low = jnp.where(me == 0, near, far)
    high = jnp.where(me == 0, far, near)
    rows[:, 0:512] = low[0:16]
    rows[:, 512:1024] = high[0:16]
    first = jnp.concatenate([low[16:32, 0:128], high[16:32, 0:128]], axis=1).astype(BF)
    taps_a[...] = jnp.concatenate([low[16:32, 128:256], high[16:32, 128:256]], axis=1)
    taps_b[...] = jnp.concatenate([low[16:32, 256:384], high[16:32, 256:384]], axis=1)
    for half, source in ((0, low), (1, high)):
        at = slice(half * 128, half * 128 + 128)
        point_a[0:128, at] = source[32:160, 0:128].astype(BF)
        point_a[128:256, at] = source[32:160, 128:256].astype(BF)
        point_b[0:128, at] = source[32:160, 256:384].astype(BF)
        point_b[128:256, at] = source[32:160, 384:512].astype(BF)
    tap = iota((256, 16), 1)
    base = jnp.where(tap < 9, (tap // 3) * MELS + tap % 3, -1000) - iota((256, 16), 0)
    for f in range(GROUP):
        place = jnp.where(base == -2 * f, 1.0, 0.0).astype(BF)
        band[:, f * 256 : (f + 1) * 256] = dot(place, first).astype(BF)


def fetch(pairs, sems, me):
    copies = []
    for number, (mine, other, held) in enumerate(pairs):
        copies.append(pltpu.make_async_copy(mine, held.at[me], sems.at[2 * number]))
        copies.append(pltpu.make_async_copy(other, held.at[1 - me], sems.at[2 * number + 1]))
    return copies


def centre(values):
    return values - jnp.mean(values, axis=1, keepdims=True)


def forward_kernel(
    incoming, band, taps_a, taps_b, point_a, point_b, rows, linear_mine, linear_other, up_mine, up_other,
    give_0, give_1, give_2, give_3, features_out, value_out, gate_out, standard_two_out, scale_out, keep_out,
    linear_s, up_s, pick_s, ext_s, x_s, first_s, spread_s, even_s, odd_s, flat_s, gated_s, kept_s, sems,
):
    step = pl.program_id(0)
    me = lax.axis_index("fsdp")
    copies = fetch(((linear_mine, linear_other, linear_s), (up_mine, up_other, up_s)), sems, me)

    @pl.when(step == 0)
    def _():
        for copy in copies:
            copy.start()

    sources = incoming.shape[0]
    lanes = incoming.shape[1] - 8
    got = jnp.concatenate([incoming[source, lanes:, :].astype(F32)[0:1] for source in range(sources)], axis=0)
    present = jnp.where(got > 0, 1.0, 0.0)
    below = jnp.where(iota((sources, sources), 1) <= iota((sources, sources), 0), 1.0, 0.0).astype(BF)
    position = dot(below, present.astype(BF)) - 1.0
    slot = (iota((sources, 128), 1) + step * BLOCK).astype(F32)
    placing = jnp.where((position == slot) & (present > 0), 1.0, 0.0).astype(BF)[:, :BLOCK]
    length = dot(placing, got.astype(BF), DOWN)
    source = dot(placing, iota((sources, 128), 0).astype(F32).astype(BF), DOWN)
    per_step = lanes // SPAN
    lane = iota((BLOCK, 128), 1).astype(F32)
    base = source * lanes - lane
    for t in range(SPAN):
        live = length > 8.0 * t
        keep_out[t * BLOCK : (t + 1) * BLOCK, :] = jnp.where(live, 1.0, 0.0)
        here = jnp.where(live, base, -1e6)
        for k in range(per_step):
            at = k * ROWS + t * BLOCK
            for c in range(sources * lanes // 128):
                hit = here == 128.0 * c - (per_step * t + k)
                pick_s[at : at + BLOCK, c * 128 : (c + 1) * 128] = jnp.where(hit, 1.0, 0.0)
    lines = jnp.concatenate([incoming[source, :lanes, :] for source in range(sources)], axis=0)
    placed = dot(pick_s[...].astype(BF), lines)
    ext_s[0:BLOCK, 0:LEAD] = jnp.zeros((BLOCK, LEAD), F32)
    for k in range(per_step):
        part = placed[k * ROWS : (k + 1) * ROWS]
        ext_s[:, LEAD + k * 128 : LEAD + (k + 1) * 128] = part
        ahead = k + LEAD // 128 - per_step
        if ahead >= 0:
            ext_s[BLOCK:, ahead * 128 : (ahead + 1) * 128] = part[: ROWS - BLOCK]
    lane = iota((ROWS, 256), 1)
    edge = (lane == 0) | (lane == MELS) | (lane == 2 * MELS)
    for q in range(5):
        for b in range(4):
            start = LEAD + (2 * q - 3) * MELS + 2 * GROUP * b - 1
            tile = start // 128 * 128
            shift = start - tile
            span = 256 if shift + 2 * MELS + WINDOW <= 256 else 384
            part = ext_s[:, tile : tile + span]
            part = pltpu.roll(part, span - shift, 1)[:, :256]
            if b == 0:
                part = jnp.where(edge, 0.0, part)
            x_s[b, q * ROWS : (q + 1) * ROWS, :] = part.astype(BF)

    first_s[0] = jnp.zeros(first_s.shape[1:], F32)
    odd_s[:, 0:BLOCK, :] = jnp.zeros((odd_s.shape[0], BLOCK, 256), F32)

    def section(b, carry):
        source = x_s[b]
        for f in range(GROUP):
            first_s[1 + f] = jnp.maximum(dot(source, band[:, f * 256 : (f + 1) * 256]), 0.0)
        for g in range(GROUP // 2):
            for s in range(2):
                total = None
                for j in range(3):
                    for i in range(3):
                        at = (2 * s + i) * ROWS
                        term = first_s[2 * g + j, at : at + ROWS, :] * taps_a[3 * i + j : 3 * i + j + 1, :]
                        total = term if total is None else total + term
                spread_s[(2 * g + s) * ROWS : (2 * g + s + 1) * ROWS, :] = total.astype(BF)
        first_s[0] = first_s[GROUP]
        second = jnp.maximum(dot(spread_s[...], point_a[...]), 0.0)
        for g in range(GROUP // 2):
            even_s[b * (GROUP // 2) + g] = second[2 * g * ROWS : (2 * g + 1) * ROWS]
            odd_s[b * (GROUP // 2) + g, BLOCK:, :] = second[(2 * g + 1) * ROWS : (2 * g + 2) * ROWS]
        return carry

    lax.fori_loop(0, BINS // GROUP, section, 0)

    for f in range(BINS // 4):
        total = None
        for j in range(3):
            at = 2 * f + j - 1
            if at < 0:
                continue
            for i, view in enumerate((odd_s.at[at, 0:ROWS, :], even_s.at[at], odd_s.at[at, BLOCK : BLOCK + ROWS, :])):
                term = view[...] * taps_b[3 * i + j : 3 * i + j + 1, :]
                total = term if total is None else total + term
        fourth = jnp.maximum(dot(total.astype(BF), point_b[...]), 0.0)
        flat_s[:, f * 256 : (f + 1) * 256] = fourth.astype(BF)

    @pl.when(step == 0)
    def _():
        copies[0].wait()
        copies[1].wait()

    half = linear_s.shape[2]
    for side in range(2):
        features_out[:, side * half : (side + 1) * half] = dot(flat_s[...], linear_s[side]).astype(BF)
    centred = centre(features_out[...].astype(F32))
    scale_one = lax.rsqrt(jnp.mean(centred * centred, axis=1, keepdims=True) + EPSILON)
    standard = centred * scale_one
    normed = (standard * rows[9:10, :]).astype(BF)

    @pl.when(step == 0)
    def _():
        copies[2].wait()
        copies[3].wait()

    row_keep = keep_out[:, 0:1]
    value = dot(normed, up_s[0])
    value_out[...] = value
    gate = jax.nn.sigmoid(dot(normed, up_s[1]))
    gate_out[...] = gate
    reach = 4 * BLOCK
    gated_s[0:reach, :] = jnp.zeros((reach, gated_s.shape[1]), F32)
    gated_s[reach + ROWS :, :] = jnp.zeros((reach, gated_s.shape[1]), F32)
    gated_s[reach : reach + ROWS, :] = (row_keep * value * gate).astype(BF).astype(F32)
    total = None
    for k in range(9):
        term = gated_s[k * BLOCK : k * BLOCK + ROWS, :] * rows[k : k + 1, :]
        total = term if total is None else total + term
    centred = centre(total)
    scale_two = lax.rsqrt(jnp.mean(centred * centred, axis=1, keepdims=True) + EPSILON)
    standard_two = centred * scale_two
    standard_two_out[...] = standard_two
    active = standard_two * rows[10:11, :]
    hidden = (active * jax.nn.sigmoid(active)).astype(BF)
    scale_out[...] = jnp.broadcast_to(scale_two, (ROWS, 128))
    kept = jnp.where(row_keep > 0, hidden, jnp.zeros_like(hidden))
    kept = dot(row_order(), kept).astype(BF)
    count = kept_s.shape[0]
    for n in range(count):
        kept_s[n] = kept[:, n * 128 : (n + 1) * 128]
    plane = lax.axis_index("dp") % 4
    for offset, give in enumerate((give_0, give_1, give_2, give_3)):
        quarter = plane ^ offset
        give[0] = kept_s[me * (count // 2) + quarter]
        give[1] = kept_s[(1 - me) * (count // 2) + quarter]


def near_kernel(*refs):
    left = jnp.concatenate([ref[0] for ref in refs[0:4]], axis=0)
    right = jnp.concatenate([ref[...] for ref in refs[4:8]], axis=0)
    refs[8][...] = dot(left, right, DOWN)


def far_kernel(groups, *refs):
    first, gifts, theirs, planes, outs, total = refs[0], refs[1:5], refs[5], refs[6], refs[7:-1], refs[-1]
    left = jnp.concatenate([ref[1] for ref in gifts], axis=0)
    right = jnp.concatenate([theirs[...]] + [planes[n] for n in range(3)], axis=0)
    total[...] = first[...] + dot(left, right, DOWN)
    me = lax.axis_index("dp") // 4
    size = total.shape[0] // (groups // 4)
    for offset, out in enumerate(outs):
        at = pl.multiple_of((me ^ offset) * size, size)
        out[...] = total[pl.ds(at, size), :].astype(out.dtype)


def layers_kernel(*refs):
    pieces, left, right, total = refs[:-3], refs[-3], refs[-2], refs[-1]
    me = lax.axis_index("dp") // 4
    size = pieces[0].shape[0]
    for offset, piece in enumerate(pieces):
        at = pl.multiple_of((me ^ offset) * size, size)
        total[pl.ds(at, size), :] = piece[...].astype(F32)
    half = left.shape[1]
    left[...] = total[:, :half].astype(BF)
    right[...] = total[:, half:].astype(BF)


def finish_kernel(*refs):
    lefts, rights, out = refs[0:4], refs[4:8], refs[8]
    plane = lax.axis_index("dp") % 4
    size, half = lefts[0].shape
    for offset in range(4):
        at = pl.multiple_of((plane ^ offset) * size, size)
        out[pl.ds(at, size), :half] = lefts[offset][...].astype(F32)
        out[pl.ds(at, size), half:] = rights[offset][...].astype(F32)


def backward_kernel(
    features_in, value_in, gate_in, standard_two_in, scale_in, keep_in, rows, cotangent,
    down_mine, down_other, up_mine, up_other, plane_1, plane_2, plane_3,
    layer_out, grad_out, planes_out,
    down_s, up_s, depth_s, sems,
):
    step = pl.program_id(0)
    me = lax.axis_index("fsdp")
    copies = fetch(((down_mine, down_other, down_s), (up_mine, up_other, up_s)), sems, me)
    for n, plane in enumerate((plane_1, plane_2, plane_3)):
        copies.append(pltpu.make_async_copy(plane, planes_out.at[n], sems.at[4 + n]))

    @pl.when(step == 0)
    def _():
        for copy in copies:
            copy.start()

    order = row_order()
    row_keep = keep_in[:, 0:1]
    back_out = jnp.where(row_keep > 0, dot(order, cotangent[...], DOWN), 0.0)
    back_bf = back_out.astype(BF)
    standard_two = standard_two_in[...]
    active = standard_two * rows[10:11, :]
    swish = jax.nn.sigmoid(active)
    slope = (swish + active * swish * (1.0 - swish)) * rows[10:11, :]
    hidden = (active * swish).astype(BF)
    values = features_in[...].astype(F32)
    centred = centre(values)
    scale_one = lax.rsqrt(jnp.mean(centred * centred, axis=1, keepdims=True) + EPSILON)
    standard = centred * scale_one

    @pl.when(step == 0)
    def _():
        copies[0].wait()
        copies[1].wait()

    half = down_s.shape[1]
    mixed = dot(hidden[:, :half], down_s[0]) + dot(hidden[:, half:], down_s[1])
    layer = jnp.where(row_keep > 0, values + mixed, 0.0).astype(BF)
    layer_out[...] = dot(order, layer).astype(BF)
    back_hidden = jnp.concatenate([dot(back_bf, down_s[0], ACROSS), dot(back_bf, down_s[1], ACROSS)], axis=1)
    gain_up = back_hidden * slope
    scale_two = scale_in[:, 0:1]
    back_depth = scale_two * (
        gain_up
        - jnp.mean(gain_up, axis=1, keepdims=True)
        - standard_two * jnp.mean(gain_up * standard_two, axis=1, keepdims=True)
    )
    reach = 4 * BLOCK
    depth_s[0:reach, :] = jnp.zeros((reach, depth_s.shape[1]), F32)
    depth_s[reach + ROWS :, :] = jnp.zeros((reach, depth_s.shape[1]), F32)
    depth_s[reach : reach + ROWS, :] = back_depth
    total = None
    for k in range(9):
        term = depth_s[(8 - k) * BLOCK : (8 - k) * BLOCK + ROWS, :] * rows[k : k + 1, :]
        total = term if total is None else total + term
    back_gated = row_keep * total
    gate = gate_in[...]
    back_value = back_gated * gate
    back_gate = (back_value * value_in[...] * (1.0 - gate)).astype(BF)

    @pl.when(step == 0)
    def _():
        copies[2].wait()
        copies[3].wait()

    back_normed = dot(back_value.astype(BF), up_s[0], ACROSS) + dot(back_gate, up_s[1], ACROSS)
    gain_in = back_normed * rows[9:10, :]
    back_input = scale_one * (
        gain_in
        - jnp.mean(gain_in, axis=1, keepdims=True)
        - standard * jnp.mean(gain_in * standard, axis=1, keepdims=True)
    )
    grad_out[...] = dot(order, (back_out + back_input).astype(BF)).astype(BF)

    @pl.when(step == 0)
    def _():
        for copy in copies[4:]:
            copy.wait()


def whole(shape):
    return pl.BlockSpec(shape, lambda g: (0,) * len(shape))


def params(megabytes):
    return pltpu.CompilerParams(vmem_limit_bytes=megabytes * 1024 * 1024)


def cost(flops, moved):
    return pl.CostEstimate(flops=int(flops), bytes_accessed=int(moved), transcendentals=0)


def swap_cores(block):
    return lax.ppermute(block, "fsdp", [(0, 1), (1, 0)])


def swap_rank(block, offset, groups):
    return lax.ppermute(block, "dp", [(i, i ^ offset) for i in range(groups)])


def held_call(kernel, outs, scratch, name, *operands):
    return pl.pallas_call(
        kernel,
        out_shape=outs,
        scratch_shapes=scratch,
        compiler_params=params(32),
        cost_estimate=cost(1e6, 1e5),
        name=name,
    )(*operands)


def local(
    mel_panels,
    frames,
    target,
    conv_first,
    depth_a,
    point_a,
    depth_b,
    point_b,
    linear_weight,
    norm_gain,
    up_weight,
    depth_kernel,
    conv_gain,
    down_weight,
    cotangent,
):
    groups = lax.axis_size("dp")
    members = lax.axis_size("fsdp")
    slots, width_in = mel_panels.shape
    rows_here, width = cotangent.shape
    blocks = rows_here // ROWS
    half = width // members
    shape = jax.ShapeDtypeStruct
    lines = width_in // 128 + 8
    anywhere = pl.BlockSpec(memory_space=pltpu.HBM)
    held = pl.BlockSpec(memory_space=pltpu.VMEM)
    small = (conv_first, depth_a, point_a, depth_b, point_b, norm_gain, depth_kernel, conv_gain)
    outgoing, packed = pl.pallas_call(
        send_kernel,
        in_specs=[anywhere, held, held] + [anywhere] * len(small),
        out_shape=(shape((groups, lines, 128), BF), shape((160, 512), BF)),
        scratch_shapes=[pltpu.VMEM(array.shape, BF) for array in (mel_panels,) + small]
        + [
            pltpu.VMEM((32, 512), F32),
            pltpu.VMEM((groups * lines, 128), F32),
            pltpu.SemaphoreType.DMA((1 + len(small),)),
        ],
        compiler_params=params(60),
        cost_estimate=cost(2e8, 1e6),
        name="send",
    )(mel_panels, frames.reshape(1, slots), target.reshape(1, slots), *small)
    incoming = lax.all_to_all(outgoing, "dp", split_axis=0, concat_axis=0, tiled=True)
    packed_other = swap_cores(packed)
    linear_other = swap_cores(linear_weight)
    up_other = swap_cores(up_weight)
    down_other = swap_cores(down_weight)
    cotangents = [cotangent] + [swap_rank(cotangent, offset, groups) for offset in range(1, 4)]
    cotangent_other = swap_cores(cotangent)
    band, taps_a, taps_b, point_one, point_two, rows = pl.pallas_call(
        weights_kernel,
        out_shape=(
            shape((256, GROUP * 256), BF),
            shape((16, 256), F32),
            shape((16, 256), F32),
            shape((256, 256), BF),
            shape((256, 256), BF),
            shape((16, width), F32),
        ),
        compiler_params=params(16),
        cost_estimate=cost(2e8, 2e6),
        name="weights",
    )(packed, packed_other)

    def by_rows(columns):
        return pl.BlockSpec((ROWS, columns), lambda g: (g, 0))

    by_plane = pl.BlockSpec((members, ROWS, 128), lambda g: (0, g, 0))
    *given, features, value, gate, standard_two, scale, keep = pl.pallas_call(
        forward_kernel,
        grid=(blocks,),
        in_specs=[
            whole(incoming.shape), whole(band.shape), whole(taps_a.shape), whole(taps_b.shape), whole(point_one.shape),
            whole(point_two.shape), whole(rows.shape), anywhere, anywhere, anywhere, anywhere,
        ],
        out_specs=[
            by_plane, by_plane, by_plane, by_plane, by_rows(width),
            by_rows(width), by_rows(width), by_rows(width), by_rows(128), by_rows(128),
        ],
        out_shape=(
            *[shape((members, rows_here, 128), BF)] * 4,
            shape((rows_here, width), BF),
            shape((rows_here, width), F32),
            shape((rows_here, width), F32),
            shape((rows_here, width), F32),
            shape((rows_here, 128), F32),
            shape((rows_here, 128), F32),
        ),
        scratch_shapes=[
            pltpu.VMEM((2,) + linear_weight.shape, BF),
            pltpu.VMEM((2,) + up_weight.shape, BF),
            pltpu.VMEM((ROWS * width_in // SPAN // 128, groups * width_in // 128), F32),
            pltpu.VMEM((ROWS, LEAD + width_in // SPAN), F32),
            pltpu.VMEM((4, 5 * ROWS, 256), BF),
            pltpu.VMEM((GROUP + 1, 5 * ROWS, 256), F32),
            pltpu.VMEM((GROUP * ROWS, 256), BF),
            pltpu.VMEM((BINS // 2, ROWS, 256), F32),
            pltpu.VMEM((BINS // 2, ROWS + BLOCK, 256), F32),
            pltpu.VMEM((ROWS, BINS // 4 * 256), BF),
            pltpu.VMEM((ROWS + 8 * BLOCK, width), F32),
            pltpu.VMEM((width // 128, ROWS, 128), BF),
            pltpu.SemaphoreType.DMA((4,)),
        ],
        compiler_params=params(FRONT + groups // 2),
        cost_estimate=cost(2e10 * blocks, 1e7),
        name="forward",
    )(incoming, band, taps_a, taps_b, point_one, point_two, rows, linear_weight, linear_other, up_weight, up_other)
    near = [swap_rank(block, offset, groups) for offset, block in enumerate(given) if offset]
    beside = pl.pallas_call(
        backward_kernel,
        grid=(blocks,),
        in_specs=[
            by_rows(width), by_rows(width), by_rows(width), by_rows(width), by_rows(128), by_rows(128),
            whole(rows.shape), by_rows(width), *[anywhere] * 7,
        ],
        out_specs=[by_rows(width), by_rows(width), anywhere],
        out_shape=(
            shape((rows_here, width), BF), shape((rows_here, width), BF), shape((3, rows_here, width), BF),
        ),
        scratch_shapes=[
            pltpu.VMEM((2,) + down_weight.shape, BF),
            pltpu.VMEM((2,) + up_weight.shape, BF),
            pltpu.VMEM((ROWS + 8 * BLOCK, width), F32),
            pltpu.SemaphoreType.DMA((7,)),
        ],
        compiler_params=params(BACK),
        cost_estimate=cost(1e6, 1e5),
        name="backward",
    )(
        features, value, gate, standard_two, scale, keep, rows, cotangent,
        down_weight, down_other, up_weight, up_other, *cotangents[1:],
    )
    *near, layer_out, grad_input, planes = lax.optimization_barrier((*near, *beside))
    near = [given[0], *near]
    far = [swap_cores(block) for block in near]
    planes_other = swap_cores(planes)
    layers = groups // 4
    block = width // members // 4
    size = block // layers
    half_sum = held_call(near_kernel, shape((block, width), F32), [], "near", *near, *cotangents)
    own, *others = held_call(
        functools.partial(far_kernel, groups),
        [shape((size, width), F32)] + [shape((size, width), BF)] * (layers - 1),
        [pltpu.VMEM((block, width), F32)],
        "far",
        half_sum, *far, cotangent_other, planes_other,
    )
    for offset, other in enumerate(others):
        own = own + swap_rank(other, 4 * (offset + 1), groups).astype(F32)
    own = (own * (1.0 / math.sqrt(rows_here * groups * members))).astype(BF)
    pieces = [own] + [swap_rank(own, 4 * offset, groups) for offset in range(1, layers)]
    left, right = held_call(
        layers_kernel, [shape((block, width // 2), BF)] * 2, [pltpu.VMEM((block, width), F32)], "layers", *pieces
    )
    left_x, right_y = swap_rank(left, 1, groups), swap_rank(right, 2, groups)
    left_y, right_x = swap_rank(left, 2, groups), swap_rank(right, 1, groups)
    left_xy, right_xy = swap_rank(left_x, 2, groups), swap_rank(right_y, 1, groups)
    grad_down = held_call(
        finish_kernel, shape((half, width), F32), [], "finish",
        left, left_x, left_y, left_xy, right, right_x, right_y, right_xy,
    )
    return (layer_out, grad_input, grad_down)


def solution(mesh):
    placed = (
        P(("dp", "fsdp"), None),
        P(("dp", "fsdp")),
        P(("dp", "fsdp")),
        P(None, "fsdp"),
        P(None, "fsdp"),
        P(None, "fsdp"),
        P(None, "fsdp"),
        P(None, "fsdp"),
        P(None, "fsdp"),
        P("fsdp"),
        P(None, "fsdp"),
        P(None, "fsdp"),
        P("fsdp"),
        P("fsdp", None),
        P(("dp", "fsdp"), None),
    )
    return jax.shard_map(
        local,
        mesh=mesh,
        in_specs=placed,
        out_specs=(P(("dp", "fsdp"), None), P(("dp", "fsdp"), None), P("fsdp", None)),
        check_vma=False,
    )
```

```python
import functools
import math

import jax
import jax.numpy as jnp
from jax import lax
from jax.experimental import pallas as pl
from jax.experimental.pallas import tpu as pltpu
from jax.sharding import PartitionSpec as P

MELS = 80
PANEL = 128
EPSILON = 1e-05
SPAN = PANEL // 8
BLOCK = 8
ROWS = BLOCK * SPAN
FRONT = 60
BACK = 61
BINS = 40
GROUP = 10
WINDOW = 2 * GROUP + 1
LEAD = 256
BF = jnp.bfloat16
F32 = jnp.float32
ACROSS = (((1,), (1,)), ((), ()))
DOWN = (((0,), (0,)), ((), ()))


def dot(left, right, dims=(((1,), (0,)), ((), ()))):
    return lax.dot_general(left, right, dims, preferred_element_type=F32)


def iota(shape, dim):
    return lax.broadcasted_iota(jnp.int32, shape, dim)


def row_order():
    n = iota((ROWS, ROWS), 0)
    r = iota((ROWS, ROWS), 1)
    return jnp.where((n % SPAN) * BLOCK + n // SPAN == r, 1.0, 0.0).astype(BF)


def send_kernel(
    mel, frames, target, first, depth_a, point_a, depth_b, point_b, norm_gain, depth_kernel, conv_gain,
    outgoing, packed,
    mel_s, first_s, depth_a_s, point_a_s, depth_b_s, point_b_s, norm_s, kernel_s, conv_s, rows, lines, sems,
):
    pairs = (
        (mel, mel_s), (first, first_s), (depth_a, depth_a_s), (point_a, point_a_s), (depth_b, depth_b_s),
        (point_b, point_b_s), (norm_gain, norm_s), (depth_kernel, kernel_s), (conv_gain, conv_s),
    )
    copies = [pltpu.make_async_copy(source, held, sems.at[n]) for n, (source, held) in enumerate(pairs)]
    for copy in copies:
        copy.start()
    count = outgoing.shape[0]
    slots = mel_s.shape[0]
    lanes = mel_s.shape[1] // 128
    wanted = iota((count, slots), 0)
    chosen = jnp.where((target[...] == wanted) & (frames[...] > 0), 1.0, 0.0)
    sent = jnp.sum(chosen * frames[...].astype(F32), axis=1, keepdims=True)
    sent = jnp.broadcast_to(sent, (count, 128))
    for k in range(8):
        lines[pl.ds(lanes + k, count, stride=lanes + 8), :] = sent
    copies[0].wait()
    chosen = chosen.astype(BF)
    for k in range(lanes):
        lines[pl.ds(k, count, stride=lanes + 8), :] = dot(chosen, mel_s[:, k * 128 : (k + 1) * 128])
    for d in range(count):
        outgoing[d] = lines[d * (lanes + 8) : (d + 1) * (lanes + 8), :].astype(BF)
    for copy in copies[1:]:
        copy.wait()
    rows[...] = jnp.zeros_like(rows)
    rows[0:9, :] = kernel_s[...].astype(F32)
    rows[9:10, :] = norm_s[...].astype(F32).reshape(1, 512)
    rows[10:11, :] = conv_s[...].astype(F32).reshape(1, 512)
    rows[16:25, 0:128] = first_s[...].astype(F32)
    rows[16:25, 128:256] = depth_a_s[...].astype(F32)
    rows[16:25, 256:384] = depth_b_s[...].astype(F32)
    packed[0:32, :] = rows[...].astype(BF)
    packed[32:160, 0:128] = point_a_s[0:128, :]
    packed[32:160, 128:256] = point_a_s[128:256, :]
    packed[32:160, 256:384] = point_b_s[0:128, :]
    packed[32:160, 384:512] = point_b_s[128:256, :]


def unpack_weights(low, high, band, taps_a, taps_b, point_a, point_b, rows):
    low, high = low[...].astype(F32), high[...].astype(F32)
    rows[:, 0:512] = low[0:16]
    rows[:, 512:1024] = high[0:16]
    first = jnp.concatenate([low[16:32, 0:128], high[16:32, 0:128]], axis=1).astype(BF)
    taps_a[...] = jnp.concatenate([low[16:32, 128:256], high[16:32, 128:256]], axis=1)
    taps_b[...] = jnp.concatenate([low[16:32, 256:384], high[16:32, 256:384]], axis=1)
    for half, source in ((0, low), (1, high)):
        at = slice(half * 128, half * 128 + 128)
        point_a[0:128, at] = source[32:160, 0:128].astype(BF)
        point_a[128:256, at] = source[32:160, 128:256].astype(BF)
        point_b[0:128, at] = source[32:160, 256:384].astype(BF)
        point_b[128:256, at] = source[32:160, 384:512].astype(BF)
    tap = iota((256, 16), 1)
    base = jnp.where(tap < 9, (tap // 3) * MELS + tap % 3, -1000) - iota((256, 16), 0)
    for f in range(GROUP):
        place = jnp.where(base == -2 * f, 1.0, 0.0).astype(BF)
        band[:, f * 256 : (f + 1) * 256] = dot(place, first).astype(BF)


def fetch(pairs, sems, me):
    copies = []
    for number, (mine, other, held) in enumerate(pairs):
        copies.append(pltpu.make_async_copy(mine, held.at[me], sems.at[2 * number]))
        copies.append(pltpu.make_async_copy(other, held.at[1 - me], sems.at[2 * number + 1]))
    return copies


def centre(values):
    return values - jnp.mean(values, axis=1, keepdims=True)


def forward_kernel(
    incoming_in, packed_mine, packed_other, linear_mine, linear_other, up_mine, up_other,
    give_0, give_1, give_2, give_3, features_o, value_o, gate_o, standard_two_o, scale_o, keep_o, rows_o,
    incoming, features_out, value_out, gate_out, standard_two_out, scale_out, keep_out, rows, packed_s, band, taps_a, taps_b, point_a, point_b, linear_s, up_s, pick_s, ext_s, x_s, first_s, spread_s, even_s, odd_s, flat_s, gated_s, kept_s, sems, out_sems,
):
    step = pl.program_id(0)
    me = lax.axis_index("fsdp")
    copies = fetch(
        ((packed_mine, packed_other, packed_s), (linear_mine, linear_other, linear_s), (up_mine, up_other, up_s)), sems, me
    )

    copies.append(pltpu.make_async_copy(incoming_in, incoming, sems.at[len(copies)]))
    here = pl.ds(step * ROWS, ROWS)
    held = (features_out, value_out, gate_out, standard_two_out, scale_out, keep_out)
    saves = [
        pltpu.make_async_copy(source, out.at[here], out_sems.at[n])
        for n, (source, out) in enumerate(zip(held, (features_o, value_o, gate_o, standard_two_o, scale_o, keep_o)))
    ]
    save_rows = pltpu.make_async_copy(rows, rows_o, out_sems.at[len(saves)])

    @pl.when(step == 0)
    def _():
        for copy in copies[:2] + copies[6:]:
            copy.start()
        copies[0].wait()
        copies[1].wait()
        unpack_weights(packed_s.at[0], packed_s.at[1], band, taps_a, taps_b, point_a, point_b, rows)

    @pl.when(step == 0)
    def _():
        copies[6].wait()
        for copy in copies[2:6]:
            copy.start()
        save_rows.start()

    sources = incoming.shape[0]
    lanes = incoming.shape[1] - 8
    got = jnp.concatenate([incoming[source, lanes:, :].astype(F32)[0:1] for source in range(sources)], axis=0)
    present = jnp.where(got > 0, 1.0, 0.0)
    below = jnp.where(iota((sources, sources), 1) <= iota((sources, sources), 0), 1.0, 0.0).astype(BF)
    position = dot(below, present.astype(BF)) - 1.0
    slot = (iota((sources, 128), 1) + step * BLOCK).astype(F32)
    placing = jnp.where((position == slot) & (present > 0), 1.0, 0.0).astype(BF)[:, :BLOCK]
    length = dot(placing, got.astype(BF), DOWN)
    source = dot(placing, iota((sources, 128), 0).astype(F32).astype(BF), DOWN)
    per_step = lanes // SPAN
    lane = iota((BLOCK, 128), 1).astype(F32)
    base = source * lanes - lane
    for t in range(SPAN):
        live = length > 8.0 * t
        keep_out[t * BLOCK : (t + 1) * BLOCK, :] = jnp.where(live, 1.0, 0.0)
        here = jnp.where(live, base, -1e6)
        for k in range(per_step):
            at = k * ROWS + t * BLOCK
            for c in range(sources * lanes // 128):
                hit = here == 128.0 * c - (per_step * t + k)
                pick_s[at : at + BLOCK, c * 128 : (c + 1) * 128] = jnp.where(hit, 1.0, 0.0)
    lines = jnp.concatenate([incoming[source, :lanes, :] for source in range(sources)], axis=0)
    placed = dot(pick_s[...].astype(BF), lines)
    ext_s[0:BLOCK, 0:LEAD] = jnp.zeros((BLOCK, LEAD), F32)
    for k in range(per_step):
        part = placed[k * ROWS : (k + 1) * ROWS]
        ext_s[:, LEAD + k * 128 : LEAD + (k + 1) * 128] = part
        ahead = k + LEAD // 128 - per_step
        if ahead >= 0:
            ext_s[BLOCK:, ahead * 128 : (ahead + 1) * 128] = part[: ROWS - BLOCK]
    lane = iota((ROWS, 256), 1)
    edge = (lane == 0) | (lane == MELS) | (lane == 2 * MELS)
    for q in range(5):
        for b in range(4):
            start = LEAD + (2 * q - 3) * MELS + 2 * GROUP * b - 1
            tile = start // 128 * 128
            shift = start - tile
            span = 256 if shift + 2 * MELS + WINDOW <= 256 else 384
            part = ext_s[:, tile : tile + span]
            part = pltpu.roll(part, span - shift, 1)[:, :256]
            if b == 0:
                part = jnp.where(edge, 0.0, part)
            x_s[b, q * ROWS : (q + 1) * ROWS, :] = part.astype(BF)

    first_s[0] = jnp.zeros(first_s.shape[1:], F32)
    odd_s[:, 0:BLOCK, :] = jnp.zeros((odd_s.shape[0], BLOCK, 256), F32)

    def section(b, carry):
        source = x_s[b]
        for f in range(GROUP):
            first_s[1 + f] = jnp.maximum(dot(source, band[:, f * 256 : (f + 1) * 256]), 0.0)
        for g in range(GROUP // 2):
            for s in range(2):
                total = None
                for j in range(3):
                    for i in range(3):
                        at = (2 * s + i) * ROWS
                        term = first_s[2 * g + j, at : at + ROWS, :] * taps_a[3 * i + j : 3 * i + j + 1, :]
                        total = term if total is None else total + term
                spread_s[(2 * g + s) * ROWS : (2 * g + s + 1) * ROWS, :] = total.astype(BF)
        first_s[0] = first_s[GROUP]
        second = jnp.maximum(dot(spread_s[...], point_a[...]), 0.0)
        for g in range(GROUP // 2):
            even_s[b * (GROUP // 2) + g] = second[2 * g * ROWS : (2 * g + 1) * ROWS]
            odd_s[b * (GROUP // 2) + g, BLOCK:, :] = second[(2 * g + 1) * ROWS : (2 * g + 2) * ROWS]
        return carry

    lax.fori_loop(0, BINS // GROUP, section, 0)

    for f in range(BINS // 4):
        total = None
        for j in range(3):
            at = 2 * f + j - 1
            if at < 0:
                continue
            for i, view in enumerate((odd_s.at[at, 0:ROWS, :], even_s.at[at], odd_s.at[at, BLOCK : BLOCK + ROWS, :])):
                term = view[...] * taps_b[3 * i + j : 3 * i + j + 1, :]
                total = term if total is None else total + term
        fourth = jnp.maximum(dot(total.astype(BF), point_b[...]), 0.0)
        flat_s[:, f * 256 : (f + 1) * 256] = fourth.astype(BF)

    @pl.when(step == 0)
    def _():
        copies[2].wait()
        copies[3].wait()

    half = linear_s.shape[2]
    for side in range(2):
        features_out[:, side * half : (side + 1) * half] = dot(flat_s[...], linear_s[side]).astype(BF)
    saves[0].start()
    saves[5].start()
    centred = centre(features_out[...].astype(F32))
    scale_one = lax.rsqrt(jnp.mean(centred * centred, axis=1, keepdims=True) + EPSILON)
    standard = centred * scale_one
    normed = (standard * rows[9:10, :]).astype(BF)

    @pl.when(step == 0)
    def _():
        copies[4].wait()
        copies[5].wait()

    row_keep = keep_out[:, 0:1]
    value = dot(normed, up_s[0])
    value_out[...] = value
    gate = jax.nn.sigmoid(dot(normed, up_s[1]))
    gate_out[...] = gate
    saves[1].start()
    saves[2].start()
    reach = 4 * BLOCK
    gated_s[0:reach, :] = jnp.zeros((reach, gated_s.shape[1]), F32)
    gated_s[reach + ROWS :, :] = jnp.zeros((reach, gated_s.shape[1]), F32)
    gated_s[reach : reach + ROWS, :] = (row_keep * value * gate).astype(BF).astype(F32)
    total = None
    for k in range(9):
        term = gated_s[k * BLOCK : k * BLOCK + ROWS, :] * rows[k : k + 1, :]
        total = term if total is None else total + term
    centred = centre(total)
    scale_two = lax.rsqrt(jnp.mean(centred * centred, axis=1, keepdims=True) + EPSILON)
    standard_two = centred * scale_two
    standard_two_out[...] = standard_two
    scale_out[...] = jnp.broadcast_to(scale_two, (ROWS, 128))
    saves[3].start()
    saves[4].start()
    active = standard_two * rows[10:11, :]
    hidden = (active * jax.nn.sigmoid(active)).astype(BF)
    kept = jnp.where(row_keep > 0, hidden, jnp.zeros_like(hidden))
    kept = dot(row_order(), kept).astype(BF)
    count = kept_s.shape[0]
    for n in range(count):
        kept_s[n] = kept[:, n * 128 : (n + 1) * 128]
    plane = lax.axis_index("dp") % 4
    for offset, give in enumerate((give_0, give_1, give_2, give_3)):
        quarter = plane ^ offset
        give[0] = kept_s[me * (count // 2) + quarter]
        give[1] = kept_s[(1 - me) * (count // 2) + quarter]
    for save in saves:
        save.wait()

    @pl.when(step == 0)
    def _():
        save_rows.wait()


def pack_kernel(*refs):
    for n in range(4):
        refs[4][n] = refs[n][1]


def near_kernel(*refs):
    left = jnp.concatenate([ref[0] for ref in refs[0:4]], axis=0)
    right = jnp.concatenate([ref[...] for ref in refs[4:8]], axis=0)
    refs[8][...] = dot(left, right, DOWN)


def far_kernel(groups, *refs):
    first, gifts, theirs, outs, total = refs[0], refs[1], refs[2:6], refs[6:-1], refs[-1]
    left = jnp.concatenate([gifts[n] for n in range(4)], axis=0)
    right = jnp.concatenate([ref[...] for ref in theirs], axis=0)
    total[...] = first[...] + dot(left, right, DOWN)
    me = lax.axis_index("dp") // 4
    size = total.shape[0] // (groups // 4)
    for offset, out in enumerate(outs):
        at = pl.multiple_of((me ^ offset) * size, size)
        out[...] = total[pl.ds(at, size), :].astype(out.dtype)


def layers_kernel(*refs):
    pieces, left, right, total = refs[:-3], refs[-3], refs[-2], refs[-1]
    me = lax.axis_index("dp") // 4
    size = pieces[0].shape[0]
    for offset, piece in enumerate(pieces):
        at = pl.multiple_of((me ^ offset) * size, size)
        total[pl.ds(at, size), :] = piece[...].astype(F32)
    half = left.shape[1]
    left[...] = total[:, :half].astype(BF)
    right[...] = total[:, half:].astype(BF)


def finish_kernel(*refs):
    lefts, rights, out = refs[0:4], refs[4:8], refs[8]
    plane = lax.axis_index("dp") % 4
    size, half = lefts[0].shape
    for offset in range(4):
        at = pl.multiple_of((plane ^ offset) * size, size)
        out[pl.ds(at, size), :half] = lefts[offset][...].astype(F32)
        out[pl.ds(at, size), half:] = rights[offset][...].astype(F32)


def back_rows(order, cotangent, row_keep):
    return jnp.where(row_keep > 0, dot(order, cotangent[...], DOWN), 0.0)


def down_kernel(
    features_in, standard_two_in, scale_in, keep_in, rows, cotangent, down_mine, down_other,
    layer_out, depth_out,
    down_s, sems,
):
    step = pl.program_id(0)
    copies = fetch(((down_mine, down_other, down_s),), sems, lax.axis_index("fsdp"))

    @pl.when(step == 0)
    def _():
        for copy in copies:
            copy.start()

    order = row_order()
    row_keep = keep_in[:, 0:1]
    back_out = back_rows(order, cotangent, row_keep).astype(BF)
    standard_two = standard_two_in[...]
    active = standard_two * rows[10:11, :]
    swish = jax.nn.sigmoid(active)
    slope = (swish + active * swish * (1.0 - swish)) * rows[10:11, :]
    hidden = (active * swish).astype(BF)

    @pl.when(step == 0)
    def _():
        for copy in copies:
            copy.wait()

    half = down_s.shape[1]
    back_hidden = jnp.concatenate([dot(back_out, down_s[0], ACROSS), dot(back_out, down_s[1], ACROSS)], axis=1)
    gain_up = back_hidden * slope
    depth_out[...] = scale_in[:, 0:1] * (
        gain_up
        - jnp.mean(gain_up, axis=1, keepdims=True)
        - standard_two * jnp.mean(gain_up * standard_two, axis=1, keepdims=True)
    )
    mixed = dot(hidden[:, :half], down_s[0]) + dot(hidden[:, half:], down_s[1])
    layer = jnp.where(row_keep > 0, features_in[...].astype(F32) + mixed, 0.0).astype(BF)
    layer_out[...] = dot(order, layer).astype(BF)


def up_kernel(
    depth_in, features_in, value_in, gate_in, keep_in, rows, cotangent, up_mine, up_other,
    grad_out,
    up_s, depth_s, sems,
):
    step = pl.program_id(0)
    copies = fetch(((up_mine, up_other, up_s),), sems, lax.axis_index("fsdp"))

    @pl.when(step == 0)
    def _():
        for copy in copies:
            copy.start()

    order = row_order()
    row_keep = keep_in[:, 0:1]
    back_out = back_rows(order, cotangent, row_keep)
    centred = centre(features_in[...].astype(F32))
    scale_one = lax.rsqrt(jnp.mean(centred * centred, axis=1, keepdims=True) + EPSILON)
    standard = centred * scale_one
    reach = 4 * BLOCK
    depth_s[0:reach, :] = jnp.zeros((reach, depth_s.shape[1]), F32)
    depth_s[reach + ROWS :, :] = jnp.zeros((reach, depth_s.shape[1]), F32)
    depth_s[reach : reach + ROWS, :] = depth_in[...]
    total = None
    for k in range(9):
        term = depth_s[(8 - k) * BLOCK : (8 - k) * BLOCK + ROWS, :] * rows[k : k + 1, :]
        total = term if total is None else total + term
    gate = gate_in[...]
    back_value = row_keep * total * gate
    back_gate = (back_value * value_in[...] * (1.0 - gate)).astype(BF)

    @pl.when(step == 0)
    def _():
        for copy in copies:
            copy.wait()

    back_normed = dot(back_value.astype(BF), up_s[0], ACROSS) + dot(back_gate, up_s[1], ACROSS)
    gain_in = back_normed * rows[9:10, :]
    back_input = scale_one * (
        gain_in
        - jnp.mean(gain_in, axis=1, keepdims=True)
        - standard * jnp.mean(gain_in * standard, axis=1, keepdims=True)
    )
    grad_out[...] = dot(order, (back_out + back_input).astype(BF)).astype(BF)


def whole(shape):
    return pl.BlockSpec(shape, lambda g: (0,) * len(shape))


def params(megabytes):
    return pltpu.CompilerParams(vmem_limit_bytes=megabytes * 1024 * 1024)


def cost(flops, moved):
    return pl.CostEstimate(flops=int(flops), bytes_accessed=int(moved), transcendentals=0)


def swap_cores(block):
    return lax.ppermute(block, "fsdp", [(0, 1), (1, 0)])


def swap_rank(block, offset, groups):
    return lax.ppermute(block, "dp", [(i, i ^ offset) for i in range(groups)])


def held_call(kernel, outs, scratch, name, *operands):
    return pl.pallas_call(
        kernel,
        out_shape=outs,
        scratch_shapes=scratch,
        compiler_params=params(32),
        cost_estimate=cost(1e6, 1e5),
        name=name,
    )(*operands)


def local(
    mel_panels,
    frames,
    target,
    conv_first,
    depth_a,
    point_a,
    depth_b,
    point_b,
    linear_weight,
    norm_gain,
    up_weight,
    depth_kernel,
    conv_gain,
    down_weight,
    cotangent,
):
    groups = lax.axis_size("dp")
    members = lax.axis_size("fsdp")
    slots, width_in = mel_panels.shape
    rows_here, width = cotangent.shape
    blocks = rows_here // ROWS
    half = width // members
    shape = jax.ShapeDtypeStruct
    lines = width_in // 128 + 8
    anywhere = pl.BlockSpec(memory_space=pltpu.HBM)
    held = pl.BlockSpec(memory_space=pltpu.VMEM)
    small = (conv_first, depth_a, point_a, depth_b, point_b, norm_gain, depth_kernel, conv_gain)
    outgoing, packed = pl.pallas_call(
        send_kernel,
        in_specs=[anywhere, held, held] + [anywhere] * len(small),
        out_shape=(shape((groups, lines, 128), BF), shape((160, 512), BF)),
        scratch_shapes=[pltpu.VMEM(array.shape, BF) for array in (mel_panels,) + small]
        + [
            pltpu.VMEM((32, 512), F32),
            pltpu.VMEM((groups * lines, 128), F32),
            pltpu.SemaphoreType.DMA((1 + len(small),)),
        ],
        compiler_params=params(60),
        cost_estimate=cost(2e8, 1e6),
        name="send",
    )(mel_panels, frames.reshape(1, slots), target.reshape(1, slots), *small)
    incoming = lax.all_to_all(outgoing, "dp", split_axis=0, concat_axis=0, tiled=True)
    packed_other = swap_cores(packed)
    linear_other = swap_cores(linear_weight)
    up_other = swap_cores(up_weight)
    down_other = swap_cores(down_weight)
    cotangents = [cotangent] + [swap_rank(cotangent, offset, groups) for offset in range(1, 4)]
    cotangent_other = swap_cores(cotangent)
    def by_rows(columns):
        return pl.BlockSpec((ROWS, columns), lambda g: (g, 0))

    by_plane = pl.BlockSpec((members, ROWS, 128), lambda g: (0, g, 0))
    *given, features, value, gate, standard_two, scale, keep, rows = pl.pallas_call(
        forward_kernel,
        grid=(blocks,),
        in_specs=[
            *[anywhere] * 7,
        ],
        out_specs=[
            *[by_plane] * 4, *[anywhere] * 7,
        ],
        out_shape=(
            *[shape((members, rows_here, 128), BF)] * 4,
            shape((rows_here, width), BF),
            shape((rows_here, width), F32),
            shape((rows_here, width), F32),
            shape((rows_here, width), F32),
            shape((rows_here, 128), F32),
            shape((rows_here, 128), F32),
            shape((16, width), F32),
        ),
        scratch_shapes=[
            pltpu.VMEM(incoming.shape, BF),
            pltpu.VMEM((ROWS, width), BF),
            pltpu.VMEM((ROWS, width), F32),
            pltpu.VMEM((ROWS, width), F32),
            pltpu.VMEM((ROWS, width), F32),
            pltpu.VMEM((ROWS, 128), F32),
            pltpu.VMEM((ROWS, 128), F32),
            pltpu.VMEM((16, width), F32),
            pltpu.VMEM((2,) + packed.shape, BF),
            pltpu.VMEM((256, GROUP * 256), BF),
            pltpu.VMEM((16, 256), F32),
            pltpu.VMEM((16, 256), F32),
            pltpu.VMEM((256, 256), BF),
            pltpu.VMEM((256, 256), BF),
            pltpu.VMEM((2,) + linear_weight.shape, BF),
            pltpu.VMEM((2,) + up_weight.shape, BF),
            pltpu.VMEM((ROWS * width_in // SPAN // 128, groups * width_in // 128), F32),
            pltpu.VMEM((ROWS, LEAD + width_in // SPAN), F32),
            pltpu.VMEM((4, 5 * ROWS, 256), BF),
            pltpu.VMEM((GROUP + 1, 5 * ROWS, 256), F32),
            pltpu.VMEM((GROUP * ROWS, 256), BF),
            pltpu.VMEM((BINS // 2, ROWS, 256), F32),
            pltpu.VMEM((BINS // 2, ROWS + BLOCK, 256), F32),
            pltpu.VMEM((ROWS, BINS // 4 * 256), BF),
            pltpu.VMEM((ROWS + 8 * BLOCK, width), F32),
            pltpu.VMEM((width // 128, ROWS, 128), BF),
            pltpu.SemaphoreType.DMA((7,)),
            pltpu.SemaphoreType.DMA((7,)),
        ],
        compiler_params=params(FRONT),
        cost_estimate=cost(2e10 * blocks, 1e7),
        name="forward",
    )(incoming, packed, packed_other, linear_weight, linear_other, up_weight, up_other)
    near = [given[0]] + [swap_rank(given[offset], offset, groups) for offset in range(1, 4)]
    far = swap_cores(held_call(pack_kernel, shape((4, rows_here, 128), BF), [], "pack", *near))
    given[0], *cotangents[1:] = lax.optimization_barrier((given[0], *cotangents[1:]))
    cotangents_other = [cotangent_other] + [swap_cores(block) for block in cotangents[1:]]
    layers = groups // 4
    block = width // members // 4
    size = block // layers
    half_sum = held_call(near_kernel, shape((block, width), F32), [], "near", *near, *cotangents)
    own, *others = held_call(
        functools.partial(far_kernel, groups),
        [shape((size, width), F32)] + [shape((size, width), BF)] * (layers - 1),
        [pltpu.VMEM((block, width), F32)],
        "far",
        half_sum, far, *cotangents_other,
    )
    moved = [swap_rank(other, 4 * (offset + 1), groups) for offset, other in enumerate(others)]
    full, thin = by_rows(width), by_rows(128)
    layer_out, depth = pl.pallas_call(
        down_kernel,
        grid=(blocks,),
        in_specs=[full, full, thin, thin, whole(rows.shape), full, anywhere, anywhere],
        out_specs=[full, full],
        out_shape=(shape((rows_here, width), BF), shape((rows_here, width), F32)),
        scratch_shapes=[pltpu.VMEM((2,) + down_weight.shape, BF), pltpu.SemaphoreType.DMA((2,))],
        compiler_params=params(BACK),
        cost_estimate=cost(1e6, 1e5),
        name="down",
    )(features, standard_two, scale, keep, rows, cotangent, down_weight, down_other)
    *moved, layer_out, depth = lax.optimization_barrier((*moved, layer_out, depth))
    for part in moved:
        own = own + part.astype(F32)
    own = (own * (1.0 / math.sqrt(rows_here * groups * members))).astype(BF)
    pieces = [own] + [swap_rank(own, 4 * offset, groups) for offset in range(1, layers)]
    grad_input = pl.pallas_call(
        up_kernel,
        grid=(blocks,),
        in_specs=[full, full, full, full, thin, whole(rows.shape), full, anywhere, anywhere],
        out_specs=full,
        out_shape=shape((rows_here, width), BF),
        scratch_shapes=[
            pltpu.VMEM((2,) + up_weight.shape, BF),
            pltpu.VMEM((ROWS + 8 * BLOCK, width), F32),
            pltpu.SemaphoreType.DMA((2,)),
        ],
        compiler_params=params(BACK),
        cost_estimate=cost(1e6, 1e5),
        name="up",
    )(depth, features, value, gate, keep, rows, cotangent, up_weight, up_other)
    *pieces, grad_input = lax.optimization_barrier((*pieces, grad_input))
    left, right = held_call(
        layers_kernel, [shape((block, width // 2), BF)] * 2, [pltpu.VMEM((block, width), F32)], "layers", *pieces
    )
    left_x, right_y = swap_rank(left, 1, groups), swap_rank(right, 2, groups)
    left_y, right_x = swap_rank(left, 2, groups), swap_rank(right, 1, groups)
    left_xy, right_xy = swap_rank(left_x, 2, groups), swap_rank(right_y, 1, groups)
    grad_down = held_call(
        finish_kernel, shape((half, width), F32), [], "finish",
        left, left_x, left_y, left_xy, right, right_x, right_y, right_xy,
    )
    return (layer_out, grad_input, grad_down)


def solution(mesh):
    placed = (
        P(("dp", "fsdp"), None),
        P(("dp", "fsdp")),
        P(("dp", "fsdp")),
        P(None, "fsdp"),
        P(None, "fsdp"),
        P(None, "fsdp"),
        P(None, "fsdp"),
        P(None, "fsdp"),
        P(None, "fsdp"),
        P("fsdp"),
        P(None, "fsdp"),
        P(None, "fsdp"),
        P("fsdp"),
        P("fsdp", None),
        P(("dp", "fsdp"), None),
    )
    return jax.shard_map(
        local,
        mesh=mesh,
        in_specs=placed,
        out_specs=(P(("dp", "fsdp"), None), P(("dp", "fsdp"), None), P("fsdp", None)),
        check_vma=False,
    )
```

```python
import functools
import math

import jax
import jax.numpy as jnp
from jax import lax
from jax.experimental import pallas as pl
from jax.experimental.pallas import tpu as pltpu
from jax.sharding import PartitionSpec as P

MELS = 80
PANEL = 128
EPSILON = 1e-05
SPAN = PANEL // 8
BLOCK = 8
ROWS = BLOCK * SPAN
FRONT = 62
BACK = 62
BINS = 40
GROUP = 10
WINDOW = 2 * GROUP + 1
LEAD = 256
BF = jnp.bfloat16
F32 = jnp.float32
ACROSS = (((1,), (1,)), ((), ()))
DOWN = (((0,), (0,)), ((), ()))


def dot(left, right, dims=(((1,), (0,)), ((), ()))):
    return lax.dot_general(left, right, dims, preferred_element_type=F32)


def iota(shape, dim):
    return lax.broadcasted_iota(jnp.int32, shape, dim)


def row_order():
    n = iota((ROWS, ROWS), 0)
    r = iota((ROWS, ROWS), 1)
    return jnp.where((n % SPAN) * BLOCK + n // SPAN == r, 1.0, 0.0).astype(BF)


def send_kernel(
    mel, frames, target, first, depth_a, point_a, depth_b, point_b, norm_gain, depth_kernel, conv_gain,
    outgoing, packed,
    mel_s, first_s, depth_a_s, point_a_s, depth_b_s, point_b_s, norm_s, kernel_s, conv_s, rows, lines, sems,
):
    pairs = (
        (mel, mel_s), (first, first_s), (depth_a, depth_a_s), (point_a, point_a_s), (depth_b, depth_b_s),
        (point_b, point_b_s), (norm_gain, norm_s), (depth_kernel, kernel_s), (conv_gain, conv_s),
    )
    copies = [pltpu.make_async_copy(source, held, sems.at[n]) for n, (source, held) in enumerate(pairs)]
    for copy in copies:
        copy.start()
    count = outgoing.shape[0]
    slots = mel_s.shape[0]
    lanes = mel_s.shape[1] // 128
    wanted = iota((count, slots), 0)
    chosen = jnp.where((target[...] == wanted) & (frames[...] > 0), 1.0, 0.0)
    sent = jnp.sum(chosen * frames[...].astype(F32), axis=1, keepdims=True)
    sent = jnp.broadcast_to(sent, (count, 128))
    for k in range(8):
        lines[pl.ds(lanes + k, count, stride=lanes + 8), :] = sent
    copies[0].wait()
    chosen = chosen.astype(BF)
    for k in range(lanes):
        lines[pl.ds(k, count, stride=lanes + 8), :] = dot(chosen, mel_s[:, k * 128 : (k + 1) * 128])
    for d in range(count):
        outgoing[d] = lines[d * (lanes + 8) : (d + 1) * (lanes + 8), :].astype(BF)
    for copy in copies[1:]:
        copy.wait()
    rows[...] = jnp.zeros_like(rows)
    rows[0:9, :] = kernel_s[...].astype(F32)
    rows[9:10, :] = norm_s[...].astype(F32).reshape(1, 512)
    rows[10:11, :] = conv_s[...].astype(F32).reshape(1, 512)
    rows[16:25, 0:128] = first_s[...].astype(F32)
    rows[16:25, 128:256] = depth_a_s[...].astype(F32)
    rows[16:25, 256:384] = depth_b_s[...].astype(F32)
    packed[0:32, :] = rows[...].astype(BF)
    packed[32:160, 0:128] = point_a_s[0:128, :]
    packed[32:160, 128:256] = point_a_s[128:256, :]
    packed[32:160, 256:384] = point_b_s[0:128, :]
    packed[32:160, 384:512] = point_b_s[128:256, :]


def unpack_weights(low, high, band, taps_a, taps_b, point_a, point_b, rows):
    low, high = low[...].astype(F32), high[...].astype(F32)
    rows[:, 0:512] = low[0:16]
    rows[:, 512:1024] = high[0:16]
    first = jnp.concatenate([low[16:32, 0:128], high[16:32, 0:128]], axis=1).astype(BF)
    taps_a[...] = jnp.concatenate([low[16:32, 128:256], high[16:32, 128:256]], axis=1)
    taps_b[...] = jnp.concatenate([low[16:32, 256:384], high[16:32, 256:384]], axis=1)
    for half, source in ((0, low), (1, high)):
        at = slice(half * 128, half * 128 + 128)
        point_a[0:128, at] = source[32:160, 0:128].astype(BF)
        point_a[128:256, at] = source[32:160, 128:256].astype(BF)
        point_b[0:128, at] = source[32:160, 256:384].astype(BF)
        point_b[128:256, at] = source[32:160, 384:512].astype(BF)
    tap = iota((256, 16), 1)
    base = jnp.where(tap < 9, (tap // 3) * MELS + tap % 3, -1000) - iota((256, 16), 0)
    for f in range(GROUP):
        place = jnp.where(base == -2 * f, 1.0, 0.0).astype(BF)
        band[:, f * 256 : (f + 1) * 256] = dot(place, first).astype(BF)


def fetch(pairs, sems, me):
    copies = []
    for number, (mine, other, held) in enumerate(pairs):
        copies.append(pltpu.make_async_copy(mine, held.at[me], sems.at[2 * number]))
        copies.append(pltpu.make_async_copy(other, held.at[1 - me], sems.at[2 * number + 1]))
    return copies


def centre(values):
    return values - jnp.mean(values, axis=1, keepdims=True)


def forward_kernel(
    incoming_in, packed_mine, packed_other, linear_mine, linear_other, up_mine, up_other,
    give_0, give_1, give_2, give_3, features_o, value_o, gate_o, standard_two_o, scale_o, keep_o, rows_o,
    incoming, features_out, value_out, gate_out, standard_two_out, scale_out, keep_out, rows, packed_s, band, taps_a, taps_b, point_a, point_b, linear_s, up_s, pick_s, ext_s, x_s, first_s, spread_s, even_s, odd_s, flat_s, gated_s, kept_s, sems, out_sems,
):
    step = pl.program_id(0)
    me = lax.axis_index("fsdp")
    copies = fetch(
        ((packed_mine, packed_other, packed_s), (linear_mine, linear_other, linear_s), (up_mine, up_other, up_s)), sems, me
    )

    copies.append(pltpu.make_async_copy(incoming_in, incoming, sems.at[len(copies)]))
    here = pl.ds(step * ROWS, ROWS)
    held = (features_out, value_out, gate_out, standard_two_out, scale_out, keep_out)
    saves = [
        pltpu.make_async_copy(source, out.at[here], out_sems.at[n])
        for n, (source, out) in enumerate(zip(held, (features_o, value_o, gate_o, standard_two_o, scale_o, keep_o)))
    ]
    save_rows = pltpu.make_async_copy(rows, rows_o, out_sems.at[len(saves)])

    @pl.when(step == 0)
    def _():
        for copy in copies[:2] + copies[6:]:
            copy.start()
        copies[0].wait()
        copies[1].wait()
        unpack_weights(packed_s.at[0], packed_s.at[1], band, taps_a, taps_b, point_a, point_b, rows)

    @pl.when(step == 0)
    def _():
        copies[6].wait()
        for copy in copies[2:6]:
            copy.start()
        save_rows.start()

    sources = incoming.shape[0]
    lanes = incoming.shape[1] - 8
    got = jnp.concatenate([incoming[source, lanes:, :].astype(F32)[0:1] for source in range(sources)], axis=0)
    present = jnp.where(got > 0, 1.0, 0.0)
    below = jnp.where(iota((sources, sources), 1) <= iota((sources, sources), 0), 1.0, 0.0).astype(BF)
    position = dot(below, present.astype(BF)) - 1.0
    slot = (iota((sources, 128), 1) + step * BLOCK).astype(F32)
    placing = jnp.where((position == slot) & (present > 0), 1.0, 0.0).astype(BF)[:, :BLOCK]
    length = dot(placing, got.astype(BF), DOWN)
    source = dot(placing, iota((sources, 128), 0).astype(F32).astype(BF), DOWN)
    per_step = lanes // SPAN
    lane = iota((BLOCK, 128), 1).astype(F32)
    base = source * lanes - lane
    for t in range(SPAN):
        live = length > 8.0 * t
        keep_out[t * BLOCK : (t + 1) * BLOCK, :] = jnp.where(live, 1.0, 0.0)
        here = jnp.where(live, base, -1e6)
        for k in range(per_step):
            at = k * ROWS + t * BLOCK
            for c in range(sources * lanes // 128):
                hit = here == 128.0 * c - (per_step * t + k)
                pick_s[at : at + BLOCK, c * 128 : (c + 1) * 128] = jnp.where(hit, 1.0, 0.0)
    lines = jnp.concatenate([incoming[source, :lanes, :] for source in range(sources)], axis=0)
    placed = dot(pick_s[...].astype(BF), lines)
    ext_s[0:BLOCK, 0:LEAD] = jnp.zeros((BLOCK, LEAD), F32)
    for k in range(per_step):
        part = placed[k * ROWS : (k + 1) * ROWS]
        ext_s[:, LEAD + k * 128 : LEAD + (k + 1) * 128] = part
        ahead = k + LEAD // 128 - per_step
        if ahead >= 0:
            ext_s[BLOCK:, ahead * 128 : (ahead + 1) * 128] = part[: ROWS - BLOCK]
    lane = iota((ROWS, 256), 1)
    edge = (lane == 0) | (lane == MELS) | (lane == 2 * MELS)
    for q in range(4):
        for b in range(4):
            start = LEAD + (2 * q - 1) * MELS + 2 * GROUP * b - 1
            tile = start // 128 * 128
            shift = start - tile
            span = 256 if shift + 2 * MELS + WINDOW <= 256 else 384
            part = ext_s[:, tile : tile + span]
            part = pltpu.roll(part, span - shift, 1)[:, :256]
            if b == 0:
                part = jnp.where(edge, 0.0, part)
            x_s[b, q * ROWS : (q + 1) * ROWS, :] = part.astype(BF)

    views = (3 * ROWS, 0, ROWS, 2 * ROWS, 3 * ROWS + BLOCK)
    first_s[0] = jnp.zeros(first_s.shape[1:], F32)
    for f in range(GROUP):
        first_s[1 + f, 3 * ROWS : 3 * ROWS + BLOCK, :] = jnp.zeros((BLOCK, 256), F32)
    odd_s[:, 0:BLOCK, :] = jnp.zeros((odd_s.shape[0], BLOCK, 256), F32)

    def section(b, carry):
        source = x_s[b]
        for f in range(GROUP):
            sums = jnp.maximum(dot(source, band[:, f * 256 : (f + 1) * 256]), 0.0)
            first_s[1 + f, : 3 * ROWS, :] = sums[: 3 * ROWS]
            first_s[1 + f, 3 * ROWS + BLOCK :, :] = sums[3 * ROWS :]
        for g in range(GROUP // 2):
            for s in range(2):
                total = None
                for j in range(3):
                    for i in range(3):
                        at = views[2 * s + i]
                        term = first_s[2 * g + j, at : at + ROWS, :] * taps_a[3 * i + j : 3 * i + j + 1, :]
                        total = term if total is None else total + term
                spread_s[(2 * g + s) * ROWS : (2 * g + s + 1) * ROWS, :] = total.astype(BF)
        first_s[0] = first_s[GROUP]
        second = jnp.maximum(dot(spread_s[...], point_a[...]), 0.0)
        for g in range(GROUP // 2):
            even_s[b * (GROUP // 2) + g] = second[2 * g * ROWS : (2 * g + 1) * ROWS]
            odd_s[b * (GROUP // 2) + g, BLOCK:, :] = second[(2 * g + 1) * ROWS : (2 * g + 2) * ROWS]
        return carry

    lax.fori_loop(0, BINS // GROUP, section, 0)

    for f in range(BINS // 4):
        total = None
        for j in range(3):
            at = 2 * f + j - 1
            if at < 0:
                continue
            for i, view in enumerate((odd_s.at[at, 0:ROWS, :], even_s.at[at], odd_s.at[at, BLOCK : BLOCK + ROWS, :])):
                term = view[...] * taps_b[3 * i + j : 3 * i + j + 1, :]
                total = term if total is None else total + term
        fourth = jnp.maximum(dot(total.astype(BF), point_b[...]), 0.0)
        flat_s[:, f * 256 : (f + 1) * 256] = fourth.astype(BF)

    @pl.when(step == 0)
    def _():
        copies[2].wait()
        copies[3].wait()

    half = linear_s.shape[2]
    for side in range(2):
        features_out[:, side * half : (side + 1) * half] = dot(flat_s[...], linear_s[side]).astype(BF)
    saves[0].start()
    saves[5].start()
    centred = centre(features_out[...].astype(F32))
    scale_one = lax.rsqrt(jnp.mean(centred * centred, axis=1, keepdims=True) + EPSILON)
    standard = centred * scale_one
    normed = (standard * rows[9:10, :]).astype(BF)

    @pl.when(step == 0)
    def _():
        copies[4].wait()
        copies[5].wait()

    row_keep = keep_out[:, 0:1]
    value = dot(normed, up_s[0])
    value_out[...] = value
    gate = jax.nn.sigmoid(dot(normed, up_s[1]))
    gate_out[...] = gate
    saves[1].start()
    saves[2].start()
    reach = 4 * BLOCK
    gated_s[0:reach, :] = jnp.zeros((reach, gated_s.shape[1]), F32)
    gated_s[reach + ROWS :, :] = jnp.zeros((reach, gated_s.shape[1]), F32)
    gated_s[reach : reach + ROWS, :] = (row_keep * value * gate).astype(BF).astype(F32)
    total = None
    for k in range(9):
        term = gated_s[k * BLOCK : k * BLOCK + ROWS, :] * rows[k : k + 1, :]
        total = term if total is None else total + term
    centred = centre(total)
    scale_two = lax.rsqrt(jnp.mean(centred * centred, axis=1, keepdims=True) + EPSILON)
    standard_two = centred * scale_two
    standard_two_out[...] = standard_two
    scale_out[...] = jnp.broadcast_to(scale_two, (ROWS, 128))
    saves[3].start()
    saves[4].start()
    active = standard_two * rows[10:11, :]
    hidden = (active * jax.nn.sigmoid(active)).astype(BF)
    kept = jnp.where(row_keep > 0, hidden, jnp.zeros_like(hidden))
    kept = dot(row_order(), kept).astype(BF)
    count = kept_s.shape[0]
    for n in range(count):
        kept_s[n] = kept[:, n * 128 : (n + 1) * 128]
    plane = lax.axis_index("dp") % 4
    for offset, give in enumerate((give_0, give_1, give_2, give_3)):
        quarter = plane ^ offset
        give[0] = kept_s[me * (count // 2) + quarter]
        give[1] = kept_s[(1 - me) * (count // 2) + quarter]
    for save in saves:
        save.wait()

    @pl.when(step == 0)
    def _():
        save_rows.wait()


def pack_kernel(*refs):
    for n in range(4):
        refs[4][n] = refs[n][1]


def near_kernel(*refs):
    left = jnp.concatenate([ref[0] for ref in refs[0:4]], axis=0)
    right = jnp.concatenate([ref[...] for ref in refs[4:8]], axis=0)
    refs[8][...] = dot(left, right, DOWN)


def far_kernel(groups, *refs):
    first, gifts, theirs, outs, total = refs[0], refs[1], refs[2:6], refs[6:-1], refs[-1]
    left = jnp.concatenate([gifts[n] for n in range(4)], axis=0)
    right = jnp.concatenate([ref[...] for ref in theirs], axis=0)
    total[...] = first[...] + dot(left, right, DOWN)
    me = lax.axis_index("dp") // 4
    size = total.shape[0] // (groups // 4)
    for offset, out in enumerate(outs):
        at = pl.multiple_of((me ^ offset) * size, size)
        out[...] = total[pl.ds(at, size), :].astype(out.dtype)


def layers_kernel(*refs):
    pieces, left, right, total = refs[:-3], refs[-3], refs[-2], refs[-1]
    me = lax.axis_index("dp") // 4
    size = pieces[0].shape[0]
    for offset, piece in enumerate(pieces):
        at = pl.multiple_of((me ^ offset) * size, size)
        total[pl.ds(at, size), :] = piece[...].astype(F32)
    half = left.shape[1]
    left[...] = total[:, :half].astype(BF)
    right[...] = total[:, half:].astype(BF)


def finish_kernel(*refs):
    pieces, out, held, sems = refs[0:8], refs[8], refs[9], refs[10]
    plane = lax.axis_index("dp") % 4
    size, half = pieces[0].shape
    copies = []
    for n, piece in enumerate(pieces):
        side = slice(n // 4 * half, (n // 4 + 1) * half)
        held[n] = piece[...].astype(F32)
        at = pl.multiple_of((plane ^ (n % 4)) * size, size)
        copies.append(pltpu.make_async_copy(held.at[n], out.at[pl.ds(at, size), side], sems.at[n]))
        copies[-1].start()
    for copy in copies:
        copy.wait()


def back_rows(order, cotangent, row_keep):
    return jnp.where(row_keep > 0, dot(order, cotangent[...], DOWN), 0.0)


def bring(body, inputs, outputs, *refs):
    sources, mine, other = refs[:inputs], refs[inputs], refs[inputs + 1]
    outs = refs[inputs + 2 : inputs + 2 + outputs]
    refs = refs[inputs + 2 + outputs :]
    held, weight, sems, extra = refs[:inputs], refs[inputs], refs[inputs + 1], refs[inputs + 2 :]
    step = pl.program_id(0)
    copies = []
    for n, (source, buffer) in enumerate(zip(sources, held)):
        if source.shape[0] != 16:
            source = source.at[pl.ds(step * ROWS, ROWS)]
        copies.append(pltpu.make_async_copy(source, buffer, sems.at[n]))
    me = lax.axis_index("fsdp")
    weights = [
        pltpu.make_async_copy(mine, weight.at[me], sems.at[inputs]),
        pltpu.make_async_copy(other, weight.at[1 - me], sems.at[inputs + 1]),
    ]
    for copy in copies:
        copy.start()

    @pl.when(step == 0)
    def _():
        for copy in weights:
            copy.start()

    for copy in copies:
        copy.wait()

    def wait_weight():
        @pl.when(step == 0)
        def _():
            for copy in weights:
                copy.wait()

    body(wait_weight, weight, *held, *outs, *extra)


def layer_kernel(wait_weight, down_s, features_in, standard_two_in, keep_in, rows, layer_out):
    active = standard_two_in[...] * rows[10:11, :]
    hidden = (active * jax.nn.sigmoid(active)).astype(BF)
    order = row_order()
    wait_weight()
    half = down_s.shape[1]
    mixed = dot(hidden[:, :half], down_s[0]) + dot(hidden[:, half:], down_s[1])
    layer = jnp.where(keep_in[:, 0:1] > 0, features_in[...].astype(F32) + mixed, 0.0).astype(BF)
    layer_out[...] = dot(order, layer).astype(BF)


def depth_kernel_back(
    wait_weight, down_s, standard_two_in, value_in, gate_in, scale_in, keep_in, rows, cotangent, value_out, gate_out, depth_s,
):
    row_keep = keep_in[:, 0:1]
    back_out = back_rows(row_order(), cotangent, row_keep).astype(BF)
    standard_two = standard_two_in[...]
    active = standard_two * rows[10:11, :]
    swish = jax.nn.sigmoid(active)
    slope = (swish + active * swish * (1.0 - swish)) * rows[10:11, :]
    wait_weight()
    back_hidden = jnp.concatenate([dot(back_out, down_s[0], ACROSS), dot(back_out, down_s[1], ACROSS)], axis=1)
    gain_up = back_hidden * slope
    reach = 4 * BLOCK
    depth_s[0:reach, :] = jnp.zeros((reach, depth_s.shape[1]), F32)
    depth_s[reach + ROWS :, :] = jnp.zeros((reach, depth_s.shape[1]), F32)
    depth_s[reach : reach + ROWS, :] = scale_in[:, 0:1] * (
        gain_up
        - jnp.mean(gain_up, axis=1, keepdims=True)
        - standard_two * jnp.mean(gain_up * standard_two, axis=1, keepdims=True)
    )
    total = None
    for k in range(9):
        term = depth_s[(8 - k) * BLOCK : (8 - k) * BLOCK + ROWS, :] * rows[k : k + 1, :]
        total = term if total is None else total + term
    gate = gate_in[...]
    back_value = row_keep * total * gate
    value_out[...] = back_value.astype(BF)
    gate_out[...] = (back_value * value_in[...] * (1.0 - gate)).astype(BF)


def up_kernel(wait_weight, up_s, back_value, back_gate, features_in, keep_in, rows, cotangent, grad_out):
    order = row_order()
    row_keep = keep_in[:, 0:1]
    back_out = back_rows(order, cotangent, row_keep)
    centred = centre(features_in[...].astype(F32))
    scale_one = lax.rsqrt(jnp.mean(centred * centred, axis=1, keepdims=True) + EPSILON)
    standard = centred * scale_one
    wait_weight()
    back_normed = dot(back_value[...], up_s[0], ACROSS) + dot(back_gate[...], up_s[1], ACROSS)
    gain_in = back_normed * rows[9:10, :]
    back_input = scale_one * (
        gain_in
        - jnp.mean(gain_in, axis=1, keepdims=True)
        - standard * jnp.mean(gain_in * standard, axis=1, keepdims=True)
    )
    grad_out[...] = dot(order, (back_out + back_input).astype(BF)).astype(BF)


def whole(shape):
    return pl.BlockSpec(shape, lambda g: (0,) * len(shape))


def params(megabytes):
    return pltpu.CompilerParams(vmem_limit_bytes=megabytes * 1024 * 1024)


def cost(flops, moved):
    return pl.CostEstimate(flops=int(flops), bytes_accessed=int(moved), transcendentals=0)


def swap_cores(block):
    return lax.ppermute(block, "fsdp", [(0, 1), (1, 0)])


def swap_rank(block, offset, groups):
    return lax.ppermute(block, "dp", [(i, i ^ offset) for i in range(groups)])


def held_call(kernel, outs, scratch, name, *operands, **specs):
    return pl.pallas_call(
        kernel,
        **specs,
        out_shape=outs,
        scratch_shapes=scratch,
        compiler_params=params(32),
        cost_estimate=cost(1e6, 1e5),
        name=name,
    )(*operands)


def local(
    mel_panels,
    frames,
    target,
    conv_first,
    depth_a,
    point_a,
    depth_b,
    point_b,
    linear_weight,
    norm_gain,
    up_weight,
    depth_kernel,
    conv_gain,
    down_weight,
    cotangent,
):
    groups = lax.axis_size("dp")
    members = lax.axis_size("fsdp")
    slots, width_in = mel_panels.shape
    rows_here, width = cotangent.shape
    blocks = rows_here // ROWS
    half = width // members
    shape = jax.ShapeDtypeStruct
    lines = width_in // 128 + 8
    anywhere = pl.BlockSpec(memory_space=pltpu.HBM)
    held = pl.BlockSpec(memory_space=pltpu.VMEM)
    small = (conv_first, depth_a, point_a, depth_b, point_b, norm_gain, depth_kernel, conv_gain)
    outgoing, packed = pl.pallas_call(
        send_kernel,
        in_specs=[anywhere, held, held] + [anywhere] * len(small),
        out_shape=(shape((groups, lines, 128), BF), shape((160, 512), BF)),
        scratch_shapes=[pltpu.VMEM(array.shape, BF) for array in (mel_panels,) + small]
        + [
            pltpu.VMEM((32, 512), F32),
            pltpu.VMEM((groups * lines, 128), F32),
            pltpu.SemaphoreType.DMA((1 + len(small),)),
        ],
        compiler_params=params(60),
        cost_estimate=cost(2e8, 1e6),
        name="send",
    )(mel_panels, frames.reshape(1, slots), target.reshape(1, slots), *small)
    incoming = lax.all_to_all(outgoing, "dp", split_axis=0, concat_axis=0, tiled=True)
    packed_other = swap_cores(packed)
    linear_other = swap_cores(linear_weight)
    up_other = swap_cores(up_weight)
    down_other = swap_cores(down_weight)
    cotangents = [cotangent] + [swap_rank(cotangent, offset, groups) for offset in range(1, 4)]
    cotangent_other = swap_cores(cotangent)
    def by_rows(columns):
        return pl.BlockSpec((ROWS, columns), lambda g: (g, 0))

    by_plane = pl.BlockSpec((members, ROWS, 128), lambda g: (0, g, 0))
    *given, features, value, gate, standard_two, scale, keep, rows = pl.pallas_call(
        forward_kernel,
        grid=(blocks,),
        in_specs=[
            *[anywhere] * 7,
        ],
        out_specs=[
            *[by_plane] * 4, *[anywhere] * 7,
        ],
        out_shape=(
            *[shape((members, rows_here, 128), BF)] * 4,
            shape((rows_here, width), BF),
            shape((rows_here, width), F32),
            shape((rows_here, width), F32),
            shape((rows_here, width), F32),
            shape((rows_here, 128), F32),
            shape((rows_here, 128), F32),
            shape((16, width), F32),
        ),
        scratch_shapes=[
            pltpu.VMEM(incoming.shape, BF),
            pltpu.VMEM((ROWS, width), BF),
            pltpu.VMEM((ROWS, width), F32),
            pltpu.VMEM((ROWS, width), F32),
            pltpu.VMEM((ROWS, width), F32),
            pltpu.VMEM((ROWS, 128), F32),
            pltpu.VMEM((ROWS, 128), F32),
            pltpu.VMEM((16, width), F32),
            pltpu.VMEM((2,) + packed.shape, BF),
            pltpu.VMEM((256, GROUP * 256), BF),
            pltpu.VMEM((16, 256), F32),
            pltpu.VMEM((16, 256), F32),
            pltpu.VMEM((256, 256), BF),
            pltpu.VMEM((256, 256), BF),
            pltpu.VMEM((2,) + linear_weight.shape, BF),
            pltpu.VMEM((2,) + up_weight.shape, BF),
            pltpu.VMEM((ROWS * width_in // SPAN // 128, groups * width_in // 128), F32),
            pltpu.VMEM((ROWS, LEAD + width_in // SPAN), F32),
            pltpu.VMEM((4, 4 * ROWS, 256), BF),
            pltpu.VMEM((GROUP + 1, 4 * ROWS + BLOCK, 256), F32),
            pltpu.VMEM((GROUP * ROWS, 256), BF),
            pltpu.VMEM((BINS // 2, ROWS, 256), F32),
            pltpu.VMEM((BINS // 2, ROWS + BLOCK, 256), F32),
            pltpu.VMEM((ROWS, BINS // 4 * 256), BF),
            pltpu.VMEM((ROWS + 8 * BLOCK, width), F32),
            pltpu.VMEM((width // 128, ROWS, 128), BF),
            pltpu.SemaphoreType.DMA((7,)),
            pltpu.SemaphoreType.DMA((7,)),
        ],
        compiler_params=params(FRONT),
        cost_estimate=cost(2e10 * blocks, 1e7),
        name="forward",
    )(incoming, packed, packed_other, linear_weight, linear_other, up_weight, up_other)
    first, *cotangents[1:3] = lax.optimization_barrier((given[0], *cotangents[1:3]))
    cotangents_other = [cotangent_other] + [swap_cores(block) for block in cotangents[1:3]]
    near = [swap_rank(given[offset], offset, groups) for offset in range(1, 4)]
    full = by_rows(width)

    def back_call(body, name, sources, mine, other, outs, extra=()):
        return pl.pallas_call(
            functools.partial(bring, body, len(sources), outs),
            grid=(blocks,),
            in_specs=[anywhere] * (len(sources) + 2),
            out_specs=[full] * outs,
            out_shape=[shape((rows_here, width), BF)] * outs,
            scratch_shapes=[
                *[pltpu.VMEM((min(array.shape[0], ROWS), array.shape[1]), array.dtype) for array in sources],
                pltpu.VMEM((2,) + mine.shape, BF),
                pltpu.SemaphoreType.DMA((len(sources) + 2,)),
                *extra,
            ],
            compiler_params=params(BACK),
            cost_estimate=cost(1e6, 1e5),
            name=name,
        )(*sources, mine, other)

    (layer_out,) = back_call(layer_kernel, "layer", (features, standard_two, keep, rows), down_weight, down_other, 1)
    *near, layer_out, cotangents[3] = lax.optimization_barrier((*near, layer_out, cotangents[3]))
    near = [first, *near]
    far = swap_cores(held_call(pack_kernel, shape((4, rows_here, 128), BF), [], "pack", *near))
    cotangents_other.append(swap_cores(cotangents[3]))
    layers = groups // 4
    block = width // members // 4
    size = block // layers
    half_sum = held_call(near_kernel, shape((block, width), F32), [], "near", *near, *cotangents)
    own, *others = held_call(
        functools.partial(far_kernel, groups),
        [shape((size, width), F32)] + [shape((size, width), BF)] * (layers - 1),
        [pltpu.VMEM((block, width), F32)],
        "far",
        half_sum, far, *cotangents_other,
    )
    moved = [swap_rank(other, 4 * (offset + 1), groups) for offset, other in enumerate(others)]
    value_back, gate_back = back_call(
        depth_kernel_back, "depth", (standard_two, value, gate, scale, keep, rows, cotangent), down_weight, down_other, 2,
        [pltpu.VMEM((ROWS + 8 * BLOCK, width), F32)],
    )
    *moved, value_back, gate_back = lax.optimization_barrier((*moved, value_back, gate_back))
    for part in moved:
        own = own + part.astype(F32)
    own = (own * (1.0 / math.sqrt(rows_here * groups * members))).astype(BF)
    pieces = [own] + [swap_rank(own, 4 * offset, groups) for offset in range(1, layers)]
    (grad_input,) = back_call(
        up_kernel, "up", (value_back, gate_back, features, keep, rows, cotangent), up_weight, up_other, 1
    )
    *pieces, grad_input = lax.optimization_barrier((*pieces, grad_input))
    left, right = held_call(
        layers_kernel, [shape((block, width // 2), BF)] * 2, [pltpu.VMEM((block, width), F32)], "layers", *pieces
    )
    left_x, right_y = swap_rank(left, 1, groups), swap_rank(right, 2, groups)
    left_y, right_x = swap_rank(left, 2, groups), swap_rank(right, 1, groups)
    left_xy, right_xy = swap_rank(left_x, 2, groups), swap_rank(right_y, 1, groups)
    grad_down = held_call(
        finish_kernel, shape((half, width), F32),
        [pltpu.VMEM((8, block, width // 2), F32), pltpu.SemaphoreType.DMA((8,))], "finish",
        left, left_x, left_y, left_xy, right, right_x, right_y, right_xy, out_specs=anywhere,
    )
    return (layer_out, grad_input, grad_down)


def solution(mesh):
    placed = (
        P(("dp", "fsdp"), None),
        P(("dp", "fsdp")),
        P(("dp", "fsdp")),
        P(None, "fsdp"),
        P(None, "fsdp"),
        P(None, "fsdp"),
        P(None, "fsdp"),
        P(None, "fsdp"),
        P(None, "fsdp"),
        P("fsdp"),
        P(None, "fsdp"),
        P(None, "fsdp"),
        P("fsdp"),
        P("fsdp", None),
        P(("dp", "fsdp"), None),
    )
    return jax.shard_map(
        local,
        mesh=mesh,
        in_specs=placed,
        out_specs=(P(("dp", "fsdp"), None), P(("dp", "fsdp"), None), P("fsdp", None)),
        check_vma=False,
    )
```

```python
import functools
import math

import jax
import jax.numpy as jnp
from jax import lax
from jax.experimental import pallas as pl
from jax.experimental.pallas import tpu as pltpu
from jax.sharding import PartitionSpec as P

MELS = 80
PANEL = 128
EPSILON = 1e-05
SPAN = PANEL // 8
BLOCK = 8
ROWS = BLOCK * SPAN
FRONT = 62
BACK = 62
BINS = 40
GROUP = 10
WINDOW = 2 * GROUP + 1
LEAD = 256
BF = jnp.bfloat16
F32 = jnp.float32
ACROSS = (((1,), (1,)), ((), ()))
DOWN = (((0,), (0,)), ((), ()))


def dot(left, right, dims=(((1,), (0,)), ((), ()))):
    return lax.dot_general(left, right, dims, preferred_element_type=F32)


def iota(shape, dim):
    return lax.broadcasted_iota(jnp.int32, shape, dim)


def row_order():
    n = iota((ROWS, ROWS), 0)
    r = iota((ROWS, ROWS), 1)
    return jnp.where((n % SPAN) * BLOCK + n // SPAN == r, 1.0, 0.0).astype(BF)


def send_kernel(
    mel, frames, target, first, depth_a, point_a, depth_b, point_b, norm_gain, depth_kernel, conv_gain,
    outgoing, packed,
    mel_s, first_s, depth_a_s, point_a_s, depth_b_s, point_b_s, norm_s, kernel_s, conv_s, rows, lines, sems,
):
    pairs = (
        (mel, mel_s), (first, first_s), (depth_a, depth_a_s), (point_a, point_a_s), (depth_b, depth_b_s),
        (point_b, point_b_s), (norm_gain, norm_s), (depth_kernel, kernel_s), (conv_gain, conv_s),
    )
    copies = [pltpu.make_async_copy(source, held, sems.at[n]) for n, (source, held) in enumerate(pairs)]
    for copy in copies:
        copy.start()
    count = outgoing.shape[0]
    slots = mel_s.shape[0]
    lanes = mel_s.shape[1] // 128
    wanted = iota((count, slots), 0)
    chosen = jnp.where((target[...] == wanted) & (frames[...] > 0), 1.0, 0.0)
    sent = jnp.sum(chosen * frames[...].astype(F32), axis=1, keepdims=True)
    sent = jnp.broadcast_to(sent, (count, 128))
    for k in range(8):
        lines[pl.ds(lanes + k, count, stride=lanes + 8), :] = sent
    copies[0].wait()
    chosen = chosen.astype(BF)
    for k in range(lanes):
        lines[pl.ds(k, count, stride=lanes + 8), :] = dot(chosen, mel_s[:, k * 128 : (k + 1) * 128])
    for d in range(count):
        outgoing[d] = lines[d * (lanes + 8) : (d + 1) * (lanes + 8), :].astype(BF)
    for copy in copies[1:]:
        copy.wait()
    rows[...] = jnp.zeros_like(rows)
    rows[0:9, :] = kernel_s[...].astype(F32)
    rows[9:10, :] = norm_s[...].astype(F32).reshape(1, 512)
    rows[10:11, :] = conv_s[...].astype(F32).reshape(1, 512)
    rows[16:25, 0:128] = first_s[...].astype(F32)
    rows[16:25, 128:256] = depth_a_s[...].astype(F32)
    rows[16:25, 256:384] = depth_b_s[...].astype(F32)
    packed[0:32, :] = rows[...].astype(BF)
    packed[32:160, 0:128] = point_a_s[0:128, :]
    packed[32:160, 128:256] = point_a_s[128:256, :]
    packed[32:160, 256:384] = point_b_s[0:128, :]
    packed[32:160, 384:512] = point_b_s[128:256, :]


def weights_kernel(mine, other, band, taps_a, taps_b, point_a, point_b, rows):
    me = lax.axis_index("fsdp")
    near, far = mine[...].astype(F32), other[...].astype(F32)
    low, high = jnp.where(me == 0, near, far), jnp.where(me == 0, far, near)
    rows[:, 0:512] = low[0:16]
    rows[:, 512:1024] = high[0:16]
    first = jnp.concatenate([low[16:32, 0:128], high[16:32, 0:128]], axis=1).astype(BF)
    taps_a[...] = jnp.concatenate([low[16:32, 128:256], high[16:32, 128:256]], axis=1)
    taps_b[...] = jnp.concatenate([low[16:32, 256:384], high[16:32, 256:384]], axis=1)
    for half, source in ((0, low), (1, high)):
        at = slice(half * 128, half * 128 + 128)
        point_a[0:128, at] = source[32:160, 0:128].astype(BF)
        point_a[128:256, at] = source[32:160, 128:256].astype(BF)
        point_b[0:128, at] = source[32:160, 256:384].astype(BF)
        point_b[128:256, at] = source[32:160, 384:512].astype(BF)
    tap = iota((256, 16), 1)
    base = jnp.where(tap < 9, (tap // 3) * MELS + tap % 3, -1000) - iota((256, 16), 0)
    for f in range(GROUP):
        place = jnp.where(base == -2 * f, 1.0, 0.0).astype(BF)
        band[:, f * 256 : (f + 1) * 256] = dot(place, first).astype(BF)


def fetch(pairs, sems, me):
    copies = []
    for number, (mine, other, held) in enumerate(pairs):
        copies.append(pltpu.make_async_copy(mine, held.at[me], sems.at[2 * number]))
        copies.append(pltpu.make_async_copy(other, held.at[1 - me], sems.at[2 * number + 1]))
    return copies


def centre(values):
    return values - jnp.mean(values, axis=1, keepdims=True)


def forward_kernel(
    incoming_in, band_in, taps_a_in, taps_b_in, point_a_in, point_b_in, rows_in, linear_mine, linear_other, up_mine, up_other,
    give_0, give_1, give_2, give_3, features_o, value_o, gate_o, standard_two_o, scale_o, keep_o,
    incoming, features_out, value_out, gate_out, standard_two_out, scale_out, keep_out, band, taps_a, taps_b, point_a, point_b, rows, linear_s, up_s, pick_s, ext_s, x_s, first_s, spread_s, even_s, odd_s, flat_s, gated_s, kept_s, sems, out_sems,
):
    step = pl.program_id(0)
    me = lax.axis_index("fsdp")
    copies = fetch(((linear_mine, linear_other, linear_s), (up_mine, up_other, up_s)), sems, me)
    pairs = (
        (incoming_in, incoming), (band_in, band), (taps_a_in, taps_a), (taps_b_in, taps_b), (point_a_in, point_a),
        (point_b_in, point_b), (rows_in, rows),
    )
    small = [pltpu.make_async_copy(source, target, sems.at[4 + n]) for n, (source, target) in enumerate(pairs)]
    here = pl.ds(step * ROWS, ROWS)
    held = (features_out, value_out, gate_out, standard_two_out, scale_out, keep_out)
    saves = [
        pltpu.make_async_copy(source, out.at[here], out_sems.at[n])
        for n, (source, out) in enumerate(zip(held, (features_o, value_o, gate_o, standard_two_o, scale_o, keep_o)))
    ]

    @pl.when(step == 0)
    def _():
        for copy in small:
            copy.start()
        small[0].wait()
        for copy in copies:
            copy.start()

    sources = incoming.shape[0]
    lanes = incoming.shape[1] - 8
    got = jnp.concatenate([incoming[source, lanes:, :].astype(F32)[0:1] for source in range(sources)], axis=0)
    present = jnp.where(got > 0, 1.0, 0.0)
    below = jnp.where(iota((sources, sources), 1) <= iota((sources, sources), 0), 1.0, 0.0).astype(BF)
    position = dot(below, present.astype(BF)) - 1.0
    slot = (iota((sources, 128), 1) + step * BLOCK).astype(F32)
    placing = jnp.where((position == slot) & (present > 0), 1.0, 0.0).astype(BF)[:, :BLOCK]
    length = dot(placing, got.astype(BF), DOWN)
    source = dot(placing, iota((sources, 128), 0).astype(F32).astype(BF), DOWN)
    per_step = lanes // SPAN
    lane = iota((BLOCK, 128), 1).astype(F32)
    base = source * lanes - lane
    for t in range(SPAN):
        live = length > 8.0 * t
        keep_out[t * BLOCK : (t + 1) * BLOCK, :] = jnp.where(live, 1.0, 0.0)
        here = jnp.where(live, base, -1e6)
        for k in range(per_step):
            at = k * ROWS + t * BLOCK
            for c in range(sources * lanes // 128):
                hit = here == 128.0 * c - (per_step * t + k)
                pick_s[at : at + BLOCK, c * 128 : (c + 1) * 128] = jnp.where(hit, 1.0, 0.0)
    lines = jnp.concatenate([incoming[source, :lanes, :] for source in range(sources)], axis=0)
    placed = dot(pick_s[...].astype(BF), lines)
    ext_s[0:BLOCK, 0:LEAD] = jnp.zeros((BLOCK, LEAD), F32)
    for k in range(per_step):
        part = placed[k * ROWS : (k + 1) * ROWS]
        ext_s[:, LEAD + k * 128 : LEAD + (k + 1) * 128] = part
        ahead = k + LEAD // 128 - per_step
        if ahead >= 0:
            ext_s[BLOCK:, ahead * 128 : (ahead + 1) * 128] = part[: ROWS - BLOCK]
    lane = iota((ROWS, 256), 1)
    edge = (lane == 0) | (lane == MELS) | (lane == 2 * MELS)
    for q in range(4):
        for b in range(4):
            start = LEAD + (2 * q - 1) * MELS + 2 * GROUP * b - 1
            tile = start // 128 * 128
            shift = start - tile
            span = 256 if shift + 2 * MELS + WINDOW <= 256 else 384
            part = ext_s[:, tile : tile + span]
            part = pltpu.roll(part, span - shift, 1)[:, :256]
            if b == 0:
                part = jnp.where(edge, 0.0, part)
            x_s[b, q * ROWS : (q + 1) * ROWS, :] = part.astype(BF)

    @pl.when(step == 0)
    def _():
        for copy in small[1:]:
            copy.wait()

    views = (3 * ROWS, 0, ROWS, 2 * ROWS, 3 * ROWS + BLOCK)
    first_s[0] = jnp.zeros(first_s.shape[1:], F32)
    for f in range(GROUP):
        first_s[1 + f, 3 * ROWS : 3 * ROWS + BLOCK, :] = jnp.zeros((BLOCK, 256), F32)
    odd_s[:, 0:BLOCK, :] = jnp.zeros((odd_s.shape[0], BLOCK, 256), F32)

    def section(b, carry):
        source = x_s[b]
        for f in range(GROUP):
            sums = jnp.maximum(dot(source, band[:, f * 256 : (f + 1) * 256]), 0.0)
            first_s[1 + f, : 3 * ROWS, :] = sums[: 3 * ROWS]
            first_s[1 + f, 3 * ROWS + BLOCK :, :] = sums[3 * ROWS :]
        for g in range(GROUP // 2):
            for s in range(2):
                total = None
                for j in range(3):
                    for i in range(3):
                        at = views[2 * s + i]
                        term = first_s[2 * g + j, at : at + ROWS, :] * taps_a[3 * i + j : 3 * i + j + 1, :]
                        total = term if total is None else total + term
                spread_s[(2 * g + s) * ROWS : (2 * g + s + 1) * ROWS, :] = total.astype(BF)
        first_s[0] = first_s[GROUP]
        second = jnp.maximum(dot(spread_s[...], point_a[...]), 0.0)
        for g in range(GROUP // 2):
            even_s[b * (GROUP // 2) + g] = second[2 * g * ROWS : (2 * g + 1) * ROWS]
            odd_s[b * (GROUP // 2) + g, BLOCK:, :] = second[(2 * g + 1) * ROWS : (2 * g + 2) * ROWS]
        return carry

    lax.fori_loop(0, BINS // GROUP, section, 0, unroll=2)

    for f in range(BINS // 4):
        total = None
        for j in range(3):
            at = 2 * f + j - 1
            if at < 0:
                continue
            for i, view in enumerate((odd_s.at[at, 0:ROWS, :], even_s.at[at], odd_s.at[at, BLOCK : BLOCK + ROWS, :])):
                term = view[...] * taps_b[3 * i + j : 3 * i + j + 1, :]
                total = term if total is None else total + term
        fourth = jnp.maximum(dot(total.astype(BF), point_b[...]), 0.0)
        flat_s[:, f * 256 : (f + 1) * 256] = fourth.astype(BF)

    @pl.when(step == 0)
    def _():
        copies[0].wait()
        copies[1].wait()

    half = linear_s.shape[2]
    for side in range(2):
        features_out[:, side * half : (side + 1) * half] = dot(flat_s[...], linear_s[side]).astype(BF)
    saves[0].start()
    saves[5].start()
    centred = centre(features_out[...].astype(F32))
    scale_one = lax.rsqrt(jnp.mean(centred * centred, axis=1, keepdims=True) + EPSILON)
    standard = centred * scale_one
    normed = (standard * rows[9:10, :]).astype(BF)

    @pl.when(step == 0)
    def _():
        copies[2].wait()
        copies[3].wait()

    row_keep = keep_out[:, 0:1]
    value = dot(normed, up_s[0])
    value_out[...] = value
    gate = jax.nn.sigmoid(dot(normed, up_s[1]))
    gate_out[...] = gate
    saves[1].start()
    saves[2].start()
    reach = 4 * BLOCK
    gated_s[0:reach, :] = jnp.zeros((reach, gated_s.shape[1]), F32)
    gated_s[reach + ROWS :, :] = jnp.zeros((reach, gated_s.shape[1]), F32)
    gated_s[reach : reach + ROWS, :] = (row_keep * value * gate).astype(BF).astype(F32)
    total = None
    for k in range(9):
        term = gated_s[k * BLOCK : k * BLOCK + ROWS, :] * rows[k : k + 1, :]
        total = term if total is None else total + term
    centred = centre(total)
    scale_two = lax.rsqrt(jnp.mean(centred * centred, axis=1, keepdims=True) + EPSILON)
    standard_two = centred * scale_two
    standard_two_out[...] = standard_two
    scale_out[...] = jnp.broadcast_to(scale_two, (ROWS, 128))
    saves[3].start()
    saves[4].start()
    active = standard_two * rows[10:11, :]
    hidden = (active * jax.nn.sigmoid(active)).astype(BF)
    kept = jnp.where(row_keep > 0, hidden, jnp.zeros_like(hidden))
    kept = dot(row_order(), kept).astype(BF)
    count = kept_s.shape[0]
    for n in range(count):
        kept_s[n] = kept[:, n * 128 : (n + 1) * 128]
    plane = lax.axis_index("dp") % 4
    for offset, give in enumerate((give_0, give_1, give_2, give_3)):
        quarter = plane ^ offset
        give[0] = kept_s[me * (count // 2) + quarter]
        give[1] = kept_s[(1 - me) * (count // 2) + quarter]
    for save in saves:
        save.wait()


def pack_kernel(*refs):
    for n in range(4):
        refs[4][n] = refs[n][1]


def near_kernel(*refs):
    left = jnp.concatenate([ref[0] for ref in refs[0:4]], axis=0)
    right = jnp.concatenate([ref[...] for ref in refs[4:8]], axis=0)
    refs[8][...] = dot(left, right, DOWN)


def far_kernel(groups, *refs):
    first, gifts, theirs, outs, total = refs[0], refs[1], refs[2:6], refs[6:-1], refs[-1]
    left = jnp.concatenate([gifts[n] for n in range(4)], axis=0)
    right = jnp.concatenate([ref[...] for ref in theirs], axis=0)
    total[...] = first[...] + dot(left, right, DOWN)
    me = lax.axis_index("dp") // 4
    size = total.shape[0] // (groups // 4)
    for offset, out in enumerate(outs):
        at = pl.multiple_of((me ^ offset) * size, size)
        out[...] = total[pl.ds(at, size), :].astype(out.dtype)


def layers_kernel(*refs):
    pieces, left, right, total = refs[:-3], refs[-3], refs[-2], refs[-1]
    me = lax.axis_index("dp") // 4
    size = pieces[0].shape[0]
    for offset, piece in enumerate(pieces):
        at = pl.multiple_of((me ^ offset) * size, size)
        total[pl.ds(at, size), :] = piece[...].astype(F32)
    half = left.shape[1]
    left[...] = total[:, :half].astype(BF)
    right[...] = total[:, half:].astype(BF)


def finish_kernel(*refs):
    pieces, out, held, sems = refs[0:8], refs[8], refs[9], refs[10]
    plane = lax.axis_index("dp") % 4
    size, half = pieces[0].shape
    copies = []
    for n, piece in enumerate(pieces):
        side = slice(n // 4 * half, (n // 4 + 1) * half)
        held[n] = piece[...].astype(F32)
        at = pl.multiple_of((plane ^ (n % 4)) * size, size)
        copies.append(pltpu.make_async_copy(held.at[n], out.at[pl.ds(at, size), side], sems.at[n]))
        copies[-1].start()
    for copy in copies:
        copy.wait()


def back_rows(order, cotangent, row_keep):
    return jnp.where(row_keep > 0, dot(order, cotangent[...], DOWN), 0.0)


def bring(body, inputs, outputs, *refs):
    sources, mine, other = refs[:inputs], refs[inputs], refs[inputs + 1]
    outs = refs[inputs + 2 : inputs + 2 + outputs]
    refs = refs[inputs + 2 + outputs :]
    held, weight, sems, extra = refs[:inputs], refs[inputs], refs[inputs + 1], refs[inputs + 2 :]
    step = pl.program_id(0)
    copies = []
    for n, (source, buffer) in enumerate(zip(sources, held)):
        if source.shape[0] != 16:
            source = source.at[pl.ds(step * ROWS, ROWS)]
        copies.append(pltpu.make_async_copy(source, buffer, sems.at[n]))
    me = lax.axis_index("fsdp")
    weights = [
        pltpu.make_async_copy(mine, weight.at[me], sems.at[inputs]),
        pltpu.make_async_copy(other, weight.at[1 - me], sems.at[inputs + 1]),
    ]
    for copy in copies:
        copy.start()

    @pl.when(step == 0)
    def _():
        for copy in weights:
            copy.start()

    for copy in copies:
        copy.wait()

    def wait_weight():
        @pl.when(step == 0)
        def _():
            for copy in weights:
                copy.wait()

    body(wait_weight, weight, *held, *outs, *extra)


def layer_kernel(wait_weight, down_s, features_in, standard_two_in, keep_in, rows, layer_out):
    active = standard_two_in[...] * rows[10:11, :]
    hidden = (active * jax.nn.sigmoid(active)).astype(BF)
    order = row_order()
    wait_weight()
    half = down_s.shape[1]
    mixed = dot(hidden[:, :half], down_s[0]) + dot(hidden[:, half:], down_s[1])
    layer = jnp.where(keep_in[:, 0:1] > 0, features_in[...].astype(F32) + mixed, 0.0).astype(BF)
    layer_out[...] = dot(order, layer).astype(BF)


def depth_kernel_back(
    wait_weight, down_s, standard_two_in, value_in, gate_in, scale_in, keep_in, rows, cotangent, value_out, gate_out, depth_s,
):
    row_keep = keep_in[:, 0:1]
    back_out = back_rows(row_order(), cotangent, row_keep).astype(BF)
    standard_two = standard_two_in[...]
    active = standard_two * rows[10:11, :]
    swish = jax.nn.sigmoid(active)
    slope = (swish + active * swish * (1.0 - swish)) * rows[10:11, :]
    wait_weight()
    back_hidden = jnp.concatenate([dot(back_out, down_s[0], ACROSS), dot(back_out, down_s[1], ACROSS)], axis=1)
    gain_up = back_hidden * slope
    reach = 4 * BLOCK
    depth_s[0:reach, :] = jnp.zeros((reach, depth_s.shape[1]), F32)
    depth_s[reach + ROWS :, :] = jnp.zeros((reach, depth_s.shape[1]), F32)
    depth_s[reach : reach + ROWS, :] = scale_in[:, 0:1] * (
        gain_up
        - jnp.mean(gain_up, axis=1, keepdims=True)
        - standard_two * jnp.mean(gain_up * standard_two, axis=1, keepdims=True)
    )
    total = None
    for k in range(9):
        term = depth_s[(8 - k) * BLOCK : (8 - k) * BLOCK + ROWS, :] * rows[k : k + 1, :]
        total = term if total is None else total + term
    gate = gate_in[...]
    back_value = row_keep * total * gate
    value_out[...] = back_value.astype(BF)
    gate_out[...] = (back_value * value_in[...] * (1.0 - gate)).astype(BF)


def up_kernel(wait_weight, up_s, back_value, back_gate, features_in, keep_in, rows, cotangent, grad_out):
    order = row_order()
    row_keep = keep_in[:, 0:1]
    back_out = back_rows(order, cotangent, row_keep)
    centred = centre(features_in[...].astype(F32))
    scale_one = lax.rsqrt(jnp.mean(centred * centred, axis=1, keepdims=True) + EPSILON)
    standard = centred * scale_one
    wait_weight()
    back_normed = dot(back_value[...], up_s[0], ACROSS) + dot(back_gate[...], up_s[1], ACROSS)
    gain_in = back_normed * rows[9:10, :]
    back_input = scale_one * (
        gain_in
        - jnp.mean(gain_in, axis=1, keepdims=True)
        - standard * jnp.mean(gain_in * standard, axis=1, keepdims=True)
    )
    grad_out[...] = dot(order, (back_out + back_input).astype(BF)).astype(BF)


def whole(shape):
    return pl.BlockSpec(shape, lambda g: (0,) * len(shape))


def params(megabytes):
    return pltpu.CompilerParams(vmem_limit_bytes=megabytes * 1024 * 1024)


def cost(flops, moved):
    return pl.CostEstimate(flops=int(flops), bytes_accessed=int(moved), transcendentals=0)


def swap_cores(block):
    return lax.ppermute(block, "fsdp", [(0, 1), (1, 0)])


def swap_rank(block, offset, groups):
    return lax.ppermute(block, "dp", [(i, i ^ offset) for i in range(groups)])


def held_call(kernel, outs, scratch, name, *operands, **specs):
    return pl.pallas_call(
        kernel,
        **specs,
        out_shape=outs,
        scratch_shapes=scratch,
        compiler_params=params(32),
        cost_estimate=cost(1e6, 1e5),
        name=name,
    )(*operands)


def local(
    mel_panels,
    frames,
    target,
    conv_first,
    depth_a,
    point_a,
    depth_b,
    point_b,
    linear_weight,
    norm_gain,
    up_weight,
    depth_kernel,
    conv_gain,
    down_weight,
    cotangent,
):
    groups = lax.axis_size("dp")
    members = lax.axis_size("fsdp")
    slots, width_in = mel_panels.shape
    rows_here, width = cotangent.shape
    blocks = rows_here // ROWS
    half = width // members
    shape = jax.ShapeDtypeStruct
    lines = width_in // 128 + 8
    anywhere = pl.BlockSpec(memory_space=pltpu.HBM)
    held = pl.BlockSpec(memory_space=pltpu.VMEM)
    small = (conv_first, depth_a, point_a, depth_b, point_b, norm_gain, depth_kernel, conv_gain)
    outgoing, packed = pl.pallas_call(
        send_kernel,
        in_specs=[anywhere, held, held] + [anywhere] * len(small),
        out_shape=(shape((groups, lines, 128), BF), shape((160, 512), BF)),
        scratch_shapes=[pltpu.VMEM(array.shape, BF) for array in (mel_panels,) + small]
        + [
            pltpu.VMEM((32, 512), F32),
            pltpu.VMEM((groups * lines, 128), F32),
            pltpu.SemaphoreType.DMA((1 + len(small),)),
        ],
        compiler_params=params(60),
        cost_estimate=cost(2e8, 1e6),
        name="send",
    )(mel_panels, frames.reshape(1, slots), target.reshape(1, slots), *small)
    incoming = lax.all_to_all(outgoing, "dp", split_axis=0, concat_axis=0, tiled=True)
    packed_other = swap_cores(packed)
    unpacked = held_call(
        weights_kernel,
        [
            shape((256, GROUP * 256), BF), shape((16, 256), F32), shape((16, 256), F32), shape((256, 256), BF),
            shape((256, 256), BF), shape((16, width), F32),
        ],
        [], "weights", packed, packed_other,
    )
    rows = unpacked[-1]
    linear_other = swap_cores(linear_weight)
    up_other = swap_cores(up_weight)
    down_other = swap_cores(down_weight)
    cotangents = [cotangent] + [swap_rank(cotangent, offset, groups) for offset in range(1, 4)]
    cotangent_other = swap_cores(cotangent)
    def by_rows(columns):
        return pl.BlockSpec((ROWS, columns), lambda g: (g, 0))

    by_plane = pl.BlockSpec((members, ROWS, 128), lambda g: (0, g, 0))
    *given, features, value, gate, standard_two, scale, keep = pl.pallas_call(
        forward_kernel,
        grid=(blocks,),
        in_specs=[
            *[anywhere] * 11,
        ],
        out_specs=[
            *[by_plane] * 4, *[anywhere] * 6,
        ],
        out_shape=(
            *[shape((members, rows_here, 128), BF)] * 4,
            shape((rows_here, width), BF),
            shape((rows_here, width), F32),
            shape((rows_here, width), F32),
            shape((rows_here, width), F32),
            shape((rows_here, 128), F32),
            shape((rows_here, 128), F32),
        ),
        scratch_shapes=[
            pltpu.VMEM(incoming.shape, BF),
            pltpu.VMEM((ROWS, width), BF),
            pltpu.VMEM((ROWS, width), F32),
            pltpu.VMEM((ROWS, width), F32),
            pltpu.VMEM((ROWS, width), F32),
            pltpu.VMEM((ROWS, 128), F32),
            pltpu.VMEM((ROWS, 128), F32),
            pltpu.VMEM((256, GROUP * 256), BF),
            pltpu.VMEM((16, 256), F32),
            pltpu.VMEM((16, 256), F32),
            pltpu.VMEM((256, 256), BF),
            pltpu.VMEM((256, 256), BF),
            pltpu.VMEM((16, width), F32),
            pltpu.VMEM((2,) + linear_weight.shape, BF),
            pltpu.VMEM((2,) + up_weight.shape, BF),
            pltpu.VMEM((ROWS * width_in // SPAN // 128, groups * width_in // 128), F32),
            pltpu.VMEM((ROWS, LEAD + width_in // SPAN), F32),
            pltpu.VMEM((4, 4 * ROWS, 256), BF),
            pltpu.VMEM((GROUP + 1, 4 * ROWS + BLOCK, 256), F32),
            pltpu.VMEM((GROUP * ROWS, 256), BF),
            pltpu.VMEM((BINS // 2, ROWS, 256), F32),
            pltpu.VMEM((BINS // 2, ROWS + BLOCK, 256), F32),
            pltpu.VMEM((ROWS, BINS // 4 * 256), BF),
            pltpu.VMEM((ROWS + 8 * BLOCK, width), F32),
            pltpu.VMEM((width // 128, ROWS, 128), BF),
            pltpu.SemaphoreType.DMA((11,)),
            pltpu.SemaphoreType.DMA((6,)),
        ],
        compiler_params=params(FRONT),
        cost_estimate=cost(2e10 * blocks, 1e7),
        name="forward",
    )(incoming, *unpacked, linear_weight, linear_other, up_weight, up_other)
    first, *cotangents[1:3] = lax.optimization_barrier((given[0], *cotangents[1:3]))
    cotangents_other = [cotangent_other] + [swap_cores(block) for block in cotangents[1:3]]
    near = [swap_rank(given[offset], offset, groups) for offset in range(1, 4)]
    full = by_rows(width)

    def back_call(body, name, sources, mine, other, outs, extra=()):
        return pl.pallas_call(
            functools.partial(bring, body, len(sources), outs),
            grid=(blocks,),
            in_specs=[anywhere] * (len(sources) + 2),
            out_specs=[full] * outs,
            out_shape=[shape((rows_here, width), BF)] * outs,
            scratch_shapes=[
                *[pltpu.VMEM((min(array.shape[0], ROWS), array.shape[1]), array.dtype) for array in sources],
                pltpu.VMEM((2,) + mine.shape, BF),
                pltpu.SemaphoreType.DMA((len(sources) + 2,)),
                *extra,
            ],
            compiler_params=params(BACK),
            cost_estimate=cost(1e6, 1e5),
            name=name,
        )(*sources, mine, other)

    (layer_out,) = back_call(layer_kernel, "layer", (features, standard_two, keep, rows), down_weight, down_other, 1)
    *near, layer_out, cotangents[3] = lax.optimization_barrier((*near, layer_out, cotangents[3]))
    near = [first, *near]
    far = swap_cores(held_call(pack_kernel, shape((4, rows_here, 128), BF), [], "pack", *near))
    cotangents_other.append(swap_cores(cotangents[3]))
    layers = groups // 4
    block = width // members // 4
    size = block // layers
    half_sum = held_call(near_kernel, shape((block, width), F32), [], "near", *near, *cotangents)
    own, *others = held_call(
        functools.partial(far_kernel, groups),
        [shape((size, width), F32)] + [shape((size, width), BF)] * (layers - 1),
        [pltpu.VMEM((block, width), F32)],
        "far",
        half_sum, far, *cotangents_other,
    )
    moved = [swap_rank(other, 4 * (offset + 1), groups) for offset, other in enumerate(others)]
    value_back, gate_back = back_call(
        depth_kernel_back, "depth", (standard_two, value, gate, scale, keep, rows, cotangent), down_weight, down_other, 2,
        [pltpu.VMEM((ROWS + 8 * BLOCK, width), F32)],
    )
    *moved, value_back, gate_back = lax.optimization_barrier((*moved, value_back, gate_back))
    for part in moved:
        own = own + part.astype(F32)
    own = (own * (1.0 / math.sqrt(rows_here * groups * members))).astype(BF)
    pieces = [own] + [swap_rank(own, 4 * offset, groups) for offset in range(1, layers)]
    (grad_input,) = back_call(
        up_kernel, "up", (value_back, gate_back, features, keep, rows, cotangent), up_weight, up_other, 1
    )
    *pieces, grad_input = lax.optimization_barrier((*pieces, grad_input))
    left, right = held_call(
        layers_kernel, [shape((block, width // 2), BF)] * 2, [pltpu.VMEM((block, width), F32)], "layers", *pieces
    )
    left_x, right_y = swap_rank(left, 1, groups), swap_rank(right, 2, groups)
    left_y, right_x = swap_rank(left, 2, groups), swap_rank(right, 1, groups)
    left_xy, right_xy = swap_rank(left_x, 2, groups), swap_rank(right_y, 1, groups)
    grad_down = held_call(
        finish_kernel, shape((half, width), F32),
        [pltpu.VMEM((8, block, width // 2), F32), pltpu.SemaphoreType.DMA((8,))], "finish",
        left, left_x, left_y, left_xy, right, right_x, right_y, right_xy, out_specs=anywhere,
    )
    return (layer_out, grad_input, grad_down)


def solution(mesh):
    placed = (
        P(("dp", "fsdp"), None),
        P(("dp", "fsdp")),
        P(("dp", "fsdp")),
        P(None, "fsdp"),
        P(None, "fsdp"),
        P(None, "fsdp"),
        P(None, "fsdp"),
        P(None, "fsdp"),
        P(None, "fsdp"),
        P("fsdp"),
        P(None, "fsdp"),
        P(None, "fsdp"),
        P("fsdp"),
        P("fsdp", None),
        P(("dp", "fsdp"), None),
    )
    return jax.shard_map(
        local,
        mesh=mesh,
        in_specs=placed,
        out_specs=(P(("dp", "fsdp"), None), P(("dp", "fsdp"), None), P("fsdp", None)),
        check_vma=False,
    )
```

```python
import functools
import math

import jax
import jax.numpy as jnp
from jax import lax
from jax.experimental import pallas as pl
from jax.experimental.pallas import tpu as pltpu
from jax.sharding import PartitionSpec as P

MELS = 80
PANEL = 128
EPSILON = 1e-05
SPAN = PANEL // 8
BLOCK = 8
ROWS = BLOCK * SPAN
FRONT = 62
BACK = 62
BINS = 40
GROUP = 10
WINDOW = 2 * GROUP + 1
LEAD = 256
BF = jnp.bfloat16
F32 = jnp.float32
ACROSS = (((1,), (1,)), ((), ()))
DOWN = (((0,), (0,)), ((), ()))


def dot(left, right, dims=(((1,), (0,)), ((), ()))):
    return lax.dot_general(left, right, dims, preferred_element_type=F32)


def iota(shape, dim):
    return lax.broadcasted_iota(jnp.int32, shape, dim)


def row_order():
    n = iota((ROWS, ROWS), 0)
    r = iota((ROWS, ROWS), 1)
    return jnp.where((n % SPAN) * BLOCK + n // SPAN == r, 1.0, 0.0).astype(BF)


def send_kernel(
    mel, frames, target, first, depth_a, point_a, depth_b, point_b, norm_gain, depth_kernel, conv_gain,
    outgoing, packed,
    mel_s, first_s, depth_a_s, point_a_s, depth_b_s, point_b_s, norm_s, kernel_s, conv_s, rows, lines, sems,
):
    pairs = (
        (mel, mel_s), (first, first_s), (depth_a, depth_a_s), (point_a, point_a_s), (depth_b, depth_b_s),
        (point_b, point_b_s), (norm_gain, norm_s), (depth_kernel, kernel_s), (conv_gain, conv_s),
    )
    copies = [pltpu.make_async_copy(source, held, sems.at[n]) for n, (source, held) in enumerate(pairs)]
    for copy in copies:
        copy.start()
    count = outgoing.shape[0]
    slots = mel_s.shape[0]
    lanes = mel_s.shape[1] // 128
    wanted = iota((count, slots), 0)
    chosen = jnp.where((target[...] == wanted) & (frames[...] > 0), 1.0, 0.0)
    sent = jnp.sum(chosen * frames[...].astype(F32), axis=1, keepdims=True)
    sent = jnp.broadcast_to(sent, (count, 128))
    for k in range(8):
        lines[pl.ds(lanes + k, count, stride=lanes + 8), :] = sent
    copies[0].wait()
    chosen = chosen.astype(BF)
    for k in range(lanes):
        lines[pl.ds(k, count, stride=lanes + 8), :] = dot(chosen, mel_s[:, k * 128 : (k + 1) * 128])
    for d in range(count):
        outgoing[d] = lines[d * (lanes + 8) : (d + 1) * (lanes + 8), :].astype(BF)
    for copy in copies[1:]:
        copy.wait()
    rows[...] = jnp.zeros_like(rows)
    rows[0:9, :] = kernel_s[...].astype(F32)
    rows[9:10, :] = norm_s[...].astype(F32).reshape(1, 512)
    rows[10:11, :] = conv_s[...].astype(F32).reshape(1, 512)
    rows[16:25, 0:128] = first_s[...].astype(F32)
    rows[16:25, 128:256] = depth_a_s[...].astype(F32)
    rows[16:25, 256:384] = depth_b_s[...].astype(F32)
    packed[0:32, :] = rows[...].astype(BF)
    packed[32:160, 0:128] = point_a_s[0:128, :]
    packed[32:160, 128:256] = point_a_s[128:256, :]
    packed[32:160, 256:384] = point_b_s[0:128, :]
    packed[32:160, 384:512] = point_b_s[128:256, :]


def weights_kernel(mine, other, band, taps_a, taps_b, point_a, point_b, rows):
    me = lax.axis_index("fsdp")
    near, far = mine[...].astype(F32), other[...].astype(F32)
    low, high = jnp.where(me == 0, near, far), jnp.where(me == 0, far, near)
    rows[:, 0:512] = low[0:16]
    rows[:, 512:1024] = high[0:16]
    first = jnp.concatenate([low[16:32, 0:128], high[16:32, 0:128]], axis=1).astype(BF)
    taps_a[...] = jnp.concatenate([low[16:32, 128:256], high[16:32, 128:256]], axis=1)
    taps_b[...] = jnp.concatenate([low[16:32, 256:384], high[16:32, 256:384]], axis=1)
    for half, source in ((0, low), (1, high)):
        at = slice(half * 128, half * 128 + 128)
        point_a[0:128, at] = source[32:160, 0:128].astype(BF)
        point_a[128:256, at] = source[32:160, 128:256].astype(BF)
        point_b[0:128, at] = source[32:160, 256:384].astype(BF)
        point_b[128:256, at] = source[32:160, 384:512].astype(BF)
    tap = iota((256, 16), 1)
    base = jnp.where(tap < 9, (tap // 3) * MELS + tap % 3, -1000) - iota((256, 16), 0)
    for f in range(GROUP):
        place = jnp.where(base == -2 * f, 1.0, 0.0).astype(BF)
        band[:, f * 256 : (f + 1) * 256] = dot(place, first).astype(BF)


def fetch(pairs, sems, me):
    copies = []
    for number, (mine, other, held) in enumerate(pairs):
        copies.append(pltpu.make_async_copy(mine, held.at[me], sems.at[2 * number]))
        copies.append(pltpu.make_async_copy(other, held.at[1 - me], sems.at[2 * number + 1]))
    return copies


def centre(values):
    return values - jnp.mean(values, axis=1, keepdims=True)


def forward_kernel(
    incoming_in, band_in, taps_a_in, taps_b_in, point_a_in, point_b_in, rows_in, linear_mine, linear_other, up_mine, up_other,
    give_0, give_1, give_2, give_3, features_o, value_o, gate_o, standard_two_o, scale_o, keep_o,
    incoming, features_out, value_out, gate_out, standard_two_out, scale_out, keep_out, band, taps_a, taps_b, point_a, point_b, rows, linear_s, up_s, pick_s, ext_s, x_s, first_s, spread_s, even_s, odd_s, flat_s, gated_s, kept_s, sems, out_sems,
):
    step = pl.program_id(0)
    me = lax.axis_index("fsdp")
    copies = fetch(((linear_mine, linear_other, linear_s), (up_mine, up_other, up_s)), sems, me)
    pairs = (
        (incoming_in, incoming), (band_in, band), (taps_a_in, taps_a), (taps_b_in, taps_b), (point_a_in, point_a),
        (point_b_in, point_b), (rows_in, rows),
    )
    small = [pltpu.make_async_copy(source, target, sems.at[4 + n]) for n, (source, target) in enumerate(pairs)]
    here = pl.ds(step * ROWS, ROWS)
    held = (features_out, value_out, gate_out, standard_two_out, scale_out, keep_out)
    saves = [
        pltpu.make_async_copy(source, out.at[here], out_sems.at[n])
        for n, (source, out) in enumerate(zip(held, (features_o, value_o, gate_o, standard_two_o, scale_o, keep_o)))
    ]

    @pl.when(step == 0)
    def _():
        for copy in small:
            copy.start()
        small[0].wait()
        for copy in copies:
            copy.start()

    sources = incoming.shape[0]
    lanes = incoming.shape[1] - 8
    got = jnp.concatenate([incoming[source, lanes:, :].astype(F32)[0:1] for source in range(sources)], axis=0)
    present = jnp.where(got > 0, 1.0, 0.0)
    below = jnp.where(iota((sources, sources), 1) <= iota((sources, sources), 0), 1.0, 0.0).astype(BF)
    position = dot(below, present.astype(BF)) - 1.0
    slot = (iota((sources, 128), 1) + step * BLOCK).astype(F32)
    placing = jnp.where((position == slot) & (present > 0), 1.0, 0.0).astype(BF)[:, :BLOCK]
    length = dot(placing, got.astype(BF), DOWN)
    source = dot(placing, iota((sources, 128), 0).astype(F32).astype(BF), DOWN)
    per_step = lanes // SPAN
    lane = iota((BLOCK, 128), 1).astype(F32)
    base = source * lanes - lane
    for t in range(SPAN):
        live = length > 8.0 * t
        keep_out[t * BLOCK : (t + 1) * BLOCK, :] = jnp.where(live, 1.0, 0.0)
        here = jnp.where(live, base, -1e6)
        for k in range(per_step):
            at = k * ROWS + t * BLOCK
            for c in range(sources * lanes // 128):
                hit = here == 128.0 * c - (per_step * t + k)
                pick_s[at : at + BLOCK, c * 128 : (c + 1) * 128] = jnp.where(hit, 1.0, 0.0)
    lines = jnp.concatenate([incoming[source, :lanes, :] for source in range(sources)], axis=0)
    placed = dot(pick_s[...].astype(BF), lines)
    ext_s[0:BLOCK, 0:LEAD] = jnp.zeros((BLOCK, LEAD), F32)
    for k in range(per_step):
        part = placed[k * ROWS : (k + 1) * ROWS]
        ext_s[:, LEAD + k * 128 : LEAD + (k + 1) * 128] = part
        ahead = k + LEAD // 128 - per_step
        if ahead >= 0:
            ext_s[BLOCK:, ahead * 128 : (ahead + 1) * 128] = part[: ROWS - BLOCK]
    lane = iota((ROWS, 256), 1)
    edge = (lane == 0) | (lane == MELS) | (lane == 2 * MELS)
    for q in range(4):
        for b in range(4):
            start = LEAD + (2 * q - 1) * MELS + 2 * GROUP * b - 1
            tile = start // 128 * 128
            shift = start - tile
            span = 256 if shift + 2 * MELS + WINDOW <= 256 else 384
            part = ext_s[:, tile : tile + span]
            part = pltpu.roll(part, span - shift, 1)[:, :256]
            if b == 0:
                part = jnp.where(edge, 0.0, part)
            x_s[b, q * ROWS : (q + 1) * ROWS, :] = part.astype(BF)

    @pl.when(step == 0)
    def _():
        for copy in small[1:]:
            copy.wait()

    views = (3 * ROWS, 0, ROWS, 2 * ROWS, 3 * ROWS + BLOCK)
    first_s[0] = jnp.zeros(first_s.shape[1:], F32)
    for f in range(GROUP):
        first_s[1 + f, 3 * ROWS : 3 * ROWS + BLOCK, :] = jnp.zeros((BLOCK, 256), F32)
    odd_s[:, 0:BLOCK, :] = jnp.zeros((odd_s.shape[0], BLOCK, 256), F32)

    def section(b, carry):
        source = x_s[b]
        for f in range(GROUP):
            sums = jnp.maximum(dot(source, band[:, f * 256 : (f + 1) * 256]), 0.0)
            first_s[1 + f, : 3 * ROWS, :] = sums[: 3 * ROWS]
            first_s[1 + f, 3 * ROWS + BLOCK :, :] = sums[3 * ROWS :]
        for g in range(GROUP // 2):
            for s in range(2):
                total = None
                for j in range(3):
                    for i in range(3):
                        at = views[2 * s + i]
                        term = first_s[2 * g + j, at : at + ROWS, :] * taps_a[3 * i + j : 3 * i + j + 1, :]
                        total = term if total is None else total + term
                spread_s[(2 * g + s) * ROWS : (2 * g + s + 1) * ROWS, :] = total.astype(BF)
        first_s[0] = first_s[GROUP]
        second = jnp.maximum(dot(spread_s[...], point_a[...]), 0.0)
        for g in range(GROUP // 2):
            even_s[b * (GROUP // 2) + g] = second[2 * g * ROWS : (2 * g + 1) * ROWS]
            odd_s[b * (GROUP // 2) + g, BLOCK:, :] = second[(2 * g + 1) * ROWS : (2 * g + 2) * ROWS]
        return carry

    lax.fori_loop(0, BINS // GROUP, section, 0, unroll=2)

    for f in range(BINS // 4):
        total = None
        for j in range(3):
            at = 2 * f + j - 1
            if at < 0:
                continue
            for i, view in enumerate((odd_s.at[at, 0:ROWS, :], even_s.at[at], odd_s.at[at, BLOCK : BLOCK + ROWS, :])):
                term = view[...] * taps_b[3 * i + j : 3 * i + j + 1, :]
                total = term if total is None else total + term
        fourth = jnp.maximum(dot(total.astype(BF), point_b[...]), 0.0)
        flat_s[:, f * 256 : (f + 1) * 256] = fourth.astype(BF)

    @pl.when(step == 0)
    def _():
        copies[0].wait()
        copies[1].wait()

    half = linear_s.shape[2]
    for side in range(2):
        features_out[:, side * half : (side + 1) * half] = dot(flat_s[...], linear_s[side]).astype(BF)
    saves[0].start()
    saves[5].start()
    centred = centre(features_out[...].astype(F32))
    scale_one = lax.rsqrt(jnp.mean(centred * centred, axis=1, keepdims=True) + EPSILON)
    standard = centred * scale_one
    normed = (standard * rows[9:10, :]).astype(BF)

    @pl.when(step == 0)
    def _():
        copies[2].wait()
        copies[3].wait()

    row_keep = keep_out[:, 0:1]
    value = dot(normed, up_s[0])
    value_out[...] = value
    gate = jax.nn.sigmoid(dot(normed, up_s[1]))
    gate_out[...] = gate
    saves[1].start()
    saves[2].start()
    reach = 4 * BLOCK
    gated_s[0:reach, :] = jnp.zeros((reach, gated_s.shape[1]), F32)
    gated_s[reach + ROWS :, :] = jnp.zeros((reach, gated_s.shape[1]), F32)
    gated_s[reach : reach + ROWS, :] = (row_keep * value * gate).astype(BF).astype(F32)
    total = None
    for k in range(9):
        term = gated_s[k * BLOCK : k * BLOCK + ROWS, :] * rows[k : k + 1, :]
        total = term if total is None else total + term
    centred = centre(total)
    scale_two = lax.rsqrt(jnp.mean(centred * centred, axis=1, keepdims=True) + EPSILON)
    standard_two = centred * scale_two
    standard_two_out[...] = standard_two
    scale_out[...] = jnp.broadcast_to(scale_two, (ROWS, 128))
    saves[3].start()
    saves[4].start()
    active = standard_two * rows[10:11, :]
    hidden = (active * jax.nn.sigmoid(active)).astype(BF)
    kept = jnp.where(row_keep > 0, hidden, jnp.zeros_like(hidden))
    kept = dot(row_order(), kept).astype(BF)
    count = kept_s.shape[0]
    for n in range(count):
        kept_s[n] = kept[:, n * 128 : (n + 1) * 128]
    plane = lax.axis_index("dp") % 4
    for offset, give in enumerate((give_0, give_1, give_2, give_3)):
        quarter = plane ^ offset
        give[0] = kept_s[me * (count // 2) + quarter]
        give[1] = kept_s[(1 - me) * (count // 2) + quarter]
    for save in saves:
        save.wait()


def pack_kernel(*refs):
    for n in range(4):
        refs[4][n] = refs[n][1]


def near_kernel(*refs):
    left = jnp.concatenate([ref[0] for ref in refs[0:4]], axis=0)
    right = jnp.concatenate([ref[...] for ref in refs[4:8]], axis=0)
    refs[8][...] = dot(left, right, DOWN)


def far_kernel(groups, *refs):
    first, gifts, theirs, outs, total = refs[0], refs[1], refs[2:6], refs[6:-1], refs[-1]
    left = jnp.concatenate([gifts[n] for n in range(4)], axis=0)
    right = jnp.concatenate([ref[...] for ref in theirs], axis=0)
    total[...] = first[...] + dot(left, right, DOWN)
    me = lax.axis_index("dp") // 4
    size = total.shape[0] // (groups // 4)
    for offset, out in enumerate(outs):
        at = pl.multiple_of((me ^ offset) * size, size)
        out[...] = total[pl.ds(at, size), :].astype(out.dtype)


def layers_kernel(*refs):
    pieces, left, right, total = refs[:-3], refs[-3], refs[-2], refs[-1]
    me = lax.axis_index("dp") // 4
    size = pieces[0].shape[0]
    for offset, piece in enumerate(pieces):
        at = pl.multiple_of((me ^ offset) * size, size)
        total[pl.ds(at, size), :] = piece[...].astype(F32)
    half = left.shape[1]
    left[...] = total[:, :half].astype(BF)
    right[...] = total[:, half:].astype(BF)


def finish_kernel(places, *refs):
    pieces, out, held, sems = refs[: len(places)], refs[-3], refs[-2], refs[-1]
    plane = lax.axis_index("dp") % 4
    size, half = pieces[0].shape
    copies = []
    for n, (piece, (offset, side)) in enumerate(zip(pieces, places)):
        held[n] = piece[...].astype(F32)
        at = pl.multiple_of((plane ^ offset) * size, size)
        columns = slice(side * half, (side + 1) * half)
        copies.append(pltpu.make_async_copy(held.at[n], out.at[pl.ds(at, size), columns], sems.at[n]))
        copies[-1].start()
    for copy in copies:
        copy.wait()


def back_rows(order, cotangent, row_keep):
    return jnp.where(row_keep > 0, dot(order, cotangent[...], DOWN), 0.0)


def bring(body, inputs, outputs, *refs):
    sources, mine, other = refs[:inputs], refs[inputs], refs[inputs + 1]
    outs = refs[inputs + 2 : inputs + 2 + outputs]
    refs = refs[inputs + 2 + outputs :]
    held, weight, sems, extra = refs[:inputs], refs[inputs], refs[inputs + 1], refs[inputs + 2 :]
    step = pl.program_id(0)
    copies = []
    for n, (source, buffer) in enumerate(zip(sources, held)):
        if source.shape[0] != 16:
            source = source.at[pl.ds(step * ROWS, ROWS)]
        copies.append(pltpu.make_async_copy(source, buffer, sems.at[n]))
    me = lax.axis_index("fsdp")
    weights = [
        pltpu.make_async_copy(mine, weight.at[me], sems.at[inputs]),
        pltpu.make_async_copy(other, weight.at[1 - me], sems.at[inputs + 1]),
    ]
    for copy in copies:
        copy.start()

    @pl.when(step == 0)
    def _():
        for copy in weights:
            copy.start()

    for copy in copies:
        copy.wait()

    def wait_weight():
        @pl.when(step == 0)
        def _():
            for copy in weights:
                copy.wait()

    body(wait_weight, weight, *held, *outs, *extra)


def layer_kernel(wait_weight, down_s, features_in, standard_two_in, keep_in, rows, layer_out):
    active = standard_two_in[...] * rows[10:11, :]
    hidden = (active * jax.nn.sigmoid(active)).astype(BF)
    order = row_order()
    wait_weight()
    half = down_s.shape[1]
    mixed = dot(hidden[:, :half], down_s[0]) + dot(hidden[:, half:], down_s[1])
    layer = jnp.where(keep_in[:, 0:1] > 0, features_in[...].astype(F32) + mixed, 0.0).astype(BF)
    layer_out[...] = dot(order, layer).astype(BF)


def depth_kernel_back(
    wait_weight, down_s, standard_two_in, value_in, gate_in, scale_in, keep_in, rows, cotangent, value_out, gate_out, depth_s,
):
    row_keep = keep_in[:, 0:1]
    back_out = back_rows(row_order(), cotangent, row_keep).astype(BF)
    standard_two = standard_two_in[...]
    active = standard_two * rows[10:11, :]
    swish = jax.nn.sigmoid(active)
    slope = (swish + active * swish * (1.0 - swish)) * rows[10:11, :]
    wait_weight()
    back_hidden = jnp.concatenate([dot(back_out, down_s[0], ACROSS), dot(back_out, down_s[1], ACROSS)], axis=1)
    gain_up = back_hidden * slope
    reach = 4 * BLOCK
    depth_s[0:reach, :] = jnp.zeros((reach, depth_s.shape[1]), F32)
    depth_s[reach + ROWS :, :] = jnp.zeros((reach, depth_s.shape[1]), F32)
    depth_s[reach : reach + ROWS, :] = scale_in[:, 0:1] * (
        gain_up
        - jnp.mean(gain_up, axis=1, keepdims=True)
        - standard_two * jnp.mean(gain_up * standard_two, axis=1, keepdims=True)
    )
    total = None
    for k in range(9):
        term = depth_s[(8 - k) * BLOCK : (8 - k) * BLOCK + ROWS, :] * rows[k : k + 1, :]
        total = term if total is None else total + term
    gate = gate_in[...]
    back_value = row_keep * total * gate
    value_out[...] = back_value.astype(BF)
    gate_out[...] = (back_value * value_in[...] * (1.0 - gate)).astype(BF)


def up_kernel(wait_weight, up_s, back_value, back_gate, features_in, keep_in, rows, cotangent, grad_out):
    order = row_order()
    row_keep = keep_in[:, 0:1]
    back_out = back_rows(order, cotangent, row_keep)
    centred = centre(features_in[...].astype(F32))
    scale_one = lax.rsqrt(jnp.mean(centred * centred, axis=1, keepdims=True) + EPSILON)
    standard = centred * scale_one
    wait_weight()
    back_normed = dot(back_value[...], up_s[0], ACROSS) + dot(back_gate[...], up_s[1], ACROSS)
    gain_in = back_normed * rows[9:10, :]
    back_input = scale_one * (
        gain_in
        - jnp.mean(gain_in, axis=1, keepdims=True)
        - standard * jnp.mean(gain_in * standard, axis=1, keepdims=True)
    )
    grad_out[...] = dot(order, (back_out + back_input).astype(BF)).astype(BF)


def whole(shape):
    return pl.BlockSpec(shape, lambda g: (0,) * len(shape))


def params(megabytes):
    return pltpu.CompilerParams(vmem_limit_bytes=megabytes * 1024 * 1024)


def cost(flops, moved):
    return pl.CostEstimate(flops=int(flops), bytes_accessed=int(moved), transcendentals=0)


def swap_cores(block):
    return lax.ppermute(block, "fsdp", [(0, 1), (1, 0)])


def swap_rank(block, offset, groups):
    return lax.ppermute(block, "dp", [(i, i ^ offset) for i in range(groups)])


def held_call(kernel, outs, scratch, name, *operands, **specs):
    return pl.pallas_call(
        kernel,
        **specs,
        out_shape=outs,
        scratch_shapes=scratch,
        compiler_params=params(32),
        cost_estimate=cost(1e6, 1e5),
        name=name,
    )(*operands)


def local(
    mel_panels,
    frames,
    target,
    conv_first,
    depth_a,
    point_a,
    depth_b,
    point_b,
    linear_weight,
    norm_gain,
    up_weight,
    depth_kernel,
    conv_gain,
    down_weight,
    cotangent,
):
    groups = lax.axis_size("dp")
    members = lax.axis_size("fsdp")
    slots, width_in = mel_panels.shape
    rows_here, width = cotangent.shape
    blocks = rows_here // ROWS
    half = width // members
    shape = jax.ShapeDtypeStruct
    lines = width_in // 128 + 8
    anywhere = pl.BlockSpec(memory_space=pltpu.HBM)
    held = pl.BlockSpec(memory_space=pltpu.VMEM)
    small = (conv_first, depth_a, point_a, depth_b, point_b, norm_gain, depth_kernel, conv_gain)
    outgoing, packed = pl.pallas_call(
        send_kernel,
        in_specs=[anywhere, held, held] + [anywhere] * len(small),
        out_shape=(shape((groups, lines, 128), BF), shape((160, 512), BF)),
        scratch_shapes=[pltpu.VMEM(array.shape, BF) for array in (mel_panels,) + small]
        + [
            pltpu.VMEM((32, 512), F32),
            pltpu.VMEM((groups * lines, 128), F32),
            pltpu.SemaphoreType.DMA((1 + len(small),)),
        ],
        compiler_params=params(60),
        cost_estimate=cost(2e8, 1e6),
        name="send",
    )(mel_panels, frames.reshape(1, slots), target.reshape(1, slots), *small)
    incoming = lax.all_to_all(outgoing, "dp", split_axis=0, concat_axis=0, tiled=True)
    packed_other = swap_cores(packed)
    unpacked = held_call(
        weights_kernel,
        [
            shape((256, GROUP * 256), BF), shape((16, 256), F32), shape((16, 256), F32), shape((256, 256), BF),
            shape((256, 256), BF), shape((16, width), F32),
        ],
        [], "weights", packed, packed_other,
    )
    rows = unpacked[-1]
    linear_other = swap_cores(linear_weight)
    up_other = swap_cores(up_weight)
    down_other = swap_cores(down_weight)
    cotangents = [cotangent] + [swap_rank(cotangent, offset, groups) for offset in range(1, 4)]
    cotangent_other = swap_cores(cotangent)
    def by_rows(columns):
        return pl.BlockSpec((ROWS, columns), lambda g: (g, 0))

    by_plane = pl.BlockSpec((members, ROWS, 128), lambda g: (0, g, 0))
    *given, features, value, gate, standard_two, scale, keep = pl.pallas_call(
        forward_kernel,
        grid=(blocks,),
        in_specs=[
            *[anywhere] * 11,
        ],
        out_specs=[
            *[by_plane] * 4, *[anywhere] * 6,
        ],
        out_shape=(
            *[shape((members, rows_here, 128), BF)] * 4,
            shape((rows_here, width), BF),
            shape((rows_here, width), F32),
            shape((rows_here, width), F32),
            shape((rows_here, width), F32),
            shape((rows_here, 128), F32),
            shape((rows_here, 128), F32),
        ),
        scratch_shapes=[
            pltpu.VMEM(incoming.shape, BF),
            pltpu.VMEM((ROWS, width), BF),
            pltpu.VMEM((ROWS, width), F32),
            pltpu.VMEM((ROWS, width), F32),
            pltpu.VMEM((ROWS, width), F32),
            pltpu.VMEM((ROWS, 128), F32),
            pltpu.VMEM((ROWS, 128), F32),
            pltpu.VMEM((256, GROUP * 256), BF),
            pltpu.VMEM((16, 256), F32),
            pltpu.VMEM((16, 256), F32),
            pltpu.VMEM((256, 256), BF),
            pltpu.VMEM((256, 256), BF),
            pltpu.VMEM((16, width), F32),
            pltpu.VMEM((2,) + linear_weight.shape, BF),
            pltpu.VMEM((2,) + up_weight.shape, BF),
            pltpu.VMEM((ROWS * width_in // SPAN // 128, groups * width_in // 128), F32),
            pltpu.VMEM((ROWS, LEAD + width_in // SPAN), F32),
            pltpu.VMEM((4, 4 * ROWS, 256), BF),
            pltpu.VMEM((GROUP + 1, 4 * ROWS + BLOCK, 256), F32),
            pltpu.VMEM((GROUP * ROWS, 256), BF),
            pltpu.VMEM((BINS // 2, ROWS, 256), F32),
            pltpu.VMEM((BINS // 2, ROWS + BLOCK, 256), F32),
            pltpu.VMEM((ROWS, BINS // 4 * 256), BF),
            pltpu.VMEM((ROWS + 8 * BLOCK, width), F32),
            pltpu.VMEM((width // 128, ROWS, 128), BF),
            pltpu.SemaphoreType.DMA((11,)),
            pltpu.SemaphoreType.DMA((6,)),
        ],
        compiler_params=params(FRONT),
        cost_estimate=cost(2e10 * blocks, 1e7),
        name="forward",
    )(incoming, *unpacked, linear_weight, linear_other, up_weight, up_other)
    first, *cotangents[1:3] = lax.optimization_barrier((given[0], *cotangents[1:3]))
    cotangents_other = [cotangent_other] + [swap_cores(block) for block in cotangents[1:3]]
    near = [swap_rank(given[offset], offset, groups) for offset in range(1, 4)]
    full = by_rows(width)

    def back_call(body, name, sources, mine, other, outs, extra=()):
        return pl.pallas_call(
            functools.partial(bring, body, len(sources), outs),
            grid=(blocks,),
            in_specs=[anywhere] * (len(sources) + 2),
            out_specs=[full] * outs,
            out_shape=[shape((rows_here, width), BF)] * outs,
            scratch_shapes=[
                *[pltpu.VMEM((min(array.shape[0], ROWS), array.shape[1]), array.dtype) for array in sources],
                pltpu.VMEM((2,) + mine.shape, BF),
                pltpu.SemaphoreType.DMA((len(sources) + 2,)),
                *extra,
            ],
            compiler_params=params(BACK),
            cost_estimate=cost(1e6, 1e5),
            name=name,
        )(*sources, mine, other)

    (layer_out,) = back_call(layer_kernel, "layer", (features, standard_two, keep, rows), down_weight, down_other, 1)
    *near, layer_out, cotangents[3] = lax.optimization_barrier((*near, layer_out, cotangents[3]))
    near = [first, *near]
    far = swap_cores(held_call(pack_kernel, shape((4, rows_here, 128), BF), [], "pack", *near))
    cotangents_other.append(swap_cores(cotangents[3]))
    layers = groups // 4
    block = width // members // 4
    size = block // layers
    half_sum = held_call(near_kernel, shape((block, width), F32), [], "near", *near, *cotangents)
    own, *others = held_call(
        functools.partial(far_kernel, groups),
        [shape((size, width), F32)] + [shape((size, width), BF)] * (layers - 1),
        [pltpu.VMEM((block, width), F32)],
        "far",
        half_sum, far, *cotangents_other,
    )
    moved = [swap_rank(other, 4 * (offset + 1), groups) for offset, other in enumerate(others)]
    value_back, gate_back = back_call(
        depth_kernel_back, "depth", (standard_two, value, gate, scale, keep, rows, cotangent), down_weight, down_other, 2,
        [pltpu.VMEM((ROWS + 8 * BLOCK, width), F32)],
    )
    *moved, value_back, gate_back = lax.optimization_barrier((*moved, value_back, gate_back))
    for part in moved:
        own = own + part.astype(F32)
    own = (own * (1.0 / math.sqrt(rows_here * groups * members))).astype(BF)
    pieces = [own] + [swap_rank(own, 4 * offset, groups) for offset in range(1, layers)]
    (grad_input,) = back_call(
        up_kernel, "up", (value_back, gate_back, features, keep, rows, cotangent), up_weight, up_other, 1
    )
    *pieces, grad_input = lax.optimization_barrier((*pieces, grad_input))
    left, right = held_call(
        layers_kernel, [shape((block, width // 2), BF)] * 2, [pltpu.VMEM((block, width), F32)], "layers", *pieces
    )
    left_x, right_y = swap_rank(left, 1, groups), swap_rank(right, 2, groups)
    left_y, right_x = swap_rank(left, 2, groups), swap_rank(right, 1, groups)
    left_xy, right_xy = swap_rank(left_x, 2, groups), swap_rank(right_y, 1, groups)
    def finish(places, *operands, **specs):
        return held_call(
            functools.partial(finish_kernel, places), shape((half, width), F32),
            [pltpu.VMEM((len(places), block, width // 2), F32), pltpu.SemaphoreType.DMA((len(places),))], "finish",
            *operands, out_specs=anywhere, **specs,
        )

    places = ((0, 0), (0, 1), (1, 0), (1, 1), (2, 0), (2, 1))
    grad_down = finish(places, left, right, left_x, right_x, left_y, right_y)
    grad_down = finish(
        ((3, 0), (3, 1)), left_xy, right_xy, grad_down,
        in_specs=[pl.BlockSpec(memory_space=pltpu.VMEM)] * 2 + [anywhere], input_output_aliases={2: 0},
    )
    return (layer_out, grad_input, grad_down)


def solution(mesh):
    placed = (
        P(("dp", "fsdp"), None),
        P(("dp", "fsdp")),
        P(("dp", "fsdp")),
        P(None, "fsdp"),
        P(None, "fsdp"),
        P(None, "fsdp"),
        P(None, "fsdp"),
        P(None, "fsdp"),
        P(None, "fsdp"),
        P("fsdp"),
        P(None, "fsdp"),
        P(None, "fsdp"),
        P("fsdp"),
        P("fsdp", None),
        P(("dp", "fsdp"), None),
    )
    return jax.shard_map(
        local,
        mesh=mesh,
        in_specs=placed,
        out_specs=(P(("dp", "fsdp"), None), P(("dp", "fsdp"), None), P("fsdp", None)),
        check_vma=False,
    )
```
